512 devices in a mesh: gx: 32 (over x, y), gy: 16 (over z, core).
Axes of the slice: x: 4, y: 8, z: 8, core: 2. Of those that a mesh axis runs over, the one named last changes fastest.
Arguments:
- tokens: bfloat16 [131072, 512], P(('gx', 'gy')), may hold values from -8 to 8
- w_qkv: bfloat16 [512, 1536], replicated, may hold values from -0.25 to 0.25
- w_out: bfloat16 [512, 512], replicated, may hold values from -0.25 to 0.25
Outputs:
- mixed: bfloat16 [131072, 512], P(('gx', 'gy'))
The draws below stay inside these ranges and needn't reach their ends.
All inputs are finite; a program needn't handle non-finite values.
Results may differ from the reference program's by a relative error of at most 0.0063.
Values may be sent and summed in bfloat16 or wider, within the bound.
No kernel may reach another device: no remote copies, remote signals or barrier semaphores. Data moves between devices by JAX's collectives and lax.ppermute only.
A program may use at most 64 MiB of HBM per device.

```python
import jax
import jax.numpy as jnp
from jax import lax

HEADS = 8
HEAD_DIM = 64
BLOCK = 64
D = 512
TOKENS = 131072


def draw_tokens(key, part):
    key = jax.random.fold_in(key, 11)
    scales = (TOKENS // BLOCK).bit_length() - 1
    noise_key, coarse_key = jax.random.split(key)
    field = jax.random.normal(noise_key, (TOKENS, D), jnp.float32)
    amplitude = 0.3
    for level_num in range(scales + 1):
        span = BLOCK * 2 ** level_num
        piece = jax.random.normal(jax.random.fold_in(coarse_key, level_num), (TOKENS // span, D), jnp.float32)
        field = field + amplitude * jnp.repeat(piece, span, axis=0)
    return jnp.clip(field, -8.0, 8.0).astype(jnp.bfloat16)


def bell_draw(stream_key, dims, width, reach, kind=jnp.bfloat16):
    result = jax.random.normal(stream_key, dims, jnp.float32) * width
    return jnp.minimum(jnp.maximum(result, -reach), reach).astype(kind)


def setup_inputs(seed: int = 0) -> dict:
    arg_keys = jax.random.split(jax.random.key(seed), 4)
    return {
        "tokens": draw_tokens(jax.random.fold_in(arg_keys[3], 71), 0),
        "w_qkv": bell_draw(arg_keys[1], (D, 3 * D), D ** -0.5, 0.25),
        "w_out": bell_draw(arg_keys[2], (D, D), D ** -0.5, 0.25),
    }


def pool_rows(values):
    shape = values.shape
    paired = values.reshape(shape[:-2] + (shape[-2] // 2, 2, shape[-1])).astype(jnp.float32)
    return lax.optimization_barrier(((paired[..., 0, :] + paired[..., 1, :]) * 0.5).astype(jnp.bfloat16))


def attend(queries, keys, values, valid):
    scores = jnp.einsum('grd,gkd->grk', queries.astype(jnp.float32), keys.astype(jnp.float32)) * HEAD_DIM ** -0.5
    weights = jnp.exp(scores) * valid[:, None, :]
    totals = jnp.sum(weights, axis=-1)
    rounded = lax.optimization_barrier(weights.astype(jnp.bfloat16)).astype(jnp.float32)
    numerator = jnp.einsum('grk,gkd->grd', rounded, values.astype(jnp.float32))
    return numerator.reshape(-1, HEAD_DIM), totals.reshape(-1)


def head_output(slices):
    queries, key_levels, value_levels = slices
    block_count = TOKENS // BLOCK
    zeros = jnp.zeros((BLOCK, HEAD_DIM), jnp.bfloat16)
    padded_keys = jnp.concatenate([zeros, key_levels[0], zeros], axis=0)
    padded_values = jnp.concatenate([zeros, value_levels[0], zeros], axis=0)

    def nearby(padded):
        parts = [padded[shift * BLOCK:shift * BLOCK + TOKENS].reshape(block_count, BLOCK, HEAD_DIM) for shift in range(3)]
        return jnp.concatenate(parts, axis=1)

    block_ids = jnp.arange(block_count)[:, None]
    key_slots = jnp.arange(3 * BLOCK)[None, :]
    invalid = ((block_ids == 0) & (key_slots < BLOCK)) | ((block_ids == block_count - 1) & (key_slots >= 2 * BLOCK))
    valid = jnp.where(invalid, 0.0, 1.0).astype(jnp.float32)
    numerator, totals = attend(queries.reshape(block_count, BLOCK, HEAD_DIM), nearby(padded_keys), nearby(padded_values), valid)
    for level_num in range(1, len(key_levels)):
        groups = block_count >> level_num
        sib_keys = key_levels[level_num].reshape(groups // 2, 2, BLOCK, HEAD_DIM)[:, ::-1].reshape(groups, BLOCK, HEAD_DIM)
        sib_values = value_levels[level_num].reshape(groups // 2, 2, BLOCK, HEAD_DIM)[:, ::-1].reshape(groups, BLOCK, HEAD_DIM)
        grouped = queries.reshape(groups, BLOCK << level_num, HEAD_DIM)
        part_num, part_tot = attend(grouped, sib_keys, sib_values, jnp.ones((groups, BLOCK), jnp.float32))
        numerator = numerator + part_num
        totals = totals + part_tot
    return numerator / totals[:, None]


def split_heads(values):
    return values.reshape(values.shape[0], HEADS, HEAD_DIM).transpose(1, 0, 2)


def reference(tokens, w_qkv, w_out):
    projected = jnp.dot(tokens, w_qkv, preferred_element_type=jnp.float32)
    queries = lax.optimization_barrier(projected[:, :D].astype(jnp.bfloat16))
    keyvals = lax.optimization_barrier(projected[:, D:].astype(jnp.bfloat16))
    level_total = (TOKENS // BLOCK).bit_length() - 1
    levels = [keyvals]
    for level_num in range(1, level_total):
        levels.append(pool_rows(levels[-1]))
    key_levels = [split_heads(level[:, :D]) for level in levels]
    value_levels = [split_heads(level[:, D:]) for level in levels]
    outputs = lax.map(head_output, (split_heads(queries), key_levels, value_levels))
    attended = outputs.transpose(1, 0, 2).reshape(TOKENS, D).astype(jnp.bfloat16)
    return jnp.dot(attended, w_out, preferred_element_type=jnp.float32).astype(jnp.bfloat16)
```

```python
import functools

import jax
import jax.numpy as jnp
import numpy as np
from jax import lax
from jax.experimental import pallas as pl
from jax.experimental.pallas import tpu as pltpu
from jax.sharding import PartitionSpec as P

HEADS = 8
BLOCK = 64
AXES = ("gx", "gy")
ROUNDS = (
    ("core", 0, "ag"),
    ("z1", 1, "ag"),
    ("z2", 2, "ag"),
    ("z4", 3, "pp"),
    ("y1", 4, "pp"),
    ("y2", 5, "ag"),
    ("y4", 6, "pp"),
    ("x1", 7, "ag"),
    ("x2", 8, "ag"),
)
FAR8 = (6, 7, 4, 5, 2, 3, 0, 1)
FAR4 = (3, 2, 1, 0)


def partners(bit, count):
    route = []
    for index in range(count):
        if bit == 3:
            z = index >> 1 & 7
            route.append(index & ~14 | FAR8[z] << 1)
        elif bit == 6:
            y = index >> 4 & 7
            route.append(index & ~112 | FAR8[y] << 4)
        elif bit == 8:
            x = index >> 7 & 3
            route.append(index & ~384 | FAR4[x] << 7)
        else:
            route.append(index ^ 1 << bit)
    return route


def vmem(count):
    return [pl.BlockSpec(memory_space=pltpu.VMEM)] * count


SMEM = pl.BlockSpec(memory_space=pltpu.SMEM)


def call(kernel, outs, in_specs, *args, flops=0, scratch=()):
    return pl.pallas_call(
        kernel,
        out_shape=outs,
        in_specs=in_specs,
        out_specs=jax.tree.map(lambda _: pl.BlockSpec(memory_space=pltpu.VMEM), outs),
        scratch_shapes=list(scratch),
        compiler_params=pltpu.CompilerParams(vmem_limit_bytes=24 * 2**20),
        cost_estimate=pl.CostEstimate(flops=flops, bytes_accessed=2**20, transcendentals=0),
    )(*args)


def pool_matrix(rows):
    r = lax.broadcasted_iota(jnp.int32, (rows, 2 * rows), 0)
    c = lax.broadcasted_iota(jnp.int32, (rows, 2 * rows), 1)
    return jnp.where(c >> 1 == r, 0.5, 0.0).astype(jnp.bfloat16)


def pooled(block):
    return jnp.dot(
        pool_matrix(block.shape[0] // 2), block, preferred_element_type=jnp.float32
    ).astype(jnp.bfloat16)


def project_kernel(place, x_ref, w_hbm, kv_ref, near_ref, other_ref, w_buf, sems):
    model = x_ref.shape[1]
    width = w_buf.shape[2]
    steps = w_buf.shape[0]
    copies = []
    for step in range(steps):
        columns = pl.ds(model + step * width, width)
        copy = pltpu.make_async_copy(w_hbm.at[:, columns], w_buf.at[step], sems.at[step])
        copy.start()
        copies.append(copy)
    core = place[0]
    x = x_ref[...]
    for step in range(steps):
        copies[step].wait()
        lanes = slice(step * width, (step + 1) * width)
        part = jnp.dot(x, w_buf[step], preferred_element_type=jnp.float32).astype(jnp.bfloat16)
        kv_ref[:, lanes] = part
        near_ref[BLOCK:, lanes] = pooled(pooled(part))
    last = x_ref.shape[0] - BLOCK
    low = pl.multiple_of(core * last, BLOCK)
    high = pl.multiple_of((1 - core) * last, BLOCK)
    near_ref[:BLOCK, :] = kv_ref[pl.ds(high, BLOCK), :]
    other_ref[...] = kv_ref[pl.ds(low, BLOCK), :]


def pool_kernel(*refs):
    ins, out_ref = refs[:-1], refs[-1]
    half = BLOCK // len(ins)
    for num, ref in enumerate(ins):
        rows = ref.shape[0]
        block = ref[...]
        if len(ins) == 1:
            out_ref[...] = pooled(block)
        else:
            out_ref[num * half : (num + 1) * half, :] = pooled(block)


def pool_near_kernel(near_ref, out_ref):
    out_ref[: BLOCK // 2, :] = pooled(near_ref[BLOCK : 2 * BLOCK, :])
    out_ref[BLOCK // 2 :, :] = pooled(near_ref[3 * BLOCK :, :])


def attend_pair(q, keys, values, ones):
    rows = q.shape[0]
    lane = lax.broadcasted_iota(jnp.int32, q.shape, 1)
    first = lane < 64
    zero = jnp.zeros_like(q)
    both = jnp.concatenate([jnp.where(first, q, zero), jnp.where(first, zero, q)], axis=0)
    scores = lax.dot_general(
        both, keys, (((1,), (1,)), ((), ())), preferred_element_type=jnp.float32
    )
    weights = jnp.exp(scores).astype(jnp.bfloat16)
    sums = jnp.dot(
        weights, jnp.concatenate([values, ones], axis=1), preferred_element_type=jnp.float32
    )
    num = jnp.where(first, sums[:rows, :128], sums[rows:, :128])
    tot = jnp.where(first, sums[:rows, 128:], sums[rows:, 128:])
    return num, tot


def local_kernel(place, x_ref, w_ref, kv_ref, near_ref, other_ref, q_ref, num_ref, tot_ref, pad, l1):
    rows, model = x_ref.shape
    blocks = rows // BLOCK
    q_ref[...] = (
        jnp.dot(x_ref[...], w_ref[...], preferred_element_type=jnp.float32)
        .astype(jnp.bfloat16) * jnp.bfloat16(0.125)
    )
    core = place[0]
    sib_halo = near_ref[pl.ds(pl.multiple_of((1 - core) * 2 * BLOCK, BLOCK), BLOCK), :]
    other = other_ref[...]
    is_first = core == 0
    pad[:BLOCK, :] = jnp.where(is_first, other, sib_halo)
    pad[BLOCK : BLOCK + rows, :] = kv_ref[...]
    pad[BLOCK + rows :, :] = jnp.where(is_first, sib_halo, other)
    l1[...] = pooled(kv_ref[...])
    key_row = lax.broadcasted_iota(jnp.int32, (4 * BLOCK, 128), 0)
    for i in range(blocks):
        ones = jnp.ones((4 * BLOCK, 128), jnp.float32)
        if i == 0:
            ones = jnp.where((key_row < BLOCK) & (place[1] == 1), 0.0, ones)
        if i == blocks - 1:
            ones = jnp.where((key_row >= 2 * BLOCK) & (key_row < 3 * BLOCK) & (place[2] == 1), 0.0, ones)
        ones = ones.astype(jnp.bfloat16)
        sib = (i >> 1) ^ 1
        here = slice(i * BLOCK, (i + 1) * BLOCK)
        for lanes in range(0, model, 128):
            kl = slice(lanes, lanes + 128)
            vl = slice(model + lanes, model + lanes + 128)
            keys = jnp.concatenate(
                [pad[i * BLOCK : (i + 3) * BLOCK, kl], l1[sib * BLOCK : (sib + 1) * BLOCK, kl]], axis=0
            )
            values = jnp.concatenate(
                [pad[i * BLOCK : (i + 3) * BLOCK, vl], l1[sib * BLOCK : (sib + 1) * BLOCK, vl]], axis=0
            )
            num, tot = attend_pair(q_ref[here, kl], keys, values, ones)
            num_ref[here, kl] = num
            tot_ref[here, kl] = tot


def sibling_rows(place, kinds, refs):
    rows = []
    for (kind, bit), ref in zip(kinds, refs):
        if kind == "near":
            start = (1 - place[0]) * 2 * BLOCK + BLOCK
        elif kind == "ag":
            start = (1 - place[3 + bit]) * BLOCK
        else:
            start = None
        rows.append((ref, start))
    return rows


def far_sums(place, kinds, refs, q_ref, lanes, model):
    keys, values = [], []
    for ref, start in sibling_rows(place, kinds, refs):
        at = slice(None) if start is None else pl.ds(pl.multiple_of(start, BLOCK), BLOCK)
        keys.append(ref[at, lanes : lanes + 128])
        values.append(ref[at, model + lanes : model + lanes + 128])
    keys = jnp.concatenate(keys, axis=0)
    values = jnp.concatenate(values, axis=0)
    ones = jnp.ones(values.shape, jnp.bfloat16)
    return attend_pair(q_ref[:, lanes : lanes + 128], keys, values, ones)


def far_kernel(kinds, place, q_ref, num_in, tot_in, *refs):
    num_ref, tot_ref = refs[-2:]
    model = q_ref.shape[1]
    for lanes in range(0, model, 128):
        at = slice(lanes, lanes + 128)
        num, tot = far_sums(place, kinds, refs[:-2], q_ref, lanes, model)
        num_ref[:, at] = num_in[:, at] + num
        tot_ref[:, at] = tot_in[:, at] + tot


def final_kernel(kinds, place, q_ref, num_in, tot_in, w_ref, *refs):
    out_ref, att = refs[-2:]
    model = q_ref.shape[1]
    for lanes in range(0, model, 128):
        at = slice(lanes, lanes + 128)
        num, tot = far_sums(place, kinds, refs[:-2], q_ref, lanes, model)
        att[:, at] = ((num_in[:, at] + num) / (tot_in[:, at] + tot)).astype(jnp.bfloat16)
    out_ref[...] = jnp.dot(att[...], w_ref[...], preferred_element_type=jnp.float32).astype(
        jnp.bfloat16
    )


def per_device(tokens, w_qkv, w_out):
    rows, model = tokens.shape
    index = lax.axis_index(AXES)
    count = lax.axis_size(AXES)
    bits = count.bit_length() - 1
    place = jnp.stack(
        [index & 1, (index == 0).astype(jnp.int32), (index == count - 1).astype(jnp.int32)]
        + [(index >> bit) & 1 for bit in range(bits)]
    ).astype(jnp.int32)
    bf16 = lambda *shape: jax.ShapeDtypeStruct(shape, jnp.bfloat16)
    f32 = lambda *shape: jax.ShapeDtypeStruct(shape, jnp.float32)
    steps = 4
    width = 2 * model // steps
    kv, near, other = call(
        project_kernel,
        (bf16(rows, 2 * model), bf16(2 * BLOCK, 2 * model), bf16(BLOCK, 2 * model)),
        [SMEM, *vmem(1), pl.BlockSpec(memory_space=pl.ANY)],
        place, tokens, w_qkv,
        flops=4 * rows * model * model,
        scratch=(pltpu.VMEM((steps, model, width), jnp.bfloat16), pltpu.SemaphoreType.DMA((steps,))),
    )
    pairs = [[i, i ^ 1] for i in range(0, count, 2)]
    near_all = lax.all_gather(near, AXES, axis_index_groups=pairs, tiled=True)
    swap = [(i, i + 1) for i in range(1, count - 1, 2)]
    swap += [(j, i) for i, j in swap]
    other_halo = lax.ppermute(other, AXES, swap)

    own = call(pool_near_kernel, bf16(BLOCK, 2 * model), vmem(1), near_all)
    found = [(("near", 0), near_all)]
    for _, bit, mode in ROUNDS[1:bits]:
        to = partners(bit, count)
        if mode == "ag":
            groups = [[i, to[i]] for i in range(count) if not i >> bit & 1]
            got = lax.all_gather(own, AXES, axis_index_groups=groups, tiled=True)
            ins = (got,)
        else:
            got = lax.ppermute(own, AXES, list(enumerate(to)))
            ins = (own, got)
        found.append(((mode, bit), got))
        if bit < bits - 1:
            own = call(pool_kernel, bf16(BLOCK, 2 * model), vmem(len(ins)), *ins)

    w_q = w_qkv[:, :model]
    q, num, tot = call(
        local_kernel,
        (bf16(rows, model), f32(rows, model), f32(rows, model)),
        [SMEM, *vmem(5)],
        place, tokens, w_q, kv, near_all, other_halo,
        flops=10**9,
        scratch=(
            pltpu.VMEM((rows + 2 * BLOCK, 2 * model), jnp.bfloat16),
            pltpu.VMEM((rows // 2, 2 * model), jnp.bfloat16),
        ),
    )
    for part in (found[0:4], found[4:8]):
        kinds = tuple(kind for kind, _ in part)
        num, tot = call(
            functools.partial(far_kernel, kinds),
            (f32(rows, model), f32(rows, model)),
            [SMEM, *vmem(3 + len(part))],
            place, q, num, tot, *[got for _, got in part],
            flops=10**9,
        )
    part = found[8:]
    return call(
        functools.partial(final_kernel, tuple(kind for kind, _ in part)),
        bf16(rows, model),
        [SMEM, *vmem(4 + len(part))],
        place, q, num, tot, w_out, *[got for _, got in part],
        flops=10**9,
        scratch=(pltpu.VMEM((rows, model), jnp.bfloat16),),
    )


def solution(mesh):
    return jax.shard_map(
        per_device,
        mesh=mesh,
        in_specs=(P(AXES, None), P(), P()),
        out_specs=P(AXES, None),
        check_vma=False,
    )
```

```python
import functools

import jax
import jax.numpy as jnp
import numpy as np
from jax import lax
from jax.experimental import pallas as pl
from jax.experimental.pallas import tpu as pltpu
from jax.sharding import PartitionSpec as P

HEADS = 8
BLOCK = 64
AXES = ("gx", "gy")
ROUNDS = ((4, "ag"), (5, "ag"), (6, "pp"), (7, "pp"), (8, "pp"))
FAR8 = (6, 7, 4, 5, 2, 3, 0, 1)
FAR4 = (3, 2, 1, 0)


def partners(bit, count):
    route = []
    for index in range(count):
        if bit == 3:
            z = index >> 1 & 7
            route.append(index & ~14 | FAR8[z] << 1)
        elif bit == 6:
            y = index >> 4 & 7
            route.append(index & ~112 | FAR8[y] << 4)
        elif bit == 8:
            x = index >> 7 & 3
            route.append(index & ~384 | FAR4[x] << 7)
        else:
            route.append(index ^ 1 << bit)
    return route


def vmem(count):
    return [pl.BlockSpec(memory_space=pltpu.VMEM)] * count


SMEM = pl.BlockSpec(memory_space=pltpu.SMEM)


def call(kernel, outs, in_specs, *args, flops=0, scratch=(), limit=24):
    return pl.pallas_call(
        kernel,
        out_shape=outs,
        in_specs=in_specs,
        out_specs=jax.tree.map(lambda _: pl.BlockSpec(memory_space=pltpu.VMEM), outs),
        scratch_shapes=list(scratch),
        compiler_params=pltpu.CompilerParams(vmem_limit_bytes=limit * 2**20),
        cost_estimate=pl.CostEstimate(flops=flops, bytes_accessed=2**20, transcendentals=0),
    )(*args)


def pool_matrix(rows):
    r = lax.broadcasted_iota(jnp.int32, (rows, 2 * rows), 0)
    c = lax.broadcasted_iota(jnp.int32, (rows, 2 * rows), 1)
    return jnp.where(c >> 1 == r, 0.5, 0.0).astype(jnp.bfloat16)


def pooled(block):
    return jnp.dot(
        pool_matrix(block.shape[0] // 2), block, preferred_element_type=jnp.float32
    ).astype(jnp.bfloat16)


def project_kernel(
    place, x_hbm, w_hbm, kv_ref, near_ref, other_ref, l3_ref, l6_ref, x_buf, w_buf, sems
):
    model = x_buf.shape[1]
    width = w_buf.shape[2]
    steps = w_buf.shape[0]
    x_copy = pltpu.make_async_copy(x_hbm, x_buf, sems.at[steps])
    x_copy.start()
    copies = []
    for step in range(steps):
        columns = pl.ds(model + step * width, width)
        copy = pltpu.make_async_copy(w_hbm.at[:, columns], w_buf.at[step], sems.at[step])
        copy.start()
        copies.append(copy)
    core = place[0]
    x_copy.wait()
    x = x_buf[...]
    pieces = []
    for step in range(steps):
        copies[step].wait()
        lanes = slice(step * width, (step + 1) * width)
        part = jnp.dot(x, w_buf[step], preferred_element_type=jnp.float32).astype(jnp.bfloat16)
        kv_ref[:, lanes] = part
        level_2 = pooled(pooled(part))
        near_ref[BLOCK:, lanes] = level_2
        level_3 = pooled(level_2)
        l3_ref[:, lanes] = level_3
        level_5 = pooled(pooled(level_3)).astype(jnp.float32)
        pieces += [level_5[:, at : at + 128] for at in range(0, width, 128)]
    level_6 = pooled(jnp.concatenate(pieces, axis=0).astype(jnp.bfloat16))
    size = level_6.shape[0]
    for copy in range(l6_ref.shape[0] // size):
        l6_ref[copy * size : (copy + 1) * size, :] = level_6
    last = x_buf.shape[0] - BLOCK
    low = pl.multiple_of(core * last, BLOCK)
    high = pl.multiple_of((1 - core) * last, BLOCK)
    near_ref[:BLOCK, :] = kv_ref[pl.ds(high, BLOCK), :]
    other_ref[...] = kv_ref[pl.ds(low, BLOCK), :]


def unpack_kernel(in_ref, out_ref):
    total = in_ref.shape[0]
    tiles = out_ref.shape[1] // 128
    each = 4
    row = lax.broadcasted_iota(jnp.int32, (BLOCK, total), 0)
    column = lax.broadcasted_iota(jnp.int32, (BLOCK, total), 1)
    source = (row >> 2) * (each * tiles) + (row & 3)
    for tile in range(tiles):
        pick = jnp.where(column == source + each * tile, 1.0, 0.0).astype(jnp.bfloat16)
        out_ref[:, tile * 128 : (tile + 1) * 128] = jnp.dot(
            pick, in_ref[...], preferred_element_type=jnp.float32
        ).astype(jnp.bfloat16)


def pool_kernel(*refs):
    ins, out_ref = refs[:-1], refs[-1]
    half = BLOCK // len(ins)
    for num, ref in enumerate(ins):
        out_ref[num * half : (num + 1) * half, :] = pooled(ref[...])


def attend_pair(q, keys, values, ones):
    rows = q.shape[0]
    lane = lax.broadcasted_iota(jnp.int32, q.shape, 1)
    first = lane < 64
    zero = jnp.zeros_like(q)
    both = jnp.concatenate([jnp.where(first, q, zero), jnp.where(first, zero, q)], axis=0)
    scores = lax.dot_general(
        both, keys, (((1,), (1,)), ((), ())), preferred_element_type=jnp.float32
    )
    weights = jnp.exp(scores).astype(jnp.bfloat16)
    sums = jnp.dot(
        weights, jnp.concatenate([values, ones], axis=1), preferred_element_type=jnp.float32
    )
    num = jnp.where(first, sums[:rows, :128], sums[rows:, :128])
    tot = jnp.where(first, sums[:rows, 128:], sums[rows:, 128:])
    return num, tot


def local_kernel(place, x_ref, w_ref, kv_ref, near_ref, other_ref, q_ref, num_ref, tot_ref, pad, l1):
    rows, model = x_ref.shape
    blocks = rows // BLOCK
    q_ref[...] = (
        jnp.dot(x_ref[...], w_ref[...], preferred_element_type=jnp.float32)
        .astype(jnp.bfloat16) * jnp.bfloat16(0.125)
    )
    core = place[0]
    sib_halo = near_ref[pl.ds(pl.multiple_of((1 - core) * 2 * BLOCK, BLOCK), BLOCK), :]
    other = other_ref[...]
    is_first = core == 0
    pad[:BLOCK, :] = jnp.where(is_first, other, sib_halo)
    pad[BLOCK : BLOCK + rows, :] = kv_ref[...]
    pad[BLOCK + rows :, :] = jnp.where(is_first, sib_halo, other)
    l1[...] = pooled(kv_ref[...])
    key_row = lax.broadcasted_iota(jnp.int32, (4 * BLOCK, 128), 0)
    for i in range(blocks):
        ones = jnp.ones((4 * BLOCK, 128), jnp.float32)
        if i == 0:
            ones = jnp.where((key_row < BLOCK) & (place[1] == 1), 0.0, ones)
        if i == blocks - 1:
            ones = jnp.where((key_row >= 2 * BLOCK) & (key_row < 3 * BLOCK) & (place[2] == 1), 0.0, ones)
        ones = ones.astype(jnp.bfloat16)
        sib = (i >> 1) ^ 1
        here = slice(i * BLOCK, (i + 1) * BLOCK)
        for lanes in range(0, model, 128):
            kl = slice(lanes, lanes + 128)
            vl = slice(model + lanes, model + lanes + 128)
            keys = jnp.concatenate(
                [pad[i * BLOCK : (i + 3) * BLOCK, kl], l1[sib * BLOCK : (sib + 1) * BLOCK, kl]], axis=0
            )
            values = jnp.concatenate(
                [pad[i * BLOCK : (i + 3) * BLOCK, vl], l1[sib * BLOCK : (sib + 1) * BLOCK, vl]], axis=0
            )
            num, tot = attend_pair(q_ref[here, kl], keys, values, ones)
            num_ref[here, kl] = num
            tot_ref[here, kl] = tot


def sibling_blocks(place, kinds, refs):
    blocks = []
    for kind, ref in zip(kinds, refs):
        if kind == "near":
            start = (1 - place[0]) * 2 * BLOCK + BLOCK
            blocks.append(ref[pl.ds(pl.multiple_of(start, BLOCK), BLOCK), :])
        elif kind == "low":
            chip = place[3]
            for shift in range(3):
                rows = BLOCK << shift
                start = ((chip >> shift) ^ 1) * rows
                block = ref[pl.ds(pl.multiple_of(start, BLOCK), rows), :]
                for _ in range(shift):
                    block = pooled(block)
                blocks.append(block)
        elif kind == "pp":
            blocks.append(ref[...])
        else:
            start = (1 - place[kind]) * BLOCK
            blocks.append(ref[pl.ds(pl.multiple_of(start, BLOCK), BLOCK), :])
    return jnp.concatenate(blocks, axis=0)


def far_sums(far, q, lanes, model):
    keys = far[:, lanes : lanes + 128]
    values = far[:, model + lanes : model + lanes + 128]
    return attend_pair(q, keys, values, jnp.ones(values.shape, jnp.bfloat16))


def far_kernel(kinds, place, q_ref, num_in, tot_in, *refs):
    num_ref, tot_ref = refs[-2:]
    model = q_ref.shape[1]
    far = sibling_blocks(place, kinds, refs[:-2])
    for lanes in range(0, model, 128):
        at = slice(lanes, lanes + 128)
        num, tot = far_sums(far, q_ref[:, at], lanes, model)
        num_ref[:, at] = num_in[:, at] + num
        tot_ref[:, at] = tot_in[:, at] + tot


def final_kernel(kinds, place, q_ref, num_in, tot_in, w_ref, *refs):
    out_ref, att = refs[-2:]
    model = q_ref.shape[1]
    far = sibling_blocks(place, kinds, refs[:-2])
    for lanes in range(0, model, 128):
        at = slice(lanes, lanes + 128)
        num, tot = far_sums(far, q_ref[:, at], lanes, model)
        att[:, at] = ((num_in[:, at] + num) / (tot_in[:, at] + tot)).astype(jnp.bfloat16)
    out_ref[...] = jnp.dot(att[...], w_ref[...], preferred_element_type=jnp.float32).astype(
        jnp.bfloat16
    )


def per_device(tokens, w_qkv, w_out):
    rows, model = tokens.shape
    index = lax.axis_index(AXES)
    inner = lax.axis_index("gy")
    count = lax.axis_size(AXES)
    members = lax.axis_size("gy")
    bits = count.bit_length() - 1
    place = jnp.stack(
        [index & 1, (index == 0).astype(jnp.int32), (index == count - 1).astype(jnp.int32), inner >> 1]
        + [(index >> bit) & 1 for bit in range(4, bits)]
    ).astype(jnp.int32)
    bf16 = lambda *shape: jax.ShapeDtypeStruct(shape, jnp.bfloat16)
    f32 = lambda *shape: jax.ShapeDtypeStruct(shape, jnp.float32)
    anywhere = pl.BlockSpec(memory_space=pl.ANY)
    steps = 4
    width = 2 * model // steps
    packed = 4 * 2 * model // 128
    kv, near, other, level_3, level_6 = call(
        project_kernel,
        (
            bf16(rows, 2 * model),
            bf16(2 * BLOCK, 2 * model),
            bf16(BLOCK, 2 * model),
            bf16(BLOCK // 2, 2 * model),
            bf16(members * packed, 128),
        ),
        [SMEM, anywhere, anywhere],
        place, tokens, w_qkv,
        flops=4 * rows * model * model,
        scratch=(
            pltpu.VMEM((rows, model), jnp.bfloat16),
            pltpu.VMEM((steps, model, width), jnp.bfloat16),
            pltpu.SemaphoreType.DMA((steps + 1,)),
        ),
        limit=56,
    )
    low = lax.all_gather(level_3, "gy", tiled=True)
    pairs = [[i, i ^ 1] for i in range(0, count, 2)]
    near_all = lax.all_gather(near, AXES, axis_index_groups=pairs, tiled=True)
    spread = lax.all_to_all(level_6, "gy", 0, 0, tiled=True)
    swap = [(i, i + 1) for i in range(1, count - 1, 2)]
    swap += [(j, i) for i, j in swap]
    other_halo = lax.ppermute(other, AXES, swap)

    own = call(unpack_kernel, bf16(BLOCK, 2 * model), vmem(1), spread)
    found = []
    for bit, mode in ROUNDS:
        to = partners(bit, count)
        if mode == "ag":
            groups = [[i, to[i]] for i in range(count) if not i >> bit & 1]
            got = lax.all_gather(own, AXES, axis_index_groups=groups, tiled=True)
            ins = (got,)
            found.append((bit, got))
        else:
            got = lax.ppermute(own, AXES, list(enumerate(to)))
            ins = (own, got)
            found.append(("pp", got))
        if bit < bits - 1:
            own = call(pool_kernel, bf16(BLOCK, 2 * model), vmem(len(ins)), *ins)

    w_q = w_qkv[:, :model]
    q, num, tot = call(
        local_kernel,
        (bf16(rows, model), f32(rows, model), f32(rows, model)),
        [SMEM, *vmem(5)],
        place, tokens, w_q, kv, near_all, other_halo,
        flops=10**9,
        scratch=(
            pltpu.VMEM((rows + 2 * BLOCK, 2 * model), jnp.bfloat16),
            pltpu.VMEM((rows // 2, 2 * model), jnp.bfloat16),
        ),
    )
    for part in (found[:3], [("near", near_all), ("low", low)]):
        num, tot = call(
            functools.partial(far_kernel, tuple(kind for kind, _ in part)),
            (f32(rows, model), f32(rows, model)),
            [SMEM, *vmem(3 + len(part))],
            place, q, num, tot, *[got for _, got in part],
            flops=10**9,
        )
    part = found[3:]
    return call(
        functools.partial(final_kernel, tuple(kind for kind, _ in part)),
        bf16(rows, model),
        [SMEM, *vmem(4 + len(part))],
        place, q, num, tot, w_out, *[got for _, got in part],
        flops=10**9,
        scratch=(pltpu.VMEM((rows, model), jnp.bfloat16),),
    )


def solution(mesh):
    return jax.shard_map(
        per_device,
        mesh=mesh,
        in_specs=(P(AXES, None), P(), P()),
        out_specs=P(AXES, None),
        check_vma=False,
    )
```

```python
import functools

import jax
import jax.numpy as jnp
import numpy as np
from jax import lax
from jax.experimental import pallas as pl
from jax.experimental.pallas import tpu as pltpu
from jax.sharding import PartitionSpec as P

HEADS = 8
BLOCK = 64
AXES = ("gx", "gy")
FAR8 = (6, 7, 4, 5, 2, 3, 0, 1)
FAR4 = (3, 2, 1, 0)


def partners(bit, count):
    route = []
    for index in range(count):
        if bit == 3:
            z = index >> 1 & 7
            route.append(index & ~14 | FAR8[z] << 1)
        elif bit == 6:
            y = index >> 4 & 7
            route.append(index & ~112 | FAR8[y] << 4)
        elif bit == 8:
            x = index >> 7 & 3
            route.append(index & ~384 | FAR4[x] << 7)
        else:
            route.append(index ^ 1 << bit)
    return route


def vmem(count):
    return [pl.BlockSpec(memory_space=pltpu.VMEM)] * count


SMEM = pl.BlockSpec(memory_space=pltpu.SMEM)


def call(kernel, outs, in_specs, *args, flops=0, scratch=(), limit=24, after=()):
    count = len(args)

    def body(*refs):
        kernel(*refs[:count], *refs[count + len(after) :])

    return pl.pallas_call(
        body,
        out_shape=outs,
        in_specs=list(in_specs) + [pl.BlockSpec(memory_space=pl.ANY)] * len(after),
        out_specs=jax.tree.map(lambda _: pl.BlockSpec(memory_space=pltpu.VMEM), outs),
        scratch_shapes=list(scratch),
        compiler_params=pltpu.CompilerParams(vmem_limit_bytes=limit * 2**20),
        cost_estimate=pl.CostEstimate(flops=flops, bytes_accessed=2**20, transcendentals=0),
    )(*args, *after)


def pool_matrix(rows):
    r = lax.broadcasted_iota(jnp.int32, (rows, 2 * rows), 0)
    c = lax.broadcasted_iota(jnp.int32, (rows, 2 * rows), 1)
    return jnp.where(c >> 1 == r, 0.5, 0.0).astype(jnp.bfloat16)


def pooled(block):
    return jnp.dot(
        pool_matrix(block.shape[0] // 2), block, preferred_element_type=jnp.float32
    ).astype(jnp.bfloat16)


def project_kernel(
    place, x_hbm, w_hbm, kv_ref, near_ref, other_ref, packed_ref, x_buf, w_buf, part_buf, sems
):
    rows, model = x_buf.shape
    width = w_buf.shape[2]
    steps = w_buf.shape[0]
    x_copy = pltpu.make_async_copy(x_hbm, x_buf, sems.at[steps])
    x_copy.start()
    copies = []
    for step in range(steps):
        columns = pl.ds(model + step * width, width)
        copy = pltpu.make_async_copy(w_hbm.at[:, columns], w_buf.at[step], sems.at[step])
        copy.start()
        copies.append(copy)
    x_copy.wait()
    x = x_buf[...]
    pieces = []
    for step in range(steps):
        copies[step].wait()
        lanes = slice(step * width, (step + 1) * width)
        part = jnp.dot(x, w_buf[step], preferred_element_type=jnp.float32).astype(jnp.bfloat16)
        kv_ref[:, lanes] = part
        wide = part.astype(jnp.float32)
        for at in range(0, width, 128):
            tile = (step * width + at) // 128
            part_buf[tile] = wide[:, at : at + 128]
            size = rows
            while size > 8:
                size //= 2
                even = part_buf[tile, pl.ds(0, size, stride=2), :]
                odd = part_buf[tile, pl.ds(1, size, stride=2), :]
                level = ((even + odd) * 0.5).astype(jnp.bfloat16)
                if size == BLOCK:
                    near_ref[BLOCK:, tile * 128 : (tile + 1) * 128] = level
                part_buf[tile, :size, :] = level.astype(jnp.float32)
            pieces.append(level.astype(jnp.float32))
    packed = pooled(pooled(jnp.concatenate(pieces, axis=0).astype(jnp.bfloat16)))
    size = packed.shape[0]
    for copy in range(packed_ref.shape[0] // size):
        packed_ref[copy * size : (copy + 1) * size, :] = packed
    core = place[0]
    last = rows - BLOCK
    low = pl.multiple_of(core * last, BLOCK)
    high = pl.multiple_of((1 - core) * last, BLOCK)
    near_ref[:BLOCK, :] = kv_ref[pl.ds(high, BLOCK), :]
    other_ref[...] = kv_ref[pl.ds(low, BLOCK), :]


def unpack_kernel(in_ref, out_ref):
    total = in_ref.shape[0]
    tiles = out_ref.shape[1] // 128
    row = lax.broadcasted_iota(jnp.int32, (BLOCK, total), 0)
    column = lax.broadcasted_iota(jnp.int32, (BLOCK, total), 1)
    source = (row >> 1) * (2 * tiles) + (row & 1)
    for tile in range(tiles):
        pick = jnp.where(column == source + 2 * tile, 1.0, 0.0).astype(jnp.bfloat16)
        out_ref[:, tile * 128 : (tile + 1) * 128] = jnp.dot(
            pick, in_ref[...], preferred_element_type=jnp.float32
        ).astype(jnp.bfloat16)


def pool_near_kernel(near_ref, out_ref):
    out_ref[: BLOCK // 2, :] = pooled(near_ref[BLOCK : 2 * BLOCK, :])
    out_ref[BLOCK // 2 :, :] = pooled(near_ref[3 * BLOCK :, :])


def pool_kernel(*refs):
    ins, out_ref = refs[:-1], refs[-1]
    half = BLOCK // len(ins)
    for num, ref in enumerate(ins):
        out_ref[num * half : (num + 1) * half, :] = pooled(ref[...])


def attend_pair(q, keys, values, ones):
    rows = q.shape[0]
    lane = lax.broadcasted_iota(jnp.int32, q.shape, 1)
    first = lane < 64
    zero = jnp.zeros_like(q)
    both = jnp.concatenate([jnp.where(first, q, zero), jnp.where(first, zero, q)], axis=0)
    scores = lax.dot_general(
        both, keys, (((1,), (1,)), ((), ())), preferred_element_type=jnp.float32
    )
    weights = jnp.exp(scores).astype(jnp.bfloat16)
    sums = jnp.dot(
        weights, jnp.concatenate([values, ones], axis=1), preferred_element_type=jnp.float32
    )
    num = jnp.where(first, sums[:rows, :128], sums[rows:, :128])
    tot = jnp.where(first, sums[:rows, 128:], sums[rows:, 128:])
    return num, tot


def local_kernel(
    place, x_ref, w_hbm, kv_ref, near_ref, other_ref, q_ref, num_ref, tot_ref, pad, l1, w_ref, sem
):
    rows, model = x_ref.shape
    blocks = rows // BLOCK
    copy = pltpu.make_async_copy(w_hbm.at[:, pl.ds(0, model)], w_ref, sem)
    copy.start()
    core = place[0]
    sib_halo = near_ref[pl.ds(pl.multiple_of((1 - core) * 2 * BLOCK, BLOCK), BLOCK), :]
    other = other_ref[...]
    is_first = core == 0
    pad[:BLOCK, :] = jnp.where(is_first, other, sib_halo)
    pad[BLOCK : BLOCK + rows, :] = kv_ref[...]
    pad[BLOCK + rows :, :] = jnp.where(is_first, sib_halo, other)
    l1[...] = pooled(kv_ref[...])
    copy.wait()
    q_ref[...] = (
        jnp.dot(x_ref[...], w_ref[...], preferred_element_type=jnp.float32)
        .astype(jnp.bfloat16) * jnp.bfloat16(0.125)
    )
    key_row = lax.broadcasted_iota(jnp.int32, (4 * BLOCK, 128), 0)
    for i in range(blocks):
        ones = jnp.ones((4 * BLOCK, 128), jnp.float32)
        if i == 0:
            ones = jnp.where((key_row < BLOCK) & (place[1] == 1), 0.0, ones)
        if i == blocks - 1:
            ones = jnp.where((key_row >= 2 * BLOCK) & (key_row < 3 * BLOCK) & (place[2] == 1), 0.0, ones)
        ones = ones.astype(jnp.bfloat16)
        sib = (i >> 1) ^ 1
        here = slice(i * BLOCK, (i + 1) * BLOCK)
        for lanes in range(0, model, 128):
            kl = slice(lanes, lanes + 128)
            vl = slice(model + lanes, model + lanes + 128)
            keys = jnp.concatenate(
                [pad[i * BLOCK : (i + 3) * BLOCK, kl], l1[sib * BLOCK : (sib + 1) * BLOCK, kl]], axis=0
            )
            values = jnp.concatenate(
                [pad[i * BLOCK : (i + 3) * BLOCK, vl], l1[sib * BLOCK : (sib + 1) * BLOCK, vl]], axis=0
            )
            num, tot = attend_pair(q_ref[here, kl], keys, values, ones)
            num_ref[here, kl] = num
            tot_ref[here, kl] = tot


def sibling_blocks(place, kinds, refs):
    blocks = []
    for kind, ref in zip(kinds, refs):
        if kind == "near":
            start = (1 - place[0]) * 2 * BLOCK + BLOCK
            blocks.append(ref[pl.ds(pl.multiple_of(start, BLOCK), BLOCK), :])
        else:
            blocks.append(ref[...])
    return jnp.concatenate(blocks, axis=0)


def far_sums(far, q, lanes, model):
    keys = far[:, lanes : lanes + 128]
    values = far[:, model + lanes : model + lanes + 128]
    return attend_pair(q, keys, values, jnp.ones(values.shape, jnp.bfloat16))


def far_kernel(kinds, place, q_ref, num_in, tot_in, *refs):
    num_ref, tot_ref = refs[-2:]
    model = q_ref.shape[1]
    far = sibling_blocks(place, kinds, refs[:-2])
    for lanes in range(0, model, 128):
        at = slice(lanes, lanes + 128)
        num, tot = far_sums(far, q_ref[:, at], lanes, model)
        num_ref[:, at] = num_in[:, at] + num
        tot_ref[:, at] = tot_in[:, at] + tot


def final_kernel(kinds, place, q_ref, num_in, tot_in, w_ref, *refs):
    out_ref, att = refs[-2:]
    model = q_ref.shape[1]
    far = sibling_blocks(place, kinds, refs[:-2])
    for lanes in range(0, model, 128):
        at = slice(lanes, lanes + 128)
        num, tot = far_sums(far, q_ref[:, at], lanes, model)
        att[:, at] = ((num_in[:, at] + num) / (tot_in[:, at] + tot)).astype(jnp.bfloat16)
    out_ref[...] = jnp.dot(att[...], w_ref[...], preferred_element_type=jnp.float32).astype(
        jnp.bfloat16
    )


def per_device(tokens, w_qkv, w_out):
    rows, model = tokens.shape
    index = lax.axis_index(AXES)
    count = lax.axis_size(AXES)
    place = jnp.stack(
        [index & 1, (index == 0).astype(jnp.int32), (index == count - 1).astype(jnp.int32)]
    ).astype(jnp.int32)
    bf16 = lambda *shape: jax.ShapeDtypeStruct(shape, jnp.bfloat16)
    f32 = lambda *shape: jax.ShapeDtypeStruct(shape, jnp.float32)
    anywhere = pl.BlockSpec(memory_space=pl.ANY)
    steps = 2
    width = 2 * model // steps
    members = 32
    packed = 2 * 2 * model // 128
    block = bf16(BLOCK, 2 * model)
    kv, near, other, level_7 = call(
        project_kernel,
        (bf16(rows, 2 * model), bf16(2 * BLOCK, 2 * model), block, bf16(members * packed, 128)),
        [SMEM, anywhere, anywhere],
        place, tokens, w_qkv,
        flops=4 * rows * model * model,
        scratch=(
            pltpu.VMEM((rows, model), jnp.bfloat16),
            pltpu.VMEM((steps, model, width), jnp.bfloat16),
            pltpu.VMEM((2 * model // 128, rows, 128), jnp.float32),
            pltpu.SemaphoreType.DMA((steps + 1,)),
        ),
        limit=56,
    )
    pairs = [[i, i ^ 1] for i in range(0, count, 2)]
    near_all = lax.all_gather(near, AXES, axis_index_groups=pairs, tiled=True)
    swap = [(i, i + 1) for i in range(1, count - 1, 2)]
    swap += [(j, i) for i, j in swap]
    other_halo = lax.ppermute(other, AXES, swap)

    def exchange(own, bit):
        return lax.ppermute(own, AXES, list(enumerate(partners(bit, count))))

    def pool(own, got, *after):
        return call(pool_kernel, block, vmem(2), own, got, after=after)

    def far(num, tot, *part, after=()):
        return call(
            functools.partial(far_kernel, tuple(kind for kind, _ in part)),
            (f32(rows, model), f32(rows, model)),
            [SMEM, *vmem(3 + len(part))],
            place, q, num, tot, *[got for _, got in part],
            flops=10**9,
            after=after,
        )

    own_3 = call(pool_near_kernel, block, vmem(1), near_all)
    sib_3 = exchange(own_3, 1)
    level_7, _ = lax.optimization_barrier((level_7, own_3))
    teams = [list(range(i, i + members)) for i in range(0, count, members)]
    spread = lax.all_to_all(level_7, AXES, 0, 0, axis_index_groups=teams, tiled=True)
    own_7 = call(unpack_kernel, block, vmem(1), spread)
    sib_7 = exchange(own_7, 5)
    own_4 = pool(own_3, sib_3, own_7)
    sib_4 = exchange(own_4, 2)
    q, num, tot = call(
        local_kernel,
        (bf16(rows, model), f32(rows, model), f32(rows, model)),
        [SMEM, *vmem(1), anywhere, *vmem(3)],
        place, tokens, w_qkv, kv, near_all, other_halo,
        flops=10**9,
        scratch=(
            pltpu.VMEM((rows + 2 * BLOCK, 2 * model), jnp.bfloat16),
            pltpu.VMEM((rows // 2, 2 * model), jnp.bfloat16),
            pltpu.VMEM((model, model), jnp.bfloat16),
            pltpu.SemaphoreType.DMA(()),
        ),
        after=(own_4,),
    )
    own_8 = pool(own_7, sib_7, q)
    sib_8 = exchange(own_8, 6)
    own_5 = pool(own_4, sib_4, own_8)
    sib_5 = exchange(own_5, 3)
    num, tot = far(
        num, tot, ("near", near_all), ("pp", sib_3), ("pp", sib_4), ("pp", sib_7), after=(own_5,)
    )
    own_9 = pool(own_8, sib_8, num)
    sib_9 = exchange(own_9, 7)
    own_6 = pool(own_5, sib_5, own_9)
    sib_6 = exchange(own_6, 4)
    own_10 = pool(own_9, sib_9, own_6)
    sib_10 = exchange(own_10, 8)
    num, tot = far(
        num, tot, ("pp", sib_5), ("pp", sib_6), ("pp", sib_8), ("pp", sib_9), after=(own_10,)
    )
    return call(
        functools.partial(final_kernel, ("pp",)),
        bf16(rows, model),
        [SMEM, *vmem(5)],
        place, q, num, tot, w_out, sib_10,
        flops=10**9,
        scratch=(pltpu.VMEM((rows, model), jnp.bfloat16),),
    )


def solution(mesh):
    return jax.shard_map(
        per_device,
        mesh=mesh,
        in_specs=(P(AXES, None), P(), P()),
        out_specs=P(AXES, None),
        check_vma=False,
    )
```

```python
import functools

import jax
import jax.numpy as jnp
import numpy as np
from jax import lax
from jax.experimental import pallas as pl
from jax.experimental.pallas import tpu as pltpu
from jax.sharding import PartitionSpec as P

HEADS = 8
BLOCK = 64
AXES = ("gx", "gy")
FAR8 = (6, 7, 4, 5, 2, 3, 0, 1)
FAR4 = (3, 2, 1, 0)


def partners(bit, count):
    route = []
    for index in range(count):
        if bit == 3:
            z = index >> 1 & 7
            route.append(index & ~14 | FAR8[z] << 1)
        elif bit == 6:
            y = index >> 4 & 7
            route.append(index & ~112 | FAR8[y] << 4)
        elif bit == 8:
            x = index >> 7 & 3
            route.append(index & ~384 | FAR4[x] << 7)
        else:
            route.append(index ^ 1 << bit)
    return route


def vmem(count):
    return [pl.BlockSpec(memory_space=pltpu.VMEM)] * count


SMEM = pl.BlockSpec(memory_space=pltpu.SMEM)


def call(kernel, outs, in_specs, *args, flops=0, scratch=(), limit=24, after=()):
    count = len(args)

    def body(*refs):
        kernel(*refs[:count], *refs[count + len(after) :])

    return pl.pallas_call(
        body,
        out_shape=outs,
        in_specs=list(in_specs) + [pl.BlockSpec(memory_space=pl.ANY)] * len(after),
        out_specs=jax.tree.map(lambda _: pl.BlockSpec(memory_space=pltpu.VMEM), outs),
        scratch_shapes=list(scratch),
        compiler_params=pltpu.CompilerParams(vmem_limit_bytes=limit * 2**20),
        cost_estimate=pl.CostEstimate(flops=flops, bytes_accessed=2**20, transcendentals=0),
    )(*args, *after)


def pool_matrix(rows):
    r = lax.broadcasted_iota(jnp.int32, (rows, 2 * rows), 0)
    c = lax.broadcasted_iota(jnp.int32, (rows, 2 * rows), 1)
    return jnp.where(c >> 1 == r, 0.5, 0.0).astype(jnp.bfloat16)


def pooled(block):
    return jnp.dot(
        pool_matrix(block.shape[0] // 2), block, preferred_element_type=jnp.float32
    ).astype(jnp.bfloat16)


def project_kernel(
    place, x_hbm, w_hbm, kv_ref, near_ref, other_ref, packed_ref, x_buf, w_buf, part_buf, sems
):
    rows, model = x_buf.shape
    width = w_buf.shape[2]
    steps = w_buf.shape[0]
    x_copy = pltpu.make_async_copy(x_hbm, x_buf, sems.at[steps])
    x_copy.start()
    copies = []
    for step in range(steps):
        columns = pl.ds(model + step * width, width)
        copy = pltpu.make_async_copy(w_hbm.at[:, columns], w_buf.at[step], sems.at[step])
        copy.start()
        copies.append(copy)
    x_copy.wait()
    x = x_buf[...]
    pieces = []
    for step in range(steps):
        copies[step].wait()
        lanes = slice(step * width, (step + 1) * width)
        part = jnp.dot(x, w_buf[step], preferred_element_type=jnp.float32).astype(jnp.bfloat16)
        kv_ref[:, lanes] = part
        wide = part.astype(jnp.float32)
        for at in range(0, width, 128):
            tile = (step * width + at) // 128
            part_buf[tile] = wide[:, at : at + 128]
            size = rows
            while size > 8:
                size //= 2
                even = part_buf[tile, pl.ds(0, size, stride=2), :]
                odd = part_buf[tile, pl.ds(1, size, stride=2), :]
                level = ((even + odd) * 0.5).astype(jnp.bfloat16)
                if size == BLOCK:
                    near_ref[BLOCK:, tile * 128 : (tile + 1) * 128] = level
                part_buf[tile, :size, :] = level.astype(jnp.float32)
            pieces.append(level.astype(jnp.float32))
    packed = pooled(jnp.concatenate(pieces, axis=0).astype(jnp.bfloat16))
    size = packed.shape[0]
    for copy in range(packed_ref.shape[0] // size):
        packed_ref[copy * size : (copy + 1) * size, :] = packed
    core = place[0] & 1
    last = rows - BLOCK
    low = pl.multiple_of(core * last, BLOCK)
    high = pl.multiple_of((1 - core) * last, BLOCK)
    near_ref[:BLOCK, :] = kv_ref[pl.ds(high, BLOCK), :]
    other_ref[...] = kv_ref[pl.ds(low, BLOCK), :]


def unpack_kernel(place, in_ref, own_6_ref, own_7_ref):
    half = in_ref.shape[0] // 2
    tiles = own_6_ref.shape[1] // 128
    row = lax.broadcasted_iota(jnp.int32, (BLOCK, half), 0)
    column = lax.broadcasted_iota(jnp.int32, (BLOCK, half), 1)
    source = (row >> 2) * (4 * tiles) + (row & 3)
    upper = (place[0] >> 4) & 1
    for tile in range(tiles):
        lanes = slice(tile * 128, (tile + 1) * 128)
        pick = jnp.where(column == source + 4 * tile, 1.0, 0.0).astype(jnp.bfloat16)
        parts = [
            jnp.dot(pick, in_ref[at : at + half, :], preferred_element_type=jnp.float32)
            for at in (0, half)
        ]
        own_6_ref[:, lanes] = jnp.where(upper == 1, parts[1], parts[0]).astype(jnp.bfloat16)
        own_7_ref[:, lanes] = pooled(jnp.concatenate(parts, axis=0).astype(jnp.bfloat16))


def pool_near_kernel(near_ref, sib_ref, out_ref):
    out_ref[: BLOCK // 2, :] = pooled(near_ref[BLOCK:, :])
    out_ref[BLOCK // 2 :, :] = pooled(sib_ref[BLOCK:, :])


def pool_kernel(*refs):
    ins, out_ref = refs[:-1], refs[-1]
    half = BLOCK // len(ins)
    for num, ref in enumerate(ins):
        out_ref[num * half : (num + 1) * half, :] = pooled(ref[...])


def attend_pair(q, keys, values, ones):
    rows = q.shape[0]
    lane = lax.broadcasted_iota(jnp.int32, q.shape, 1)
    first = lane < 64
    zero = jnp.zeros_like(q)
    both = jnp.concatenate([jnp.where(first, q, zero), jnp.where(first, zero, q)], axis=0)
    scores = lax.dot_general(
        both, keys, (((1,), (1,)), ((), ())), preferred_element_type=jnp.float32
    )
    weights = jnp.exp(scores).astype(jnp.bfloat16)
    sums = jnp.dot(
        weights, jnp.concatenate([values, ones], axis=1), preferred_element_type=jnp.float32
    )
    num = jnp.where(first, sums[:rows, :128], sums[rows:, :128])
    tot = jnp.where(first, sums[:rows, 128:], sums[rows:, 128:])
    return num, tot


def local_kernel(
    count, place, x_ref, w_hbm, kv_ref, near_ref, other_ref, q_ref, num_ref, tot_ref, pad, l1, w_ref, sem
):
    rows, model = x_ref.shape
    blocks = rows // BLOCK
    copy = pltpu.make_async_copy(w_hbm.at[:, pl.ds(0, model)], w_ref, sem)
    copy.start()
    core = place[0] & 1
    sib_halo = near_ref[:BLOCK, :]
    other = other_ref[...]
    is_first = core == 0
    pad[:BLOCK, :] = jnp.where(is_first, other, sib_halo)
    pad[BLOCK : BLOCK + rows, :] = kv_ref[...]
    pad[BLOCK + rows :, :] = jnp.where(is_first, sib_halo, other)
    l1[...] = pooled(kv_ref[...])
    copy.wait()
    q_ref[...] = (
        jnp.dot(x_ref[...], w_ref[...], preferred_element_type=jnp.float32)
        .astype(jnp.bfloat16) * jnp.bfloat16(0.125)
    )
    key_row = lax.broadcasted_iota(jnp.int32, (4 * BLOCK, 128), 0)
    for i in range(blocks):
        ones = jnp.ones((4 * BLOCK, 128), jnp.float32)
        if i == 0:
            ones = jnp.where((key_row < BLOCK) & (place[0] == 0), 0.0, ones)
        if i == blocks - 1:
            ones = jnp.where((key_row >= 2 * BLOCK) & (key_row < 3 * BLOCK) & (place[0] == count - 1), 0.0, ones)
        ones = ones.astype(jnp.bfloat16)
        sib = (i >> 1) ^ 1
        here = slice(i * BLOCK, (i + 1) * BLOCK)
        for lanes in range(0, model, 128):
            kl = slice(lanes, lanes + 128)
            vl = slice(model + lanes, model + lanes + 128)
            keys = jnp.concatenate(
                [pad[i * BLOCK : (i + 3) * BLOCK, kl], l1[sib * BLOCK : (sib + 1) * BLOCK, kl]], axis=0
            )
            values = jnp.concatenate(
                [pad[i * BLOCK : (i + 3) * BLOCK, vl], l1[sib * BLOCK : (sib + 1) * BLOCK, vl]], axis=0
            )
            num, tot = attend_pair(q_ref[here, kl], keys, values, ones)
            num_ref[here, kl] = num
            tot_ref[here, kl] = tot


def far_blocks(refs):
    return jnp.concatenate(
        [ref[BLOCK:, :] if ref.shape[0] == 2 * BLOCK else ref[...] for ref in refs], axis=0
    )


def far_sums(far, q, lanes, model):
    keys = far[:, lanes : lanes + 128]
    values = far[:, model + lanes : model + lanes + 128]
    return attend_pair(q, keys, values, jnp.ones(values.shape, jnp.bfloat16))


def far_kernel(q_ref, num_in, tot_in, *refs):
    num_ref, tot_ref = refs[-2:]
    model = q_ref.shape[1]
    far = far_blocks(refs[:-2])
    for lanes in range(0, model, 128):
        at = slice(lanes, lanes + 128)
        num, tot = far_sums(far, q_ref[:, at], lanes, model)
        num_ref[:, at] = num_in[:, at] + num
        tot_ref[:, at] = tot_in[:, at] + tot


def final_kernel(q_ref, num_in, tot_in, w_ref, *refs):
    out_ref, att = refs[-2:]
    model = q_ref.shape[1]
    far = far_blocks(refs[:-2])
    for lanes in range(0, model, 128):
        at = slice(lanes, lanes + 128)
        num, tot = far_sums(far, q_ref[:, at], lanes, model)
        att[:, at] = ((num_in[:, at] + num) / (tot_in[:, at] + tot)).astype(jnp.bfloat16)
    out_ref[...] = jnp.dot(att[...], w_ref[...], preferred_element_type=jnp.float32).astype(
        jnp.bfloat16
    )


def per_device(tokens, w_qkv, w_out):
    rows, model = tokens.shape
    index = lax.axis_index(AXES)
    count = lax.axis_size(AXES)
    place = index.astype(jnp.int32).reshape(1)
    bf16 = lambda *shape: jax.ShapeDtypeStruct(shape, jnp.bfloat16)
    f32 = lambda *shape: jax.ShapeDtypeStruct(shape, jnp.float32)
    anywhere = pl.BlockSpec(memory_space=pl.ANY)
    steps = 2
    width = 2 * model // steps
    members = 32
    packed = 4 * 2 * model // 128
    block = bf16(BLOCK, 2 * model)
    kv, near, other, level_6 = call(
        project_kernel,
        (bf16(rows, 2 * model), bf16(2 * BLOCK, 2 * model), block, bf16(members * packed, 128)),
        [SMEM, anywhere, anywhere],
        place, tokens, w_qkv,
        flops=4 * rows * model * model,
        scratch=(
            pltpu.VMEM((rows, model), jnp.bfloat16),
            pltpu.VMEM((steps, model, width), jnp.bfloat16),
            pltpu.VMEM((2 * model // 128, rows, 128), jnp.float32),
            pltpu.SemaphoreType.DMA((steps + 1,)),
        ),
        limit=56,
    )
    swap = [(i, i + 1) for i in range(1, count - 1, 2)]
    swap += [(j, i) for i, j in swap]
    def exchange(own, bit):
        return lax.ppermute(own, AXES, list(enumerate(partners(bit, count))))

    def pool(own, got, *after):
        return call(pool_kernel, block, vmem(2), own, got, after=after)

    def far(num, tot, *part, after=()):
        return call(
            far_kernel,
            (f32(rows, model), f32(rows, model)),
            vmem(3 + len(part)),
            q, num, tot, *part,
            flops=10**9,
            after=after,
        )

    teams = [list(range(i, i + members)) for i in range(0, count, members)]
    spread = lax.all_to_all(level_6, AXES, 0, 0, axis_index_groups=teams, tiled=True)
    near_sib = exchange(near, 0)
    other_halo = lax.ppermute(other, AXES, swap)

    own_3 = call(pool_near_kernel, block, vmem(2), near, near_sib)
    sib_3 = exchange(own_3, 1)
    own_6, own_7 = call(
        unpack_kernel, (block, block), [SMEM, *vmem(1)], place, spread, after=(own_3, other_halo)
    )
    sib_7 = exchange(own_7, 5)
    sib_6 = exchange(own_6, 4)
    own_4 = pool(own_3, sib_3, own_7)
    sib_4 = exchange(own_4, 2)
    own_8 = pool(own_7, sib_7, own_4)
    sib_8 = exchange(own_8, 6)
    own_5 = pool(own_4, sib_4, own_8)
    sib_5 = exchange(own_5, 3)
    q, num, tot = call(
        functools.partial(local_kernel, count),
        (bf16(rows, model), f32(rows, model), f32(rows, model)),
        [SMEM, *vmem(1), anywhere, *vmem(3)],
        place, tokens, w_qkv, kv, near_sib, other_halo,
        flops=10**9,
        scratch=(
            pltpu.VMEM((rows + 2 * BLOCK, 2 * model), jnp.bfloat16),
            pltpu.VMEM((rows // 2, 2 * model), jnp.bfloat16),
            pltpu.VMEM((model, model), jnp.bfloat16),
            pltpu.SemaphoreType.DMA(()),
        ),
        after=(own_5,),
    )
    own_9 = pool(own_8, sib_8, q, sib_6)
    sib_9 = exchange(own_9, 7)
    own_10 = pool(own_9, sib_9)
    num, tot = far(num, tot, near_sib, sib_3, sib_4, sib_6, after=(own_10,))
    sib_10 = exchange(own_10, 8)
    num, tot = far(num, tot, sib_5, sib_7, sib_8, sib_9, after=(own_10,))
    return call(
        final_kernel,
        bf16(rows, model),
        vmem(5),
        q, num, tot, w_out, sib_10,
        flops=10**9,
        scratch=(pltpu.VMEM((rows, model), jnp.bfloat16),),
    )


def solution(mesh):
    return jax.shard_map(
        per_device,
        mesh=mesh,
        in_specs=(P(AXES, None), P(), P()),
        out_specs=P(AXES, None),
        check_vma=False,
    )
```

```python
import functools

import jax
import jax.numpy as jnp
import numpy as np
from jax import lax
from jax.experimental import pallas as pl
from jax.experimental.pallas import tpu as pltpu
from jax.sharding import PartitionSpec as P

HEADS = 8
BLOCK = 64
AXES = ("gx", "gy")
FAR8 = (6, 7, 4, 5, 2, 3, 0, 1)
FAR4 = (3, 2, 1, 0)


def partners(bit, count):
    route = []
    for index in range(count):
        if bit == 3:
            z = index >> 1 & 7
            route.append(index & ~14 | FAR8[z] << 1)
        elif bit == 6:
            y = index >> 4 & 7
            route.append(index & ~112 | FAR8[y] << 4)
        elif bit == 8:
            x = index >> 7 & 3
            route.append(index & ~384 | FAR4[x] << 7)
        else:
            route.append(index ^ 1 << bit)
    return route


def vmem(count):
    return [pl.BlockSpec(memory_space=pltpu.VMEM)] * count


SMEM = pl.BlockSpec(memory_space=pltpu.SMEM)


def call(kernel, outs, in_specs, *args, flops=0, scratch=(), limit=24, after=()):
    count = len(args)

    def body(*refs):
        kernel(*refs[:count], *refs[count + len(after) :])

    return pl.pallas_call(
        body,
        out_shape=outs,
        in_specs=list(in_specs) + [pl.BlockSpec(memory_space=pl.ANY)] * len(after),
        out_specs=jax.tree.map(lambda _: pl.BlockSpec(memory_space=pltpu.VMEM), outs),
        scratch_shapes=list(scratch),
        compiler_params=pltpu.CompilerParams(vmem_limit_bytes=limit * 2**20),
        cost_estimate=pl.CostEstimate(flops=flops, bytes_accessed=2**20, transcendentals=0),
    )(*args, *after)


def pool_matrix(rows):
    r = lax.broadcasted_iota(jnp.int32, (rows, 2 * rows), 0)
    c = lax.broadcasted_iota(jnp.int32, (rows, 2 * rows), 1)
    return jnp.where(c >> 1 == r, 0.5, 0.0).astype(jnp.bfloat16)


def pooled(block):
    return jnp.dot(
        pool_matrix(block.shape[0] // 2), block, preferred_element_type=jnp.float32
    ).astype(jnp.bfloat16)


def project_kernel(
    place, x_hbm, w_hbm, kv_ref, near_ref, other_ref, l3_ref, packed_ref, x_buf, w_buf, part_buf, sems
):
    rows, model = x_buf.shape
    width = w_buf.shape[2]
    steps = w_buf.shape[0]
    x_copy = pltpu.make_async_copy(x_hbm, x_buf, sems.at[steps])
    x_copy.start()
    copies = []
    for step in range(steps):
        columns = pl.ds(model + step * width, width)
        copy = pltpu.make_async_copy(w_hbm.at[:, columns], w_buf.at[step], sems.at[step])
        copy.start()
        copies.append(copy)
    x_copy.wait()
    x = x_buf[...]
    pieces = []
    for step in range(steps):
        copies[step].wait()
        lanes = slice(step * width, (step + 1) * width)
        part = jnp.dot(x, w_buf[step], preferred_element_type=jnp.float32).astype(jnp.bfloat16)
        kv_ref[:, lanes] = part
        wide = part.astype(jnp.float32)
        for at in range(0, width, 128):
            tile = (step * width + at) // 128
            part_buf[tile] = wide[:, at : at + 128]
            size = rows
            while size > 8:
                size //= 2
                even = part_buf[tile, pl.ds(0, size, stride=2), :]
                odd = part_buf[tile, pl.ds(1, size, stride=2), :]
                level = ((even + odd) * 0.5).astype(jnp.bfloat16)
                if size == BLOCK:
                    near_ref[BLOCK:, tile * 128 : (tile + 1) * 128] = level
                if size == BLOCK // 2:
                    l3_ref[:, tile * 128 : (tile + 1) * 128] = level
                part_buf[tile, :size, :] = level.astype(jnp.float32)
            pieces.append(level.astype(jnp.float32))
    packed = pooled(jnp.concatenate(pieces, axis=0).astype(jnp.bfloat16))
    size = packed.shape[0]
    for copy in range(packed_ref.shape[0] // size):
        packed_ref[copy * size : (copy + 1) * size, :] = packed
    core = place[0] & 1
    last = rows - BLOCK
    low = pl.multiple_of(core * last, BLOCK)
    high = pl.multiple_of((1 - core) * last, BLOCK)
    near_ref[:BLOCK, :] = kv_ref[pl.ds(high, BLOCK), :]
    other_ref[...] = kv_ref[pl.ds(low, BLOCK), :]


def unpack_kernel(place, in_ref, own_6_ref, own_7_ref, wide):
    members, rows, _ = in_ref.shape
    half = members // 2
    wide[...] = in_ref[...].reshape(members * rows, 128).astype(jnp.float32)
    upper = (place[0] >> 4) & 1
    for tile in range(rows // 4):
        lanes = slice(tile * 128, (tile + 1) * 128)
        parts = [
            wide[pl.ds(tile * 4 + row, members, stride=rows), :] for row in range(4)
        ]
        own = [jnp.where(upper == 1, part[half:], part[:half]) for part in parts]
        own_6_ref[:, lanes] = jnp.concatenate(own, axis=0).astype(jnp.bfloat16)
        pairs = [(parts[0] + parts[1]) * 0.5, (parts[2] + parts[3]) * 0.5]
        own_7_ref[:, lanes] = jnp.concatenate(pairs, axis=0).astype(jnp.bfloat16)


def pool_near_kernel(mine_ref, sib_ref, out_ref):
    out_ref[: BLOCK // 2, :] = mine_ref[...]
    out_ref[BLOCK // 2 :, :] = pooled(sib_ref[BLOCK:, :])


def pool_halves_kernel(own_ref, sib_ref, out_ref):
    half = BLOCK // 2
    for num, ref in enumerate((own_ref, sib_ref)):
        block = ref[...].astype(jnp.float32)
        out_ref[num * half : (num + 1) * half, :] = (
            (block[:half] + block[half:]) * 0.5
        ).astype(jnp.bfloat16)


def pool_kernel(*refs):
    ins, out_ref = refs[:-1], refs[-1]
    half = BLOCK // len(ins)
    for num, ref in enumerate(ins):
        out_ref[num * half : (num + 1) * half, :] = pooled(ref[...])


def attend_pair(q, keys, values, ones):
    rows = q.shape[0]
    lane = lax.broadcasted_iota(jnp.int32, q.shape, 1)
    first = lane < 64
    zero = jnp.zeros_like(q)
    both = jnp.concatenate([jnp.where(first, q, zero), jnp.where(first, zero, q)], axis=0)
    scores = lax.dot_general(
        both, keys, (((1,), (1,)), ((), ())), preferred_element_type=jnp.float32
    )
    weights = jnp.exp(scores).astype(jnp.bfloat16)
    sums = jnp.dot(
        weights, jnp.concatenate([values, ones], axis=1), preferred_element_type=jnp.float32
    )
    num = jnp.where(first, sums[:rows, :128], sums[rows:, :128])
    tot = jnp.where(first, sums[:rows, 128:], sums[rows:, 128:])
    return num, tot


def local_kernel(
    count, place, x_ref, w_hbm, kv_ref, near_ref, other_ref, q_ref, num_ref, tot_ref, pad, l1, w_ref, sem
):
    rows, model = x_ref.shape
    blocks = rows // BLOCK
    copy = pltpu.make_async_copy(w_hbm.at[:, pl.ds(0, model)], w_ref, sem)
    copy.start()
    core = place[0] & 1
    sib_halo = near_ref[:BLOCK, :]
    other = other_ref[...]
    is_first = core == 0
    pad[:BLOCK, :] = jnp.where(is_first, other, sib_halo)
    pad[BLOCK : BLOCK + rows, :] = kv_ref[...]
    pad[BLOCK + rows :, :] = jnp.where(is_first, sib_halo, other)
    l1[...] = pooled(kv_ref[...])
    copy.wait()
    q_ref[...] = (
        jnp.dot(x_ref[...], w_ref[...], preferred_element_type=jnp.float32)
        .astype(jnp.bfloat16) * jnp.bfloat16(0.125)
    )
    key_row = lax.broadcasted_iota(jnp.int32, (4 * BLOCK, 128), 0)
    for i in range(blocks):
        ones = jnp.ones((4 * BLOCK, 128), jnp.float32)
        if i == 0:
            ones = jnp.where((key_row < BLOCK) & (place[0] == 0), 0.0, ones)
        if i == blocks - 1:
            ones = jnp.where((key_row >= 2 * BLOCK) & (key_row < 3 * BLOCK) & (place[0] == count - 1), 0.0, ones)
        ones = ones.astype(jnp.bfloat16)
        sib = (i >> 1) ^ 1
        here = slice(i * BLOCK, (i + 1) * BLOCK)
        for lanes in range(0, model, 128):
            kl = slice(lanes, lanes + 128)
            vl = slice(model + lanes, model + lanes + 128)
            keys = jnp.concatenate(
                [pad[i * BLOCK : (i + 3) * BLOCK, kl], l1[sib * BLOCK : (sib + 1) * BLOCK, kl]], axis=0
            )
            values = jnp.concatenate(
                [pad[i * BLOCK : (i + 3) * BLOCK, vl], l1[sib * BLOCK : (sib + 1) * BLOCK, vl]], axis=0
            )
            num, tot = attend_pair(q_ref[here, kl], keys, values, ones)
            num_ref[here, kl] = num
            tot_ref[here, kl] = tot


def far_blocks(refs):
    return jnp.concatenate(
        [ref[BLOCK:, :] if ref.shape[0] == 2 * BLOCK else ref[...] for ref in refs], axis=0
    )


def far_sums(far, q, lanes, model):
    keys = far[:, lanes : lanes + 128]
    values = far[:, model + lanes : model + lanes + 128]
    return attend_pair(q, keys, values, jnp.ones(values.shape, jnp.bfloat16))


def far_kernel(q_ref, num_in, tot_in, *refs):
    num_ref, tot_ref = refs[-2:]
    model = q_ref.shape[1]
    far = far_blocks(refs[:-2])
    for lanes in range(0, model, 128):
        at = slice(lanes, lanes + 128)
        num, tot = far_sums(far, q_ref[:, at], lanes, model)
        num_ref[:, at] = num_in[:, at] + num
        tot_ref[:, at] = tot_in[:, at] + tot


def final_kernel(q_ref, num_in, tot_in, w_ref, *refs):
    out_ref, att = refs[-2:]
    model = q_ref.shape[1]
    far = far_blocks(refs[:-2])
    for lanes in range(0, model, 128):
        at = slice(lanes, lanes + 128)
        num, tot = far_sums(far, q_ref[:, at], lanes, model)
        att[:, at] = ((num_in[:, at] + num) / (tot_in[:, at] + tot)).astype(jnp.bfloat16)
    out_ref[...] = jnp.dot(att[...], w_ref[...], preferred_element_type=jnp.float32).astype(
        jnp.bfloat16
    )


def per_device(tokens, w_qkv, w_out):
    rows, model = tokens.shape
    index = lax.axis_index(AXES)
    count = lax.axis_size(AXES)
    place = index.astype(jnp.int32).reshape(1)
    bf16 = lambda *shape: jax.ShapeDtypeStruct(shape, jnp.bfloat16)
    f32 = lambda *shape: jax.ShapeDtypeStruct(shape, jnp.float32)
    anywhere = pl.BlockSpec(memory_space=pl.ANY)
    steps = 2
    width = 2 * model // steps
    members = 32
    packed = 4 * 2 * model // 128
    block = bf16(BLOCK, 2 * model)
    kv, near, other, level_3, level_6 = call(
        project_kernel,
        (
            bf16(rows, 2 * model), bf16(2 * BLOCK, 2 * model), block,
            bf16(BLOCK // 2, 2 * model), bf16(members * packed, 128),
        ),
        [SMEM, anywhere, anywhere],
        place, tokens, w_qkv,
        flops=4 * rows * model * model,
        scratch=(
            pltpu.VMEM((rows, model), jnp.bfloat16),
            pltpu.VMEM((steps, model, width), jnp.bfloat16),
            pltpu.VMEM((2 * model // 128, rows, 128), jnp.float32),
            pltpu.SemaphoreType.DMA((steps + 1,)),
        ),
        limit=56,
    )
    swap = [(i, i + 1) for i in range(1, count - 1, 2)]
    swap += [(j, i) for i, j in swap]
    def exchange(own, bit):
        return lax.ppermute(own, AXES, list(enumerate(partners(bit, count))))

    def pool(own, got, *after):
        return call(pool_kernel, block, vmem(2), own, got, after=after)

    def far(num, tot, *part, after=()):
        return call(
            far_kernel,
            (f32(rows, model), f32(rows, model)),
            vmem(3 + len(part)),
            q, num, tot, *part,
            flops=10**9,
            after=after,
        )

    teams = [list(range(i, i + members)) for i in range(0, count, members)]
    spread = lax.all_to_all(level_6, AXES, 0, 0, axis_index_groups=teams, tiled=True)
    near_sib = exchange(near, 0)
    other_halo = lax.ppermute(other, AXES, swap)

    own_3 = call(pool_near_kernel, block, vmem(2), level_3, near_sib)
    sib_3 = exchange(own_3, 1)
    own_6, own_7 = call(
        unpack_kernel, (block, block), [SMEM, *vmem(1)],
        place, spread.reshape(members, packed, 128),
        scratch=(pltpu.VMEM((members * packed, 128), jnp.float32),),
        after=(own_3, other_halo),
    )
    sib_7 = exchange(own_7, 5)
    own_4 = pool(own_3, sib_3, own_7)
    sib_4 = exchange(own_4, 2)
    own_8 = call(pool_halves_kernel, block, vmem(2), own_7, sib_7, after=(own_4,))
    sib_8 = exchange(own_8, 6)
    own_6, _ = lax.optimization_barrier((own_6, own_8))
    sib_6 = exchange(own_6, 4)
    own_5 = pool(own_4, sib_4, own_8)
    sib_5 = exchange(own_5, 3)
    own_9 = pool(own_8, sib_8, own_5)
    sib_9 = exchange(own_9, 7)
    own_10 = pool(own_9, sib_9, sib_6)
    q, num, tot = call(
        functools.partial(local_kernel, count),
        (bf16(rows, model), f32(rows, model), f32(rows, model)),
        [SMEM, *vmem(1), anywhere, *vmem(3)],
        place, tokens, w_qkv, kv, near_sib, other_halo,
        flops=10**9,
        scratch=(
            pltpu.VMEM((rows + 2 * BLOCK, 2 * model), jnp.bfloat16),
            pltpu.VMEM((rows // 2, 2 * model), jnp.bfloat16),
            pltpu.VMEM((model, model), jnp.bfloat16),
            pltpu.SemaphoreType.DMA(()),
        ),
        after=(own_10,),
    )
    num, tot = far(num, tot, near_sib, sib_3, sib_4, sib_6, after=(own_10,))
    sib_10 = exchange(own_10, 8)
    num, tot = far(num, tot, sib_5, sib_7, sib_8, sib_9, after=(own_10,))
    return call(
        final_kernel,
        bf16(rows, model),
        vmem(5),
        q, num, tot, w_out, sib_10,
        flops=10**9,
        scratch=(pltpu.VMEM((rows, model), jnp.bfloat16),),
    )


def solution(mesh):
    return jax.shard_map(
        per_device,
        mesh=mesh,
        in_specs=(P(AXES, None), P(), P()),
        out_specs=P(AXES, None),
        check_vma=False,
    )
```

```python
import functools

import jax
import jax.numpy as jnp
import numpy as np
from jax import lax
from jax.experimental import pallas as pl
from jax.experimental.pallas import tpu as pltpu
from jax.sharding import PartitionSpec as P

HEADS = 8
BLOCK = 64
AXES = ("gx", "gy")
FAR8 = (6, 7, 4, 5, 2, 3, 0, 1)


def partners(bit, count):
    route = []
    for index in range(count):
        if bit == 3:
            route.append(index & ~14 | FAR8[index >> 1 & 7] << 1)
        else:
            route.append(index ^ 1 << bit)
    return route


def vmem(count):
    return [pl.BlockSpec(memory_space=pltpu.VMEM)] * count


SMEM = pl.BlockSpec(memory_space=pltpu.SMEM)


def call(kernel, outs, in_specs, *args, flops=0, scratch=(), limit=24, after=()):
    count = len(args)

    def body(*refs):
        kernel(*refs[:count], *refs[count + len(after) :])

    return pl.pallas_call(
        body,
        out_shape=outs,
        in_specs=list(in_specs) + [pl.BlockSpec(memory_space=pl.ANY)] * len(after),
        out_specs=jax.tree.map(lambda _: pl.BlockSpec(memory_space=pltpu.VMEM), outs),
        scratch_shapes=list(scratch),
        compiler_params=pltpu.CompilerParams(vmem_limit_bytes=limit * 2**20),
        cost_estimate=pl.CostEstimate(flops=flops, bytes_accessed=2**20, transcendentals=0),
    )(*args, *after)


def pool_matrix(rows):
    r = lax.broadcasted_iota(jnp.int32, (rows, 2 * rows), 0)
    c = lax.broadcasted_iota(jnp.int32, (rows, 2 * rows), 1)
    return jnp.where(c >> 1 == r, 0.5, 0.0).astype(jnp.bfloat16)


def pooled(block):
    return jnp.dot(
        pool_matrix(block.shape[0] // 2), block, preferred_element_type=jnp.float32
    ).astype(jnp.bfloat16)


def project_kernel(
    place, x_hbm, w_hbm, kv_ref, near_ref, other_ref, l3_ref, packed_ref, x_buf, w_buf, part_buf, sems
):
    rows, model = x_buf.shape
    width = w_buf.shape[2]
    steps = w_buf.shape[0]
    x_copy = pltpu.make_async_copy(x_hbm, x_buf, sems.at[steps])
    x_copy.start()
    copies = []
    for step in range(steps):
        columns = pl.ds(model + step * width, width)
        copy = pltpu.make_async_copy(w_hbm.at[:, columns], w_buf.at[step], sems.at[step])
        copy.start()
        copies.append(copy)
    x_copy.wait()
    x = x_buf[...]
    pieces = []
    for step in range(steps):
        copies[step].wait()
        lanes = slice(step * width, (step + 1) * width)
        part = jnp.dot(x, w_buf[step], preferred_element_type=jnp.float32).astype(jnp.bfloat16)
        kv_ref[:, lanes] = part
        wide = part.astype(jnp.float32)
        for at in range(0, width, 128):
            tile = (step * width + at) // 128
            part_buf[tile] = wide[:, at : at + 128]
            size = rows
            while size > 8:
                size //= 2
                even = part_buf[tile, pl.ds(0, size, stride=2), :]
                odd = part_buf[tile, pl.ds(1, size, stride=2), :]
                level = ((even + odd) * 0.5).astype(jnp.bfloat16)
                if size == BLOCK:
                    near_ref[BLOCK:, tile * 128 : (tile + 1) * 128] = level
                if size == BLOCK // 2:
                    l3_ref[:, tile * 128 : (tile + 1) * 128] = level
                part_buf[tile, :size, :] = level.astype(jnp.float32)
            pieces.append(level.astype(jnp.float32))
    packed = pooled(jnp.concatenate(pieces, axis=0).astype(jnp.bfloat16))
    size = packed.shape[0]
    for copy in range(packed_ref.shape[0] // size):
        packed_ref[copy * size : (copy + 1) * size, :] = packed
    core = place[0] & 1
    last = rows - BLOCK
    low = pl.multiple_of(core * last, BLOCK)
    high = pl.multiple_of((1 - core) * last, BLOCK)
    near_ref[:BLOCK, :] = kv_ref[pl.ds(high, BLOCK), :]
    other_ref[...] = kv_ref[pl.ds(low, BLOCK), :]


def unpack_kernel(place, in_ref, out_ref, wide):
    members, rows, _ = in_ref.shape
    wide[...] = in_ref[...].reshape(members * rows, 128).astype(jnp.float32)
    y = (place[0] >> 4) & 7

    def mean(one, two):
        return ((one + two) * 0.5).astype(jnp.bfloat16).astype(jnp.float32)

    for tile in range(rows // 4):
        lanes = slice(tile * 128, (tile + 1) * 128)

        def level_6(start, count):
            return [
                wide[pl.ds(start * rows + tile * 4 + row, count, stride=rows), :]
                for row in range(4)
            ]

        def level_7(start, count):
            r = level_6(start, count)
            return [mean(r[0], r[1]), mean(r[2], r[3])]

        parts = (
            level_6((y ^ 1) * 8, 8)
            + level_7(((y >> 1) ^ 1) * 16, 16)
            + [mean(*level_7(((y >> 2) ^ 1) * 32, 32))]
            + [mean(*level_7(0, members))]
        )
        out_ref[:, lanes] = jnp.concatenate(parts, axis=0).astype(jnp.bfloat16)


def own_9_kernel(mine_ref, sib_ref, out_ref):
    at = 3 * BLOCK // 2
    both = mine_ref[at:, :].astype(jnp.float32) + sib_ref[at:, :].astype(jnp.float32)
    block = (both * 0.5).astype(jnp.bfloat16)
    for copy in range(out_ref.shape[0] // BLOCK):
        out_ref[copy * BLOCK : (copy + 1) * BLOCK, :] = block


def pool_near_kernel(mine_ref, sib_ref, out_ref):
    out_ref[: BLOCK // 2, :] = mine_ref[...]
    out_ref[BLOCK // 2 :, :] = pooled(sib_ref[BLOCK:, :])


def pool_kernel(*refs):
    ins, out_ref = refs[:-1], refs[-1]
    half = BLOCK // len(ins)
    for num, ref in enumerate(ins):
        out_ref[num * half : (num + 1) * half, :] = pooled(ref[...])


def attend_pair(q, keys, values, ones):
    rows = q.shape[0]
    lane = lax.broadcasted_iota(jnp.int32, q.shape, 1)
    first = lane < 64
    zero = jnp.zeros_like(q)
    both = jnp.concatenate([jnp.where(first, q, zero), jnp.where(first, zero, q)], axis=0)
    scores = lax.dot_general(
        both, keys, (((1,), (1,)), ((), ())), preferred_element_type=jnp.float32
    )
    weights = jnp.exp(scores).astype(jnp.bfloat16)
    sums = jnp.dot(
        weights, jnp.concatenate([values, ones], axis=1), preferred_element_type=jnp.float32
    )
    num = jnp.where(first, sums[:rows, :128], sums[rows:, :128])
    tot = jnp.where(first, sums[:rows, 128:], sums[rows:, 128:])
    return num, tot


def local_kernel(
    count, place, x_ref, w_hbm, kv_ref, near_ref, other_ref, q_ref, num_ref, tot_ref, pad, l1, w_ref, sem
):
    rows, model = x_ref.shape
    blocks = rows // BLOCK
    copy = pltpu.make_async_copy(w_hbm.at[:, pl.ds(0, model)], w_ref, sem)
    copy.start()
    core = place[0] & 1
    sib_halo = near_ref[:BLOCK, :]
    other = other_ref[...]
    is_first = core == 0
    pad[:BLOCK, :] = jnp.where(is_first, other, sib_halo)
    pad[BLOCK : BLOCK + rows, :] = kv_ref[...]
    pad[BLOCK + rows :, :] = jnp.where(is_first, sib_halo, other)
    l1[...] = pooled(kv_ref[...])
    copy.wait()
    q_ref[...] = (
        jnp.dot(x_ref[...], w_ref[...], preferred_element_type=jnp.float32)
        .astype(jnp.bfloat16) * jnp.bfloat16(0.125)
    )
    key_row = lax.broadcasted_iota(jnp.int32, (4 * BLOCK, 128), 0)
    for i in range(blocks):
        ones = jnp.ones((4 * BLOCK, 128), jnp.float32)
        if i == 0:
            ones = jnp.where((key_row < BLOCK) & (place[0] == 0), 0.0, ones)
        if i == blocks - 1:
            ones = jnp.where((key_row >= 2 * BLOCK) & (key_row < 3 * BLOCK) & (place[0] == count - 1), 0.0, ones)
        ones = ones.astype(jnp.bfloat16)
        sib = (i >> 1) ^ 1
        here = slice(i * BLOCK, (i + 1) * BLOCK)
        for lanes in range(0, model, 128):
            kl = slice(lanes, lanes + 128)
            vl = slice(model + lanes, model + lanes + 128)
            keys = jnp.concatenate(
                [pad[i * BLOCK : (i + 3) * BLOCK, kl], l1[sib * BLOCK : (sib + 1) * BLOCK, kl]], axis=0
            )
            values = jnp.concatenate(
                [pad[i * BLOCK : (i + 3) * BLOCK, vl], l1[sib * BLOCK : (sib + 1) * BLOCK, vl]], axis=0
            )
            num, tot = attend_pair(q_ref[here, kl], keys, values, ones)
            num_ref[here, kl] = num
            tot_ref[here, kl] = tot


def far_blocks(refs):
    blocks = []
    for ref in refs:
        if ref.shape[0] == 2 * BLOCK:
            blocks.append(ref[BLOCK:, :])
        elif ref.shape[0] > 2 * BLOCK:
            blocks.append(ref[: 3 * BLOCK // 2, :])
        else:
            blocks.append(ref[...])
    return jnp.concatenate(blocks, axis=0)


def far_sums(far, q, lanes, model):
    keys = far[:, lanes : lanes + 128]
    values = far[:, model + lanes : model + lanes + 128]
    return attend_pair(q, keys, values, jnp.ones(values.shape, jnp.bfloat16))


def far_kernel(q_ref, num_in, tot_in, *refs):
    num_ref, tot_ref = refs[-2:]
    model = q_ref.shape[1]
    far = far_blocks(refs[:-2])
    for lanes in range(0, model, 128):
        at = slice(lanes, lanes + 128)
        num, tot = far_sums(far, q_ref[:, at], lanes, model)
        num_ref[:, at] = num_in[:, at] + num
        tot_ref[:, at] = tot_in[:, at] + tot


def final_kernel(place, q_ref, num_in, tot_in, w_ref, sib_5_ref, wide_ref, out_ref, att):
    model = q_ref.shape[1]
    x = place[0] >> 7
    near = pl.multiple_of((x ^ 1) * BLOCK, BLOCK)
    other = pl.multiple_of(((x >> 1) ^ 1) * 2 * BLOCK, BLOCK)
    far = jnp.concatenate(
        [
            sib_5_ref[...],
            wide_ref[pl.ds(near, BLOCK), :],
            pooled(wide_ref[pl.ds(other, 2 * BLOCK), :]),
        ],
        axis=0,
    )
    for lanes in range(0, model, 128):
        at = slice(lanes, lanes + 128)
        num, tot = far_sums(far, q_ref[:, at], lanes, model)
        att[:, at] = ((num_in[:, at] + num) / (tot_in[:, at] + tot)).astype(jnp.bfloat16)
    out_ref[...] = jnp.dot(att[...], w_ref[...], preferred_element_type=jnp.float32).astype(
        jnp.bfloat16
    )


def per_device(tokens, w_qkv, w_out):
    rows, model = tokens.shape
    index = lax.axis_index(AXES)
    count = lax.axis_size(AXES)
    place = index.astype(jnp.int32).reshape(1)
    bf16 = lambda *shape: jax.ShapeDtypeStruct(shape, jnp.bfloat16)
    f32 = lambda *shape: jax.ShapeDtypeStruct(shape, jnp.float32)
    anywhere = pl.BlockSpec(memory_space=pl.ANY)
    steps = 2
    width = 2 * model // steps
    members = 64
    packed = 4 * 2 * model // 128
    block = bf16(BLOCK, 2 * model)
    kv, near, other, level_3, level_6 = call(
        project_kernel,
        (
            bf16(rows, 2 * model), bf16(2 * BLOCK, 2 * model), block,
            bf16(BLOCK // 2, 2 * model), bf16(members * packed, 128),
        ),
        [SMEM, anywhere, anywhere],
        place, tokens, w_qkv,
        flops=4 * rows * model * model,
        scratch=(
            pltpu.VMEM((rows, model), jnp.bfloat16),
            pltpu.VMEM((steps, model, width), jnp.bfloat16),
            pltpu.VMEM((2 * model // 128, rows, 128), jnp.float32),
            pltpu.SemaphoreType.DMA((steps + 1,)),
        ),
        limit=56,
    )
    swap = [(i, i + 1) for i in range(1, count - 1, 2)]
    swap += [(j, i) for i, j in swap]
    def exchange(own, bit):
        return lax.ppermute(own, AXES, list(enumerate(partners(bit, count))))

    def pool(own, got, *after):
        return call(pool_kernel, block, vmem(2), own, got, after=after)

    def far(num, tot, *part, after=()):
        return call(
            far_kernel,
            (f32(rows, model), f32(rows, model)),
            vmem(3 + len(part)),
            q, num, tot, *part,
            flops=10**9,
            after=after,
        )

    teams = [
        [i for i in range(count) if i >> 7 == x and i & 1 == core]
        for x in range(count >> 7)
        for core in range(2)
    ]
    spread = lax.all_to_all(level_6, AXES, 0, 0, axis_index_groups=teams, tiled=True)
    near_sib = exchange(near, 0)
    own_3 = call(pool_near_kernel, block, vmem(2), level_3, near_sib)
    sib_3 = exchange(own_3, 1)
    other_halo = lax.ppermute(other, AXES, swap)
    own_4 = pool(own_3, sib_3, other_halo)
    sib_4 = exchange(own_4, 2)
    mine = call(
        unpack_kernel, bf16(5 * BLOCK // 2, 2 * model), [SMEM, *vmem(1)],
        place, spread.reshape(members, packed, 128),
        scratch=(pltpu.VMEM((members * packed, 128), jnp.float32),),
        after=(own_4,),
    )
    theirs = exchange(mine, 0)
    own_9 = call(own_9_kernel, bf16(4 * BLOCK, 2 * model), vmem(2), mine, theirs)
    own_5 = pool(own_4, sib_4, own_9)
    columns = [list(range(i, count, count >> 2)) for i in range(count >> 2)]
    wide = lax.all_to_all(own_9, AXES, 0, 0, axis_index_groups=columns, tiled=True)
    sib_5 = exchange(own_5, 3)
    q, num, tot = call(
        functools.partial(local_kernel, count),
        (bf16(rows, model), f32(rows, model), f32(rows, model)),
        [SMEM, *vmem(1), anywhere, *vmem(3)],
        place, tokens, w_qkv, kv, near_sib, other_halo,
        flops=10**9,
        scratch=(
            pltpu.VMEM((rows + 2 * BLOCK, 2 * model), jnp.bfloat16),
            pltpu.VMEM((rows // 2, 2 * model), jnp.bfloat16),
            pltpu.VMEM((model, model), jnp.bfloat16),
            pltpu.SemaphoreType.DMA(()),
        ),
        limit=48,
        after=(own_9,),
    )
    num, tot = far(num, tot, mine, theirs)
    num, tot = far(num, tot, near_sib, sib_3, sib_4)
    return call(
        final_kernel,
        bf16(rows, model),
        [SMEM, *vmem(6)],
        place, q, num, tot, w_out, sib_5, wide,
        flops=10**9,
        scratch=(pltpu.VMEM((rows, model), jnp.bfloat16),),
    )


def solution(mesh):
    return jax.shard_map(
        per_device,
        mesh=mesh,
        in_specs=(P(AXES, None), P(), P()),
        out_specs=P(AXES, None),
        check_vma=False,
    )
```

```python
import functools

import jax
import jax.numpy as jnp
import numpy as np
from jax import lax
from jax.experimental import pallas as pl
from jax.experimental.pallas import tpu as pltpu
from jax.sharding import PartitionSpec as P

HEADS = 8
BLOCK = 64
AXES = ("gx", "gy")
FAR8 = (6, 7, 4, 5, 2, 3, 0, 1)
FAR4 = (3, 2, 1, 0)


def partners(bit, count):
    route = []
    for index in range(count):
        if bit == 3:
            route.append(index & ~14 | FAR8[index >> 1 & 7] << 1)
        elif bit == 8:
            route.append(index & ~384 | FAR4[index >> 7 & 3] << 7)
        else:
            route.append(index ^ 1 << bit)
    return route


def vmem(count):
    return [pl.BlockSpec(memory_space=pltpu.VMEM)] * count


SMEM = pl.BlockSpec(memory_space=pltpu.SMEM)


def call(kernel, outs, in_specs, *args, flops=0, scratch=(), limit=10, after=()):
    count = len(args)

    def body(*refs):
        kernel(*refs[:count], *refs[count + len(after) :])

    return pl.pallas_call(
        body,
        out_shape=outs,
        in_specs=list(in_specs) + [pl.BlockSpec(memory_space=pl.ANY)] * len(after),
        out_specs=jax.tree.map(lambda _: pl.BlockSpec(memory_space=pltpu.VMEM), outs),
        scratch_shapes=list(scratch),
        compiler_params=pltpu.CompilerParams(vmem_limit_bytes=limit * 2**20),
        cost_estimate=pl.CostEstimate(flops=flops, bytes_accessed=2**20, transcendentals=0),
    )(*args, *after)


def pool_matrix(rows):
    r = lax.broadcasted_iota(jnp.int32, (rows, 2 * rows), 0)
    c = lax.broadcasted_iota(jnp.int32, (rows, 2 * rows), 1)
    return jnp.where(c >> 1 == r, 0.5, 0.0).astype(jnp.bfloat16)


def pooled(block):
    return jnp.dot(
        pool_matrix(block.shape[0] // 2), block, preferred_element_type=jnp.float32
    ).astype(jnp.bfloat16)


def project_kernel(
    place, x_hbm, w_hbm, kv_ref, near_ref, other_ref, l3_ref, packed_ref, x_buf, w_buf, part_buf, sems
):
    rows, model = x_buf.shape
    width = w_buf.shape[2]
    steps = w_buf.shape[0]
    x_copy = pltpu.make_async_copy(x_hbm, x_buf, sems.at[steps])
    x_copy.start()
    copies = []
    for step in range(steps):
        columns = pl.ds(model + step * width, width)
        copy = pltpu.make_async_copy(w_hbm.at[:, columns], w_buf.at[step], sems.at[step])
        copy.start()
        copies.append(copy)
    x_copy.wait()
    x = x_buf[...]
    pieces = []
    for step in range(steps):
        copies[step].wait()
        lanes = slice(step * width, (step + 1) * width)
        part = jnp.dot(x, w_buf[step], preferred_element_type=jnp.float32).astype(jnp.bfloat16)
        kv_ref[:, lanes] = part
        wide = part.astype(jnp.float32)
        for at in range(0, width, 128):
            tile = (step * width + at) // 128
            part_buf[tile] = wide[:, at : at + 128]
            size = rows
            while size > 8:
                size //= 2
                even = part_buf[tile, pl.ds(0, size, stride=2), :]
                odd = part_buf[tile, pl.ds(1, size, stride=2), :]
                level = ((even + odd) * 0.5).astype(jnp.bfloat16)
                if size == BLOCK:
                    near_ref[BLOCK:, tile * 128 : (tile + 1) * 128] = level
                if size == BLOCK // 2:
                    l3_ref[:, tile * 128 : (tile + 1) * 128] = level
                part_buf[tile, :size, :] = level.astype(jnp.float32)
            pieces.append(level.astype(jnp.float32))
    packed = pooled(jnp.concatenate(pieces, axis=0).astype(jnp.bfloat16))
    size = packed.shape[0]
    for copy in range(packed_ref.shape[0] // size):
        packed_ref[copy * size : (copy + 1) * size, :] = packed
    core = place[0] & 1
    last = rows - BLOCK
    low = pl.multiple_of(core * last, BLOCK)
    high = pl.multiple_of((1 - core) * last, BLOCK)
    near_ref[:BLOCK, :] = kv_ref[pl.ds(high, BLOCK), :]
    other_ref[...] = kv_ref[pl.ds(low, BLOCK), :]


def unpack_kernel(place, in_ref, out_ref, wide):
    members, rows, _ = in_ref.shape
    wide[...] = in_ref[...].reshape(members * rows, 128).astype(jnp.float32)
    y = (place[0] >> 4) & 7

    def mean(one, two):
        return ((one + two) * 0.5).astype(jnp.bfloat16).astype(jnp.float32)

    for tile in range(rows // 4):
        lanes = slice(tile * 128, (tile + 1) * 128)

        def level_6(start, count):
            return [
                wide[pl.ds(start * rows + tile * 4 + row, count, stride=rows), :]
                for row in range(4)
            ]

        def level_7(start, count):
            r = level_6(start, count)
            return [mean(r[0], r[1]), mean(r[2], r[3])]

        parts = (
            level_6((y ^ 1) * 8, 8)
            + level_7(((y >> 1) ^ 1) * 16, 16)
            + [mean(*level_7(((y >> 2) ^ 1) * 32, 32))]
            + [mean(*level_7(0, members))]
        )
        out_ref[:, lanes] = jnp.concatenate(parts, axis=0).astype(jnp.bfloat16)


def own_9_kernel(mine_ref, sib_ref, out_ref):
    at = 3 * BLOCK // 2
    both = mine_ref[at:, :].astype(jnp.float32) + sib_ref[at:, :].astype(jnp.float32)
    out_ref[...] = (both * 0.5).astype(jnp.bfloat16)


def pool_near_kernel(mine_ref, sib_ref, out_ref):
    out_ref[: BLOCK // 2, :] = mine_ref[...]
    out_ref[BLOCK // 2 :, :] = pooled(sib_ref[BLOCK:, :])


def pool_kernel(*refs):
    ins, out_ref = refs[:-1], refs[-1]
    half = BLOCK // len(ins)
    for num, ref in enumerate(ins):
        out_ref[num * half : (num + 1) * half, :] = pooled(ref[...])


def attend_pair(q, keys, values, ones):
    rows = q.shape[0]
    lane = lax.broadcasted_iota(jnp.int32, q.shape, 1)
    first = lane < 64
    zero = jnp.zeros_like(q)
    both = jnp.concatenate([jnp.where(first, q, zero), jnp.where(first, zero, q)], axis=0)
    scores = lax.dot_general(
        both, keys, (((1,), (1,)), ((), ())), preferred_element_type=jnp.float32
    )
    weights = jnp.exp(scores).astype(jnp.bfloat16)
    sums = jnp.dot(
        weights, jnp.concatenate([values, ones], axis=1), preferred_element_type=jnp.float32
    )
    num = jnp.where(first, sums[:rows, :128], sums[rows:, :128])
    tot = jnp.where(first, sums[:rows, 128:], sums[rows:, 128:])
    return num, tot


def local_kernel(
    count, place, x_ref, w_hbm, kv_ref, near_ref, other_ref, mine_ref, theirs_ref, sib_3_ref,
    sib_4_ref, q_ref, num_ref, tot_ref, pad, l1, w_ref, sem
):
    rows, model = x_ref.shape
    blocks = rows // BLOCK
    copy = pltpu.make_async_copy(w_hbm.at[:, pl.ds(0, model)], w_ref, sem)
    copy.start()
    core = place[0] & 1
    sib_halo = near_ref[:BLOCK, :]
    other = other_ref[...]
    is_first = core == 0
    pad[:BLOCK, :] = jnp.where(is_first, other, sib_halo)
    pad[BLOCK : BLOCK + rows, :] = kv_ref[...]
    pad[BLOCK + rows :, :] = jnp.where(is_first, sib_halo, other)
    l1[...] = pooled(kv_ref[...])
    copy.wait()
    q_ref[...] = (
        jnp.dot(x_ref[...], w_ref[...], preferred_element_type=jnp.float32)
        .astype(jnp.bfloat16) * jnp.bfloat16(0.125)
    )
    key_row = lax.broadcasted_iota(jnp.int32, (4 * BLOCK, 128), 0)
    for i in range(blocks):
        ones = jnp.ones((4 * BLOCK, 128), jnp.float32)
        if i == 0:
            ones = jnp.where((key_row < BLOCK) & (place[0] == 0), 0.0, ones)
        if i == blocks - 1:
            ones = jnp.where((key_row >= 2 * BLOCK) & (key_row < 3 * BLOCK) & (place[0] == count - 1), 0.0, ones)
        ones = ones.astype(jnp.bfloat16)
        sib = (i >> 1) ^ 1
        here = slice(i * BLOCK, (i + 1) * BLOCK)
        for lanes in range(0, model, 128):
            kl = slice(lanes, lanes + 128)
            vl = slice(model + lanes, model + lanes + 128)
            keys = jnp.concatenate(
                [pad[i * BLOCK : (i + 3) * BLOCK, kl], l1[sib * BLOCK : (sib + 1) * BLOCK, kl]], axis=0
            )
            values = jnp.concatenate(
                [pad[i * BLOCK : (i + 3) * BLOCK, vl], l1[sib * BLOCK : (sib + 1) * BLOCK, vl]], axis=0
            )
            num, tot = attend_pair(q_ref[here, kl], keys, values, ones)
            num_ref[here, kl] = num
            tot_ref[here, kl] = tot
    for refs in ((mine_ref, theirs_ref), (near_ref, sib_3_ref, sib_4_ref)):
        far = far_blocks(refs)
        for lanes in range(0, model, 128):
            kl = slice(lanes, lanes + 128)
            num, tot = far_sums(far, q_ref[:, kl], lanes, model)
            num_ref[:, kl] += num
            tot_ref[:, kl] += tot


def far_blocks(refs):
    blocks = []
    for ref in refs:
        if ref.shape[0] == 2 * BLOCK:
            blocks.append(ref[BLOCK:, :])
        elif ref.shape[0] > 2 * BLOCK:
            blocks.append(ref[: 3 * BLOCK // 2, :])
        else:
            blocks.append(ref[...])
    return jnp.concatenate(blocks, axis=0)


def far_sums(far, q, lanes, model):
    keys = far[:, lanes : lanes + 128]
    values = far[:, model + lanes : model + lanes + 128]
    return attend_pair(q, keys, values, jnp.ones(values.shape, jnp.bfloat16))


def final_kernel(
    q_ref, num_in, tot_in, sib_5_ref, sib_9_ref, sib_10_ref, w_hbm, out_ref, att, w_ref, sem
):
    copy = pltpu.make_async_copy(w_hbm, w_ref, sem)
    copy.start()
    model = q_ref.shape[1]
    far = far_blocks((sib_5_ref, sib_9_ref, sib_10_ref))
    for lanes in range(0, model, 128):
        at = slice(lanes, lanes + 128)
        num, tot = far_sums(far, q_ref[:, at], lanes, model)
        att[:, at] = ((num_in[:, at] + num) / (tot_in[:, at] + tot)).astype(jnp.bfloat16)
    copy.wait()
    out_ref[...] = jnp.dot(att[...], w_ref[...], preferred_element_type=jnp.float32).astype(
        jnp.bfloat16
    )


def per_device(tokens, w_qkv, w_out):
    rows, model = tokens.shape
    index = lax.axis_index(AXES)
    count = lax.axis_size(AXES)
    place = index.astype(jnp.int32).reshape(1)
    bf16 = lambda *shape: jax.ShapeDtypeStruct(shape, jnp.bfloat16)
    f32 = lambda *shape: jax.ShapeDtypeStruct(shape, jnp.float32)
    in_hbm = pl.BlockSpec(memory_space=pl.ANY)
    stay = lambda array: pltpu.with_memory_space_constraint(array, pltpu.HBM)
    steps = 2
    width = 2 * model // steps
    members = 64
    packed = 4 * 2 * model // 128
    block = bf16(BLOCK, 2 * model)
    kv, near, other, level_3, level_6 = call(
        project_kernel,
        (
            bf16(rows, 2 * model), bf16(2 * BLOCK, 2 * model), block,
            bf16(BLOCK // 2, 2 * model), bf16(members * packed, 128),
        ),
        [SMEM, in_hbm, in_hbm],
        place, stay(tokens), stay(w_qkv),
        flops=4 * rows * model * model,
        scratch=(
            pltpu.VMEM((rows, model), jnp.bfloat16),
            pltpu.VMEM((steps, model, width), jnp.bfloat16),
            pltpu.VMEM((2 * model // 128, rows, 128), jnp.float32),
            pltpu.SemaphoreType.DMA((steps + 1,)),
        ),
    )
    swap = [(i, i + 1) for i in range(1, count - 1, 2)]
    swap += [(j, i) for i, j in swap]
    def exchange(own, bit):
        return lax.ppermute(own, AXES, list(enumerate(partners(bit, count))))

    def pool(own, got, *after):
        return call(pool_kernel, block, vmem(2), own, got, after=after)

    teams = [
        [i for i in range(count) if i >> 7 == x and i & 1 == core]
        for x in range(count >> 7)
        for core in range(2)
    ]
    spread = lax.all_to_all(level_6, AXES, 0, 0, axis_index_groups=teams, tiled=True)
    near_sib = exchange(near, 0)
    own_3 = call(pool_near_kernel, block, vmem(2), level_3, near_sib)
    sib_3 = exchange(own_3, 1)
    other_halo = lax.ppermute(other, AXES, swap)
    own_4 = pool(own_3, sib_3)
    sib_4 = exchange(own_4, 2)
    mine = call(
        unpack_kernel, bf16(5 * BLOCK // 2, 2 * model), [SMEM, *vmem(1)],
        place, spread.reshape(members, packed, 128),
        scratch=(pltpu.VMEM((members * packed, 128), jnp.float32),),
        after=(own_4, other_halo),
    )
    theirs = exchange(mine, 0)
    own_9 = call(own_9_kernel, block, vmem(2), mine, theirs)
    sib_9 = exchange(own_9, 7)
    own_5 = pool(own_4, sib_4, own_9)
    sib_5 = exchange(own_5, 3)
    own_10 = pool(own_9, sib_9, own_5)
    sib_10 = exchange(own_10, 8)
    q, num, tot = call(
        functools.partial(local_kernel, count),
        (bf16(rows, model), f32(rows, model), f32(rows, model)),
        [SMEM, *vmem(1), in_hbm, *vmem(7)],
        place, tokens, stay(w_qkv), kv, near_sib, other_halo, mine, theirs, sib_3, sib_4,
        flops=10**9,
        scratch=(
            pltpu.VMEM((rows + 2 * BLOCK, 2 * model), jnp.bfloat16),
            pltpu.VMEM((rows // 2, 2 * model), jnp.bfloat16),
            pltpu.VMEM((model, model), jnp.bfloat16),
            pltpu.SemaphoreType.DMA(()),
        ),
        after=(own_10,),
    )
    return call(
        final_kernel,
        bf16(rows, model),
        [*vmem(6), in_hbm],
        q, num, tot, sib_5, sib_9, sib_10, stay(w_out),
        flops=10**9,
        scratch=(
            pltpu.VMEM((rows, model), jnp.bfloat16),
            pltpu.VMEM((model, model), jnp.bfloat16),
            pltpu.SemaphoreType.DMA(()),
        ),
    )


def solution(mesh):
    return jax.shard_map(
        per_device,
        mesh=mesh,
        in_specs=(P(AXES, None), P(), P()),
        out_specs=P(AXES, None),
        check_vma=False,
    )
```

```python
import functools

import jax
import jax.numpy as jnp
import numpy as np
from jax import lax
from jax.experimental import pallas as pl
from jax.experimental.pallas import tpu as pltpu
from jax.sharding import PartitionSpec as P

HEADS = 8
BLOCK = 64
AXES = ("gx", "gy")
FAR8 = (6, 7, 4, 5, 2, 3, 0, 1)
FAR4 = (3, 2, 1, 0)


def partners(bit, count):
    route = []
    for index in range(count):
        if bit == 3:
            route.append(index & ~14 | FAR8[index >> 1 & 7] << 1)
        elif bit == 6:
            route.append(index & ~112 | FAR8[index >> 4 & 7] << 4)
        elif bit == 8:
            route.append(index & ~384 | FAR4[index >> 7 & 3] << 7)
        else:
            route.append(index ^ 1 << bit)
    return route


def vmem(count):
    return [pl.BlockSpec(memory_space=pltpu.VMEM)] * count


SMEM = pl.BlockSpec(memory_space=pltpu.SMEM)


def call(kernel, outs, in_specs, *args, flops=0, scratch=(), limit=10, after=()):
    count = len(args)

    def body(*refs):
        kernel(*refs[:count], *refs[count + len(after) :])

    return pl.pallas_call(
        body,
        out_shape=outs,
        in_specs=list(in_specs) + [pl.BlockSpec(memory_space=pl.ANY)] * len(after),
        out_specs=jax.tree.map(lambda _: pl.BlockSpec(memory_space=pltpu.VMEM), outs),
        scratch_shapes=list(scratch),
        compiler_params=pltpu.CompilerParams(vmem_limit_bytes=limit * 2**20),
        cost_estimate=pl.CostEstimate(flops=flops, bytes_accessed=2**20, transcendentals=0),
    )(*args, *after)


def pool_matrix(rows):
    r = lax.broadcasted_iota(jnp.int32, (rows, 2 * rows), 0)
    c = lax.broadcasted_iota(jnp.int32, (rows, 2 * rows), 1)
    return jnp.where(c >> 1 == r, 0.5, 0.0).astype(jnp.bfloat16)


def pooled(block):
    return jnp.dot(
        pool_matrix(block.shape[0] // 2), block, preferred_element_type=jnp.float32
    ).astype(jnp.bfloat16)


def project_kernel(
    place, x_hbm, w_hbm, kv_ref, near_ref, other_ref, l3_ref, packed_ref, x_buf, w_buf, part_buf, sems
):
    rows, model = x_buf.shape
    width = w_buf.shape[2]
    steps = w_buf.shape[0]
    x_copy = pltpu.make_async_copy(x_hbm, x_buf, sems.at[steps])
    x_copy.start()
    copies = []
    for step in range(steps):
        columns = pl.ds(model + step * width, width)
        copy = pltpu.make_async_copy(w_hbm.at[:, columns], w_buf.at[step], sems.at[step])
        copy.start()
        copies.append(copy)
    x_copy.wait()
    x = x_buf[...]
    pieces = []
    for step in range(steps):
        copies[step].wait()
        lanes = slice(step * width, (step + 1) * width)
        part = jnp.dot(x, w_buf[step], preferred_element_type=jnp.float32).astype(jnp.bfloat16)
        kv_ref[:, lanes] = part
        wide = part.astype(jnp.float32)
        for at in range(0, width, 128):
            tile = (step * width + at) // 128
            part_buf[tile] = wide[:, at : at + 128]
            size = rows
            while size > 8:
                size //= 2
                even = part_buf[tile, pl.ds(0, size, stride=2), :]
                odd = part_buf[tile, pl.ds(1, size, stride=2), :]
                level = ((even + odd) * 0.5).astype(jnp.bfloat16)
                if size == BLOCK:
                    near_ref[BLOCK:, tile * 128 : (tile + 1) * 128] = level
                if size == BLOCK // 2:
                    l3_ref[:, tile * 128 : (tile + 1) * 128] = level
                part_buf[tile, :size, :] = level.astype(jnp.float32)
            pieces.append(level.astype(jnp.float32))
    packed = pooled(jnp.concatenate(pieces, axis=0).astype(jnp.bfloat16))
    size = packed.shape[0]
    for copy in range(packed_ref.shape[0] // size):
        packed_ref[copy * size : (copy + 1) * size, :] = packed
    core = place[0] & 1
    last = rows - BLOCK
    low = pl.multiple_of(core * last, BLOCK)
    high = pl.multiple_of((1 - core) * last, BLOCK)
    near_ref[:BLOCK, :] = kv_ref[pl.ds(high, BLOCK), :]
    other_ref[...] = kv_ref[pl.ds(low, BLOCK), :]


def unpack_kernel(place, in_ref, sib_6_ref, own_7_ref, wide):
    members, rows, _ = in_ref.shape
    half = members // 2
    wide[...] = in_ref[...].reshape(members * rows, 128).astype(jnp.float32)
    upper = (place[0] >> 4) & 1
    for tile in range(rows // 4):
        lanes = slice(tile * 128, (tile + 1) * 128)
        parts = [
            wide[pl.ds(tile * 4 + row, members, stride=rows), :] for row in range(4)
        ]
        sib = [jnp.where(upper == 1, part[:half], part[half:]) for part in parts]
        sib_6_ref[:, lanes] = jnp.concatenate(sib, axis=0).astype(jnp.bfloat16)
        pairs = [(parts[0] + parts[1]) * 0.5, (parts[2] + parts[3]) * 0.5]
        own_7_ref[:, lanes] = jnp.concatenate(pairs, axis=0).astype(jnp.bfloat16)


def pool_near_kernel(mine_ref, sib_ref, out_ref):
    out_ref[: BLOCK // 2, :] = mine_ref[...]
    out_ref[BLOCK // 2 :, :] = pooled(sib_ref[BLOCK:, :])


def pool_halves_kernel(own_ref, sib_ref, out_ref):
    half = BLOCK // 2
    for num, ref in enumerate((own_ref, sib_ref)):
        block = ref[...].astype(jnp.float32)
        out_ref[num * half : (num + 1) * half, :] = (
            (block[:half] + block[half:]) * 0.5
        ).astype(jnp.bfloat16)


def pool_kernel(*refs):
    ins, out_ref = refs[:-1], refs[-1]
    half = BLOCK // len(ins)
    for num, ref in enumerate(ins):
        out_ref[num * half : (num + 1) * half, :] = pooled(ref[...])


def attend_pair(q, keys, values, ones):
    rows = q.shape[0]
    lane = lax.broadcasted_iota(jnp.int32, q.shape, 1)
    first = lane < 64
    zero = jnp.zeros_like(q)
    both = jnp.concatenate([jnp.where(first, q, zero), jnp.where(first, zero, q)], axis=0)
    scores = lax.dot_general(
        both, keys, (((1,), (1,)), ((), ())), preferred_element_type=jnp.float32
    )
    weights = jnp.exp(scores).astype(jnp.bfloat16)
    sums = jnp.dot(
        weights, jnp.concatenate([values, ones], axis=1), preferred_element_type=jnp.float32
    )
    num = jnp.where(first, sums[:rows, :128], sums[rows:, :128])
    tot = jnp.where(first, sums[:rows, 128:], sums[rows:, 128:])
    return num, tot


def local_kernel(
    count, place, x_ref, w_hbm, kv_ref, near_ref, other_ref, sib_3_ref, sib_4_ref,
    sib_5_ref, q_ref, num_ref, tot_ref, pad, l1, w_ref, sem
):
    rows, model = x_ref.shape
    blocks = rows // BLOCK
    copy = pltpu.make_async_copy(w_hbm.at[:, pl.ds(0, model)], w_ref, sem)
    copy.start()
    core = place[0] & 1
    sib_halo = near_ref[:BLOCK, :]
    other = other_ref[...]
    is_first = core == 0
    pad[:BLOCK, :] = jnp.where(is_first, other, sib_halo)
    pad[BLOCK : BLOCK + rows, :] = kv_ref[...]
    pad[BLOCK + rows :, :] = jnp.where(is_first, sib_halo, other)
    l1[...] = pooled(kv_ref[...])
    copy.wait()
    q_ref[...] = (
        jnp.dot(x_ref[...], w_ref[...], preferred_element_type=jnp.float32)
        .astype(jnp.bfloat16) * jnp.bfloat16(0.125)
    )
    key_row = lax.broadcasted_iota(jnp.int32, (4 * BLOCK, 128), 0)
    for i in range(blocks):
        ones = jnp.ones((4 * BLOCK, 128), jnp.float32)
        if i == 0:
            ones = jnp.where((key_row < BLOCK) & (place[0] == 0), 0.0, ones)
        if i == blocks - 1:
            ones = jnp.where((key_row >= 2 * BLOCK) & (key_row < 3 * BLOCK) & (place[0] == count - 1), 0.0, ones)
        ones = ones.astype(jnp.bfloat16)
        sib = (i >> 1) ^ 1
        here = slice(i * BLOCK, (i + 1) * BLOCK)
        for lanes in range(0, model, 128):
            kl = slice(lanes, lanes + 128)
            vl = slice(model + lanes, model + lanes + 128)
            keys = jnp.concatenate(
                [pad[i * BLOCK : (i + 3) * BLOCK, kl], l1[sib * BLOCK : (sib + 1) * BLOCK, kl]], axis=0
            )
            values = jnp.concatenate(
                [pad[i * BLOCK : (i + 3) * BLOCK, vl], l1[sib * BLOCK : (sib + 1) * BLOCK, vl]], axis=0
            )
            num, tot = attend_pair(q_ref[here, kl], keys, values, ones)
            num_ref[here, kl] = num
            tot_ref[here, kl] = tot
    far = far_blocks((near_ref, sib_3_ref, sib_4_ref, sib_5_ref))
    for lanes in range(0, model, 128):
        kl = slice(lanes, lanes + 128)
        num, tot = far_sums(far, q_ref[:, kl], lanes, model)
        num_ref[:, kl] += num
        tot_ref[:, kl] += tot


def far_blocks(refs):
    return jnp.concatenate(
        [ref[BLOCK:, :] if ref.shape[0] == 2 * BLOCK else ref[...] for ref in refs], axis=0
    )


def far_sums(far, q, lanes, model):
    keys = far[:, lanes : lanes + 128]
    values = far[:, model + lanes : model + lanes + 128]
    return attend_pair(q, keys, values, jnp.ones(values.shape, jnp.bfloat16))


def far_kernel(q_ref, num_in, tot_in, *refs):
    num_ref, tot_ref = refs[-2:]
    model = q_ref.shape[1]
    far = far_blocks(refs[:-2])
    for lanes in range(0, model, 128):
        at = slice(lanes, lanes + 128)
        num, tot = far_sums(far, q_ref[:, at], lanes, model)
        num_ref[:, at] = num_in[:, at] + num
        tot_ref[:, at] = tot_in[:, at] + tot


def final_kernel(
    q_ref, num_in, tot_in, sib_ref, w_hbm, out_ref, att, w_ref, sem
):
    copy = pltpu.make_async_copy(w_hbm, w_ref, sem)
    copy.start()
    model = q_ref.shape[1]
    far = sib_ref[...]
    for lanes in range(0, model, 128):
        at = slice(lanes, lanes + 128)
        num, tot = far_sums(far, q_ref[:, at], lanes, model)
        att[:, at] = ((num_in[:, at] + num) / (tot_in[:, at] + tot)).astype(jnp.bfloat16)
    copy.wait()
    out_ref[...] = jnp.dot(att[...], w_ref[...], preferred_element_type=jnp.float32).astype(
        jnp.bfloat16
    )


def per_device(tokens, w_qkv, w_out):
    rows, model = tokens.shape
    index = lax.axis_index(AXES)
    count = lax.axis_size(AXES)
    place = index.astype(jnp.int32).reshape(1)
    bf16 = lambda *shape: jax.ShapeDtypeStruct(shape, jnp.bfloat16)
    f32 = lambda *shape: jax.ShapeDtypeStruct(shape, jnp.float32)
    in_hbm = pl.BlockSpec(memory_space=pl.ANY)
    stay = lambda array: pltpu.with_memory_space_constraint(array, pltpu.HBM)
    steps = 2
    width = 2 * model // steps
    members = 32
    packed = 4 * 2 * model // 128
    block = bf16(BLOCK, 2 * model)
    kv, near, other, level_3, level_6 = call(
        project_kernel,
        (
            bf16(rows, 2 * model), bf16(2 * BLOCK, 2 * model), block,
            bf16(BLOCK // 2, 2 * model), bf16(members * packed, 128),
        ),
        [SMEM, in_hbm, in_hbm],
        place, stay(tokens), stay(w_qkv),
        flops=4 * rows * model * model,
        scratch=(
            pltpu.VMEM((rows, model), jnp.bfloat16),
            pltpu.VMEM((steps, model, width), jnp.bfloat16),
            pltpu.VMEM((2 * model // 128, rows, 128), jnp.float32),
            pltpu.SemaphoreType.DMA((steps + 1,)),
        ),
    )
    swap = [(i, i + 1) for i in range(1, count - 1, 2)]
    swap += [(j, i) for i, j in swap]
    def exchange(own, bit):
        return lax.ppermute(own, AXES, list(enumerate(partners(bit, count))))

    def pool(own, got, *after):
        return call(pool_kernel, block, vmem(2), own, got, after=after)

    teams = [list(range(i, i + members)) for i in range(0, count, members)]
    spread = lax.all_to_all(level_6, AXES, 0, 0, axis_index_groups=teams, tiled=True)
    near_sib = exchange(near, 0)
    own_3 = call(pool_near_kernel, block, vmem(2), level_3, near_sib)
    sib_3 = exchange(own_3, 1)
    other_halo = lax.ppermute(other, AXES, swap)
    sib_6, own_7 = call(
        unpack_kernel, (block, block), [SMEM, *vmem(1)],
        place, spread.reshape(members, packed, 128),
        scratch=(pltpu.VMEM((members * packed, 128), jnp.float32),),
        after=(own_3, other_halo),
    )
    sib_7 = exchange(own_7, 5)
    own_4 = pool(own_3, sib_3, own_7)
    sib_4 = exchange(own_4, 2)
    own_8 = call(pool_halves_kernel, block, vmem(2), own_7, sib_7, after=(own_4,))
    sib_8 = exchange(own_8, 6)
    own_5 = pool(own_4, sib_4, own_8)
    sib_5 = exchange(own_5, 3)
    own_9 = pool(own_8, sib_8, own_5)
    sib_9 = exchange(own_9, 7)
    q, num, tot = call(
        functools.partial(local_kernel, count),
        (bf16(rows, model), f32(rows, model), f32(rows, model)),
        [SMEM, *vmem(1), in_hbm, *vmem(6)],
        place, tokens, stay(w_qkv), kv, near_sib, other_halo, sib_3, sib_4, sib_5,
        flops=10**9,
        scratch=(
            pltpu.VMEM((rows + 2 * BLOCK, 2 * model), jnp.bfloat16),
            pltpu.VMEM((rows // 2, 2 * model), jnp.bfloat16),
            pltpu.VMEM((model, model), jnp.bfloat16),
            pltpu.SemaphoreType.DMA(()),
        ),
        after=(own_9,),
    )
    own_10 = pool(own_9, sib_9, q)
    sib_10 = exchange(own_10, 8)
    num, tot = call(
        far_kernel,
        (f32(rows, model), f32(rows, model)),
        vmem(7),
        q, num, tot, sib_6, sib_7, sib_8, sib_9,
        flops=10**9,
        after=(own_10,),
    )
    return call(
        final_kernel,
        bf16(rows, model),
        [*vmem(4), in_hbm],
        q, num, tot, sib_10, stay(w_out),
        flops=10**9,
        scratch=(
            pltpu.VMEM((rows, model), jnp.bfloat16),
            pltpu.VMEM((model, model), jnp.bfloat16),
            pltpu.SemaphoreType.DMA(()),
        ),
    )


def solution(mesh):
    return jax.shard_map(
        per_device,
        mesh=mesh,
        in_specs=(P(AXES, None), P(), P()),
        out_specs=P(AXES, None),
        check_vma=False,
    )
```

```python
import functools

import jax
import jax.numpy as jnp
import numpy as np
from jax import lax
from jax.experimental import pallas as pl
from jax.experimental.pallas import tpu as pltpu
from jax.sharding import PartitionSpec as P

HEADS = 8
BLOCK = 64
AXES = ("gx", "gy")
FAR8 = (6, 7, 4, 5, 2, 3, 0, 1)
FAR4 = (3, 2, 1, 0)


def partners(bit, count):
    route = []
    for index in range(count):
        if bit == 3:
            route.append(index & ~14 | FAR8[index >> 1 & 7] << 1)
        elif bit == 6:
            route.append(index & ~112 | FAR8[index >> 4 & 7] << 4)
        elif bit == 8:
            route.append(index & ~384 | FAR4[index >> 7 & 3] << 7)
        else:
            route.append(index ^ 1 << bit)
    return route


def vmem(count):
    return [pl.BlockSpec(memory_space=pltpu.VMEM)] * count


SMEM = pl.BlockSpec(memory_space=pltpu.SMEM)


def call(kernel, outs, in_specs, *args, flops=0, scratch=(), limit=10, after=()):
    count = len(args)

    def body(*refs):
        kernel(*refs[:count], *refs[count + len(after) :])

    return pl.pallas_call(
        body,
        out_shape=outs,
        in_specs=list(in_specs) + [pl.BlockSpec(memory_space=pl.ANY)] * len(after),
        out_specs=jax.tree.map(lambda _: pl.BlockSpec(memory_space=pltpu.VMEM), outs),
        scratch_shapes=list(scratch),
        compiler_params=pltpu.CompilerParams(vmem_limit_bytes=limit * 2**20),
        cost_estimate=pl.CostEstimate(flops=flops, bytes_accessed=2**20, transcendentals=0),
    )(*args, *after)


def pool_matrix(rows):
    r = lax.broadcasted_iota(jnp.int32, (rows, 2 * rows), 0)
    c = lax.broadcasted_iota(jnp.int32, (rows, 2 * rows), 1)
    return jnp.where(c >> 1 == r, 0.5, 0.0).astype(jnp.bfloat16)


def pooled(block):
    return jnp.dot(
        pool_matrix(block.shape[0] // 2), block, preferred_element_type=jnp.float32
    ).astype(jnp.bfloat16)


def project_kernel(
    place, x_hbm, w_hbm, kv_ref, near_ref, other_ref, l3_ref, packed_ref, x_buf, w_buf, part_buf, sems
):
    rows, model = x_buf.shape
    width = w_buf.shape[2]
    steps = w_buf.shape[0]
    x_copy = pltpu.make_async_copy(x_hbm, x_buf, sems.at[steps])
    x_copy.start()
    copies = []
    for step in range(steps):
        columns = pl.ds(model + step * width, width)
        copy = pltpu.make_async_copy(w_hbm.at[:, columns], w_buf.at[step], sems.at[step])
        copy.start()
        copies.append(copy)
    x_copy.wait()
    x = x_buf[...]
    pieces = []
    for step in range(steps):
        copies[step].wait()
        lanes = slice(step * width, (step + 1) * width)
        part = jnp.dot(x, w_buf[step], preferred_element_type=jnp.float32).astype(jnp.bfloat16)
        kv_ref[:, lanes] = part
        wide = part.astype(jnp.float32)
        for at in range(0, width, 128):
            tile = (step * width + at) // 128
            part_buf[tile] = wide[:, at : at + 128]
            size = rows
            while size > 8:
                size //= 2
                even = part_buf[tile, pl.ds(0, size, stride=2), :]
                odd = part_buf[tile, pl.ds(1, size, stride=2), :]
                level = ((even + odd) * 0.5).astype(jnp.bfloat16)
                if size == BLOCK:
                    near_ref[BLOCK:, tile * 128 : (tile + 1) * 128] = level
                if size == BLOCK // 2:
                    l3_ref[:, tile * 128 : (tile + 1) * 128] = level
                part_buf[tile, :size, :] = level.astype(jnp.float32)
            pieces.append(level.astype(jnp.float32))
    packed = pooled(jnp.concatenate(pieces, axis=0).astype(jnp.bfloat16))
    size = packed.shape[0]
    for copy in range(packed_ref.shape[0] // size):
        packed_ref[copy * size : (copy + 1) * size, :] = packed
    core = place[0] & 1
    last = rows - BLOCK
    low = pl.multiple_of(core * last, BLOCK)
    high = pl.multiple_of((1 - core) * last, BLOCK)
    near_ref[:BLOCK, :] = kv_ref[pl.ds(high, BLOCK), :]
    other_ref[...] = kv_ref[pl.ds(low, BLOCK), :]


def unpack_kernel(place, in_ref, out_ref, wide):
    members, rows, _ = in_ref.shape
    wide[...] = in_ref[...].reshape(members * rows, 128).astype(jnp.float32)
    y = (place[0] >> 4) & 3

    def mean(one, two):
        return ((one + two) * 0.5).astype(jnp.bfloat16).astype(jnp.float32)

    for tile in range(rows // 4):
        lanes = slice(tile * 128, (tile + 1) * 128)

        def level_6(start, count):
            return [
                wide[pl.ds(start * rows + tile * 4 + row, count, stride=rows), :]
                for row in range(4)
            ]

        def level_7(start, count):
            r = level_6(start, count)
            return [mean(r[0], r[1]), mean(r[2], r[3])]

        parts = (
            level_6((y ^ 1) * 8, 8)
            + level_7(((y >> 1) ^ 1) * 16, 16)
            + [mean(*level_7(0, members))]
        )
        out_ref[:, lanes] = jnp.concatenate(parts, axis=0).astype(jnp.bfloat16)


def own_8_kernel(mine_ref, sib_ref, out_ref):
    half = BLOCK // 2
    out_ref[:half, :] = mine_ref[BLOCK:, :]
    out_ref[half:, :] = sib_ref[BLOCK:, :]


def pool_near_kernel(mine_ref, sib_ref, out_ref):
    out_ref[: BLOCK // 2, :] = mine_ref[...]
    out_ref[BLOCK // 2 :, :] = pooled(sib_ref[BLOCK:, :])


def pool_halves_kernel(own_ref, sib_ref, out_ref):
    half = BLOCK // 2
    for num, ref in enumerate((own_ref, sib_ref)):
        block = ref[...].astype(jnp.float32)
        out_ref[num * half : (num + 1) * half, :] = (
            (block[:half] + block[half:]) * 0.5
        ).astype(jnp.bfloat16)


def pool_kernel(*refs):
    ins, out_ref = refs[:-1], refs[-1]
    half = BLOCK // len(ins)
    for num, ref in enumerate(ins):
        out_ref[num * half : (num + 1) * half, :] = pooled(ref[...])


def attend_pair(q, keys, values, ones):
    rows = q.shape[0]
    lane = lax.broadcasted_iota(jnp.int32, q.shape, 1)
    first = lane < 64
    zero = jnp.zeros_like(q)
    both = jnp.concatenate([jnp.where(first, q, zero), jnp.where(first, zero, q)], axis=0)
    scores = lax.dot_general(
        both, keys, (((1,), (1,)), ((), ())), preferred_element_type=jnp.float32
    )
    weights = jnp.exp(scores).astype(jnp.bfloat16)
    sums = jnp.dot(
        weights, jnp.concatenate([values, ones], axis=1), preferred_element_type=jnp.float32
    )
    num = jnp.where(first, sums[:rows, :128], sums[rows:, :128])
    tot = jnp.where(first, sums[:rows, 128:], sums[rows:, 128:])
    return num, tot


def local_kernel(
    count, place, x_ref, w_hbm, kv_ref, near_ref, other_ref, sib_3_ref, sib_4_ref,
    mine_ref, theirs_ref, sib_8_ref, q_ref, num_ref, tot_ref, pad, l1, w_ref, sem
):
    rows, model = x_ref.shape
    blocks = rows // BLOCK
    copy = pltpu.make_async_copy(w_hbm.at[:, pl.ds(0, model)], w_ref, sem)
    copy.start()
    core = place[0] & 1
    sib_halo = near_ref[:BLOCK, :]
    other = other_ref[...]
    is_first = core == 0
    pad[:BLOCK, :] = jnp.where(is_first, other, sib_halo)
    pad[BLOCK : BLOCK + rows, :] = kv_ref[...]
    pad[BLOCK + rows :, :] = jnp.where(is_first, sib_halo, other)
    l1[...] = pooled(kv_ref[...])
    copy.wait()
    q_ref[...] = (
        jnp.dot(x_ref[...], w_ref[...], preferred_element_type=jnp.float32)
        .astype(jnp.bfloat16) * jnp.bfloat16(0.125)
    )
    key_row = lax.broadcasted_iota(jnp.int32, (4 * BLOCK, 128), 0)
    for i in range(blocks):
        ones = jnp.ones((4 * BLOCK, 128), jnp.float32)
        if i == 0:
            ones = jnp.where((key_row < BLOCK) & (place[0] == 0), 0.0, ones)
        if i == blocks - 1:
            ones = jnp.where((key_row >= 2 * BLOCK) & (key_row < 3 * BLOCK) & (place[0] == count - 1), 0.0, ones)
        ones = ones.astype(jnp.bfloat16)
        sib = (i >> 1) ^ 1
        here = slice(i * BLOCK, (i + 1) * BLOCK)
        for lanes in range(0, model, 128):
            kl = slice(lanes, lanes + 128)
            vl = slice(model + lanes, model + lanes + 128)
            keys = jnp.concatenate(
                [pad[i * BLOCK : (i + 3) * BLOCK, kl], l1[sib * BLOCK : (sib + 1) * BLOCK, kl]], axis=0
            )
            values = jnp.concatenate(
                [pad[i * BLOCK : (i + 3) * BLOCK, vl], l1[sib * BLOCK : (sib + 1) * BLOCK, vl]], axis=0
            )
            num, tot = attend_pair(q_ref[here, kl], keys, values, ones)
            num_ref[here, kl] = num
            tot_ref[here, kl] = tot
    far = far_blocks((near_ref, sib_3_ref, sib_4_ref, mine_ref, theirs_ref, sib_8_ref))
    for lanes in range(0, model, 128):
        kl = slice(lanes, lanes + 128)
        num, tot = far_sums(far, q_ref[:, kl], lanes, model)
        num_ref[:, kl] += num
        tot_ref[:, kl] += tot


def far_blocks(refs):
    blocks = []
    for ref in refs:
        if ref.shape[0] == 2 * BLOCK:
            blocks.append(ref[BLOCK:, :])
        else:
            blocks.append(ref[:BLOCK, :])
    return jnp.concatenate(blocks, axis=0)


def far_sums(far, q, lanes, model):
    keys = far[:, lanes : lanes + 128]
    values = far[:, model + lanes : model + lanes + 128]
    return attend_pair(q, keys, values, jnp.ones(values.shape, jnp.bfloat16))


def final_kernel(
    place, q_ref, num_in, tot_in, sib_5_ref, sib_9_ref, pair_ref, w_hbm, out_ref, att, w_ref, sem
):
    copy = pltpu.make_async_copy(w_hbm, w_ref, sem)
    copy.start()
    model = q_ref.shape[1]
    start = pl.multiple_of((1 - (place[0] >> 8)) * BLOCK, BLOCK)
    far = jnp.concatenate(
        [sib_5_ref[...], sib_9_ref[...], pair_ref[pl.ds(start, BLOCK), :]], axis=0
    )
    for lanes in range(0, model, 128):
        at = slice(lanes, lanes + 128)
        num, tot = far_sums(far, q_ref[:, at], lanes, model)
        att[:, at] = ((num_in[:, at] + num) / (tot_in[:, at] + tot)).astype(jnp.bfloat16)
    copy.wait()
    out_ref[...] = jnp.dot(att[...], w_ref[...], preferred_element_type=jnp.float32).astype(
        jnp.bfloat16
    )


def per_device(tokens, w_qkv, w_out):
    rows, model = tokens.shape
    index = lax.axis_index(AXES)
    count = lax.axis_size(AXES)
    place = index.astype(jnp.int32).reshape(1)
    bf16 = lambda *shape: jax.ShapeDtypeStruct(shape, jnp.bfloat16)
    f32 = lambda *shape: jax.ShapeDtypeStruct(shape, jnp.float32)
    in_hbm = pl.BlockSpec(memory_space=pl.ANY)
    stay = lambda array: pltpu.with_memory_space_constraint(array, pltpu.HBM)
    steps = 2
    width = 2 * model // steps
    members = 32
    packed = 4 * 2 * model // 128
    block = bf16(BLOCK, 2 * model)
    kv, near, other, level_3, level_6 = call(
        project_kernel,
        (
            bf16(rows, 2 * model), bf16(2 * BLOCK, 2 * model), block,
            bf16(BLOCK // 2, 2 * model), bf16(members * packed, 128),
        ),
        [SMEM, in_hbm, in_hbm],
        place, stay(tokens), stay(w_qkv),
        flops=4 * rows * model * model,
        scratch=(
            pltpu.VMEM((rows, model), jnp.bfloat16),
            pltpu.VMEM((steps, model, width), jnp.bfloat16),
            pltpu.VMEM((2 * model // 128, rows, 128), jnp.float32),
            pltpu.SemaphoreType.DMA((steps + 1,)),
        ),
    )
    swap = [(i, i + 1) for i in range(1, count - 1, 2)]
    swap += [(j, i) for i, j in swap]
    def exchange(own, bit):
        return lax.ppermute(own, AXES, list(enumerate(partners(bit, count))))

    def pool(own, got, *after):
        return call(pool_kernel, block, vmem(2), own, got, after=after)

    teams = [
        [i for i in range(count) if i >> 6 == part and i & 1 == core]
        for part in range(count >> 6)
        for core in range(2)
    ]
    spread = lax.all_to_all(level_6, AXES, 0, 0, axis_index_groups=teams, tiled=True)
    near_sib = exchange(near, 0)
    own_3 = call(pool_near_kernel, block, vmem(2), level_3, near_sib)
    sib_3 = exchange(own_3, 1)
    other_halo = lax.ppermute(other, AXES, swap)
    own_4 = pool(own_3, sib_3)
    mine = call(
        unpack_kernel, bf16(3 * BLOCK // 2, 2 * model), [SMEM, *vmem(1)],
        place, spread.reshape(members, packed, 128),
        scratch=(pltpu.VMEM((members * packed, 128), jnp.float32),),
        after=(own_4, other_halo),
    )
    theirs = exchange(mine, 0)
    sib_4 = exchange(own_4, 2)
    own_8 = call(own_8_kernel, block, vmem(2), mine, theirs)
    sib_8 = exchange(own_8, 6)
    own_5 = pool(own_4, sib_4, own_8)
    sib_5 = exchange(own_5, 3)
    own_9 = call(pool_halves_kernel, block, vmem(2), own_8, sib_8, after=(own_5,))
    sib_9 = exchange(own_9, 7)
    q, num, tot = call(
        functools.partial(local_kernel, count),
        (bf16(rows, model), f32(rows, model), f32(rows, model)),
        [SMEM, *vmem(1), in_hbm, *vmem(8)],
        place, tokens, stay(w_qkv), kv, near_sib, other_halo, sib_3, sib_4, mine, theirs, sib_8,
        flops=10**9,
        scratch=(
            pltpu.VMEM((rows + 2 * BLOCK, 2 * model), jnp.bfloat16),
            pltpu.VMEM((rows // 2, 2 * model), jnp.bfloat16),
            pltpu.VMEM((model, model), jnp.bfloat16),
            pltpu.SemaphoreType.DMA(()),
        ),
        after=(own_9,),
    )
    own_10 = pool(own_9, sib_9, q, sib_5)
    to = partners(8, count)
    pairs = [[i, to[i]] for i in range(count >> 1)]
    pair = lax.all_gather(own_10, AXES, axis_index_groups=pairs, tiled=True)
    return call(
        final_kernel,
        bf16(rows, model),
        [SMEM, *vmem(6), in_hbm],
        place, q, num, tot, sib_5, sib_9, pair, stay(w_out),
        flops=10**9,
        scratch=(
            pltpu.VMEM((rows, model), jnp.bfloat16),
            pltpu.VMEM((model, model), jnp.bfloat16),
            pltpu.SemaphoreType.DMA(()),
        ),
    )


def solution(mesh):
    return jax.shard_map(
        per_device,
        mesh=mesh,
        in_specs=(P(AXES, None), P(), P()),
        out_specs=P(AXES, None),
        check_vma=False,
    )
```

```python
import functools

import jax
import jax.numpy as jnp
import numpy as np
from jax import lax
from jax.experimental import pallas as pl
from jax.experimental.pallas import tpu as pltpu
from jax.sharding import PartitionSpec as P

HEADS = 8
BLOCK = 64
AXES = ("gx", "gy")
FAR8 = (6, 7, 4, 5, 2, 3, 0, 1)
FAR4 = (3, 2, 1, 0)


def partners(bit, count):
    route = []
    for index in range(count):
        if bit == 3:
            route.append(index & ~14 | FAR8[index >> 1 & 7] << 1)
        elif bit == 6:
            route.append(index & ~112 | FAR8[index >> 4 & 7] << 4)
        elif bit == 8:
            route.append(index & ~384 | FAR4[index >> 7 & 3] << 7)
        else:
            route.append(index ^ 1 << bit)
    return route


def vmem(count):
    return [pl.BlockSpec(memory_space=pltpu.VMEM)] * count


SMEM = pl.BlockSpec(memory_space=pltpu.SMEM)


def call(kernel, outs, in_specs, *args, flops=0, scratch=(), limit=10, after=()):
    count = len(args)

    def body(*refs):
        kernel(*refs[:count], *refs[count + len(after) :])

    return pl.pallas_call(
        body,
        out_shape=outs,
        in_specs=list(in_specs) + [pl.BlockSpec(memory_space=pl.ANY)] * len(after),
        out_specs=jax.tree.map(lambda _: pl.BlockSpec(memory_space=pltpu.VMEM), outs),
        scratch_shapes=list(scratch),
        compiler_params=pltpu.CompilerParams(vmem_limit_bytes=limit * 2**20),
        cost_estimate=pl.CostEstimate(flops=flops, bytes_accessed=2**20, transcendentals=0),
    )(*args, *after)


def pool_matrix(rows):
    r = lax.broadcasted_iota(jnp.int32, (rows, 2 * rows), 0)
    c = lax.broadcasted_iota(jnp.int32, (rows, 2 * rows), 1)
    return jnp.where(c >> 1 == r, 0.5, 0.0).astype(jnp.bfloat16)


def pooled(block):
    return jnp.dot(
        pool_matrix(block.shape[0] // 2), block, preferred_element_type=jnp.float32
    ).astype(jnp.bfloat16)


def project_kernel(
    place, x_hbm, w_hbm, kv_ref, near_ref, other_ref, l3_ref, packed_ref, x_buf, w_buf, part_buf, sems
):
    rows, model = x_buf.shape
    width = w_buf.shape[2]
    steps = w_buf.shape[0]
    x_copy = pltpu.make_async_copy(x_hbm, x_buf, sems.at[steps])
    x_copy.start()
    copies = []
    for step in range(steps):
        columns = pl.ds(model + step * width, width)
        copy = pltpu.make_async_copy(w_hbm.at[:, columns], w_buf.at[step], sems.at[step])
        copy.start()
        copies.append(copy)
    x_copy.wait()
    x = x_buf[...]
    pieces = []
    for step in range(steps):
        copies[step].wait()
        lanes = slice(step * width, (step + 1) * width)
        part = jnp.dot(x, w_buf[step], preferred_element_type=jnp.float32).astype(jnp.bfloat16)
        kv_ref[:, lanes] = part
        wide = part.astype(jnp.float32)
        for at in range(0, width, 128):
            tile = (step * width + at) // 128
            part_buf[tile] = wide[:, at : at + 128]
            size = rows
            while size > 8:
                size //= 2
                even = part_buf[tile, pl.ds(0, size, stride=2), :]
                odd = part_buf[tile, pl.ds(1, size, stride=2), :]
                level = ((even + odd) * 0.5).astype(jnp.bfloat16)
                if size == BLOCK:
                    near_ref[BLOCK:, tile * 128 : (tile + 1) * 128] = level
                if size == BLOCK // 2:
                    l3_ref[:, tile * 128 : (tile + 1) * 128] = level
                part_buf[tile, :size, :] = level.astype(jnp.float32)
            pieces.append(level.astype(jnp.float32))
    packed = pooled(jnp.concatenate(pieces, axis=0).astype(jnp.bfloat16))
    size = packed.shape[0]
    for copy in range(packed_ref.shape[0] // size):
        packed_ref[copy * size : (copy + 1) * size, :] = packed
    core = place[0] & 1
    last = rows - BLOCK
    low = pl.multiple_of(core * last, BLOCK)
    high = pl.multiple_of((1 - core) * last, BLOCK)
    near_ref[:BLOCK, :] = kv_ref[pl.ds(high, BLOCK), :]
    other_ref[...] = kv_ref[pl.ds(low, BLOCK), :]


def unpack_kernel(place, in_ref, out_ref, wide):
    members, rows, _ = in_ref.shape
    wide[...] = in_ref[...].reshape(members * rows, 128).astype(jnp.float32)
    y = (place[0] >> 4) & 3

    def mean(one, two):
        return ((one + two) * 0.5).astype(jnp.bfloat16).astype(jnp.float32)

    for tile in range(rows // 4):
        lanes = slice(tile * 128, (tile + 1) * 128)

        def level_6(start, count):
            return [
                wide[pl.ds(start * rows + tile * 4 + row, count, stride=rows), :]
                for row in range(4)
            ]

        def level_7(start, count):
            r = level_6(start, count)
            return [mean(r[0], r[1]), mean(r[2], r[3])]

        parts = (
            level_6((y ^ 1) * 8, 8)
            + level_7(((y >> 1) ^ 1) * 16, 16)
            + [mean(*level_7(0, members))]
        )
        out_ref[:, lanes] = jnp.concatenate(parts, axis=0).astype(jnp.bfloat16)


def own_8_kernel(mine_ref, sib_ref, out_ref):
    half = BLOCK // 2
    out_ref[:half, :] = mine_ref[BLOCK:, :]
    out_ref[half:, :] = sib_ref[BLOCK:, :]


def pool_near_kernel(mine_ref, sib_ref, out_ref):
    out_ref[: BLOCK // 2, :] = mine_ref[...]
    out_ref[BLOCK // 2 :, :] = pooled(sib_ref[BLOCK:, :])


def pool_halves_kernel(own_ref, sib_ref, out_ref):
    half = BLOCK // 2
    for num, ref in enumerate((own_ref, sib_ref)):
        block = ref[...].astype(jnp.float32)
        out_ref[num * half : (num + 1) * half, :] = (
            (block[:half] + block[half:]) * 0.5
        ).astype(jnp.bfloat16)


def pool_kernel(*refs):
    ins, out_ref = refs[:-1], refs[-1]
    half = BLOCK // len(ins)
    for num, ref in enumerate(ins):
        out_ref[num * half : (num + 1) * half, :] = pooled(ref[...])


def attend_pair(q, keys, values, ones):
    rows = q.shape[0]
    lane = lax.broadcasted_iota(jnp.int32, q.shape, 1)
    first = lane < 64
    zero = jnp.zeros_like(q)
    both = jnp.concatenate([jnp.where(first, q, zero), jnp.where(first, zero, q)], axis=0)
    scores = lax.dot_general(
        both, keys, (((1,), (1,)), ((), ())), preferred_element_type=jnp.float32
    )
    weights = jnp.exp(scores).astype(jnp.bfloat16)
    sums = jnp.dot(
        weights, jnp.concatenate([values, ones], axis=1), preferred_element_type=jnp.float32
    )
    num = jnp.where(first, sums[:rows, :128], sums[rows:, :128])
    tot = jnp.where(first, sums[:rows, 128:], sums[rows:, 128:])
    return num, tot


def local_kernel(
    count, place, x_ref, w_hbm, kv_ref, near_ref, other_ref, both_3_ref, sib_4_ref,
    mine_ref, theirs_ref, sib_8_ref, q_ref, num_ref, tot_ref, pad, l1, w_ref, sem
):
    rows, model = x_ref.shape
    blocks = rows // BLOCK
    copy = pltpu.make_async_copy(w_hbm.at[:, pl.ds(0, model)], w_ref, sem)
    copy.start()
    core = place[0] & 1
    sib_halo = near_ref[:BLOCK, :]
    other = other_ref[...]
    is_first = core == 0
    pad[:BLOCK, :] = jnp.where(is_first, other, sib_halo)
    pad[BLOCK : BLOCK + rows, :] = kv_ref[...]
    pad[BLOCK + rows :, :] = jnp.where(is_first, sib_halo, other)
    l1[...] = pooled(kv_ref[...])
    copy.wait()
    q_ref[...] = (
        jnp.dot(x_ref[...], w_ref[...], preferred_element_type=jnp.float32)
        .astype(jnp.bfloat16) * jnp.bfloat16(0.125)
    )
    key_row = lax.broadcasted_iota(jnp.int32, (4 * BLOCK, 128), 0)
    for i in range(blocks):
        ones = jnp.ones((4 * BLOCK, 128), jnp.float32)
        if i == 0:
            ones = jnp.where((key_row < BLOCK) & (place[0] == 0), 0.0, ones)
        if i == blocks - 1:
            ones = jnp.where((key_row >= 2 * BLOCK) & (key_row < 3 * BLOCK) & (place[0] == count - 1), 0.0, ones)
        ones = ones.astype(jnp.bfloat16)
        sib = (i >> 1) ^ 1
        here = slice(i * BLOCK, (i + 1) * BLOCK)
        for lanes in range(0, model, 128):
            kl = slice(lanes, lanes + 128)
            vl = slice(model + lanes, model + lanes + 128)
            keys = jnp.concatenate(
                [pad[i * BLOCK : (i + 3) * BLOCK, kl], l1[sib * BLOCK : (sib + 1) * BLOCK, kl]], axis=0
            )
            values = jnp.concatenate(
                [pad[i * BLOCK : (i + 3) * BLOCK, vl], l1[sib * BLOCK : (sib + 1) * BLOCK, vl]], axis=0
            )
            num, tot = attend_pair(q_ref[here, kl], keys, values, ones)
            num_ref[here, kl] = num
            tot_ref[here, kl] = tot
    start = pl.multiple_of((1 - ((place[0] >> 1) & 1)) * BLOCK, BLOCK)
    sib_3 = both_3_ref[pl.ds(start, BLOCK), :]
    far = far_blocks((near_ref, sib_3, sib_4_ref, mine_ref, theirs_ref, sib_8_ref))
    for lanes in range(0, model, 128):
        kl = slice(lanes, lanes + 128)
        num, tot = far_sums(far, q_ref[:, kl], lanes, model)
        num_ref[:, kl] += num
        tot_ref[:, kl] += tot


def far_blocks(refs):
    blocks = []
    for ref in refs:
        if ref.shape[0] == 2 * BLOCK:
            blocks.append(ref[BLOCK:, :])
        else:
            blocks.append(ref[:BLOCK, :])
    return jnp.concatenate(blocks, axis=0)


def far_sums(far, q, lanes, model):
    keys = far[:, lanes : lanes + 128]
    values = far[:, model + lanes : model + lanes + 128]
    return attend_pair(q, keys, values, jnp.ones(values.shape, jnp.bfloat16))


def final_kernel(
    place, q_ref, num_in, tot_in, sib_5_ref, sib_9_ref, pair_ref, w_hbm, out_ref, att, w_ref, sem
):
    copy = pltpu.make_async_copy(w_hbm, w_ref, sem)
    copy.start()
    model = q_ref.shape[1]
    start = pl.multiple_of((1 - (place[0] >> 8)) * BLOCK, BLOCK)
    far = jnp.concatenate(
        [sib_5_ref[...], sib_9_ref[...], pair_ref[pl.ds(start, BLOCK), :]], axis=0
    )
    for lanes in range(0, model, 128):
        at = slice(lanes, lanes + 128)
        num, tot = far_sums(far, q_ref[:, at], lanes, model)
        att[:, at] = ((num_in[:, at] + num) / (tot_in[:, at] + tot)).astype(jnp.bfloat16)
    copy.wait()
    out_ref[...] = jnp.dot(att[...], w_ref[...], preferred_element_type=jnp.float32).astype(
        jnp.bfloat16
    )


def per_device(tokens, w_qkv, w_out):
    rows, model = tokens.shape
    index = lax.axis_index(AXES)
    count = lax.axis_size(AXES)
    place = index.astype(jnp.int32).reshape(1)
    bf16 = lambda *shape: jax.ShapeDtypeStruct(shape, jnp.bfloat16)
    f32 = lambda *shape: jax.ShapeDtypeStruct(shape, jnp.float32)
    in_hbm = pl.BlockSpec(memory_space=pl.ANY)
    stay = lambda array: pltpu.with_memory_space_constraint(array, pltpu.HBM)
    steps = 2
    width = 2 * model // steps
    members = 32
    packed = 4 * 2 * model // 128
    block = bf16(BLOCK, 2 * model)
    kv, near, other, level_3, level_6 = call(
        project_kernel,
        (
            bf16(rows, 2 * model), bf16(2 * BLOCK, 2 * model), block,
            bf16(BLOCK // 2, 2 * model), bf16(members * packed, 128),
        ),
        [SMEM, in_hbm, in_hbm],
        place, stay(tokens), stay(w_qkv),
        flops=4 * rows * model * model,
        scratch=(
            pltpu.VMEM((rows, model), jnp.bfloat16),
            pltpu.VMEM((steps, model, width), jnp.bfloat16),
            pltpu.VMEM((2 * model // 128, rows, 128), jnp.float32),
            pltpu.SemaphoreType.DMA((steps + 1,)),
        ),
    )
    swap = [(i, i + 1) for i in range(1, count - 1, 2)]
    swap += [(j, i) for i, j in swap]
    def exchange(own, bit):
        return lax.ppermute(own, AXES, list(enumerate(partners(bit, count))))

    def pool(own, got, *after):
        return call(pool_kernel, block, vmem(2), own, got, after=after)

    teams = [
        [i for i in range(count) if i >> 6 == part and i & 1 == core]
        for part in range(count >> 6)
        for core in range(2)
    ]
    spread = lax.all_to_all(level_6, AXES, 0, 0, axis_index_groups=teams, tiled=True)
    near_sib = exchange(near, 0)
    own_3 = call(pool_near_kernel, block, vmem(2), level_3, near_sib)
    z_pairs = [[i, i ^ 2] for i in range(count) if not i & 2]
    both_3 = lax.all_gather(own_3, AXES, axis_index_groups=z_pairs, tiled=True)
    other_halo = lax.ppermute(other, AXES, swap)
    mine = call(
        unpack_kernel, bf16(3 * BLOCK // 2, 2 * model), [SMEM, *vmem(1)],
        place, spread.reshape(members, packed, 128),
        scratch=(pltpu.VMEM((members * packed, 128), jnp.float32),),
        after=(both_3, other_halo),
    )
    theirs = exchange(mine, 0)
    own_4 = call(pool_kernel, block, vmem(1), both_3, after=(mine,))
    sib_4 = exchange(own_4, 2)
    own_8 = call(own_8_kernel, block, vmem(2), mine, theirs)
    sib_8 = exchange(own_8, 6)
    own_5 = pool(own_4, sib_4, own_8)
    sib_5 = exchange(own_5, 3)
    own_9 = call(pool_halves_kernel, block, vmem(2), own_8, sib_8, after=(own_5,))
    sib_9 = exchange(own_9, 7)
    q, num, tot = call(
        functools.partial(local_kernel, count),
        (bf16(rows, model), f32(rows, model), f32(rows, model)),
        [SMEM, *vmem(1), in_hbm, *vmem(8)],
        place, tokens, stay(w_qkv), kv, near_sib, other_halo, both_3, sib_4, mine, theirs, sib_8,
        flops=10**9,
        scratch=(
            pltpu.VMEM((rows + 2 * BLOCK, 2 * model), jnp.bfloat16),
            pltpu.VMEM((rows // 2, 2 * model), jnp.bfloat16),
            pltpu.VMEM((model, model), jnp.bfloat16),
            pltpu.SemaphoreType.DMA(()),
        ),
        after=(own_9,),
    )
    own_10 = pool(own_9, sib_9, q, sib_5)
    to = partners(8, count)
    pairs = [[i, to[i]] for i in range(count >> 1)]
    pair = lax.all_gather(own_10, AXES, axis_index_groups=pairs, tiled=True)
    return call(
        final_kernel,
        bf16(rows, model),
        [SMEM, *vmem(6), in_hbm],
        place, q, num, tot, sib_5, sib_9, pair, stay(w_out),
        flops=10**9,
        scratch=(
            pltpu.VMEM((rows, model), jnp.bfloat16),
            pltpu.VMEM((model, model), jnp.bfloat16),
            pltpu.SemaphoreType.DMA(()),
        ),
    )


def solution(mesh):
    return jax.shard_map(
        per_device,
        mesh=mesh,
        in_specs=(P(AXES, None), P(), P()),
        out_specs=P(AXES, None),
        check_vma=False,
    )
```

```python
import functools

import jax
import jax.numpy as jnp
import numpy as np
from jax import lax
from jax.experimental import pallas as pl
from jax.experimental.pallas import tpu as pltpu
from jax.sharding import PartitionSpec as P

HEADS = 8
BLOCK = 64
AXES = ("gx", "gy")
FAR8 = (6, 7, 4, 5, 2, 3, 0, 1)
FAR4 = (3, 2, 1, 0)


def partners(bit, count):
    route = []
    for index in range(count):
        if bit == 3:
            route.append(index & ~14 | FAR8[index >> 1 & 7] << 1)
        elif bit == 6:
            route.append(index & ~112 | FAR8[index >> 4 & 7] << 4)
        elif bit == 8:
            route.append(index & ~384 | FAR4[index >> 7 & 3] << 7)
        else:
            route.append(index ^ 1 << bit)
    return route


def vmem(count):
    return [pl.BlockSpec(memory_space=pltpu.VMEM)] * count


SMEM = pl.BlockSpec(memory_space=pltpu.SMEM)


def call(kernel, outs, in_specs, *args, flops=0, scratch=(), limit=10, after=()):
    count = len(args)

    def body(*refs):
        kernel(*refs[:count], *refs[count + len(after) :])

    return pl.pallas_call(
        body,
        out_shape=outs,
        in_specs=list(in_specs) + [pl.BlockSpec(memory_space=pl.ANY)] * len(after),
        out_specs=jax.tree.map(lambda _: pl.BlockSpec(memory_space=pltpu.VMEM), outs),
        scratch_shapes=list(scratch),
        compiler_params=pltpu.CompilerParams(vmem_limit_bytes=limit * 2**20),
        cost_estimate=pl.CostEstimate(flops=flops, bytes_accessed=2**20, transcendentals=0),
    )(*args, *after)


def pool_matrix(rows):
    r = lax.broadcasted_iota(jnp.int32, (rows, 2 * rows), 0)
    c = lax.broadcasted_iota(jnp.int32, (rows, 2 * rows), 1)
    return jnp.where(c >> 1 == r, 0.5, 0.0).astype(jnp.bfloat16)


def pooled(block):
    return jnp.dot(
        pool_matrix(block.shape[0] // 2), block, preferred_element_type=jnp.float32
    ).astype(jnp.bfloat16)


def project_kernel(
    place, x_hbm, w_hbm, kv_ref, near_ref, other_ref, l3_ref, packed_ref, x_buf, w_buf, part_buf, sems
):
    rows, model = x_buf.shape
    width = w_buf.shape[2]
    steps = w_buf.shape[0]
    x_copy = pltpu.make_async_copy(x_hbm, x_buf, sems.at[steps])
    x_copy.start()
    copies = []
    for step in range(steps):
        columns = pl.ds(model + step * width, width)
        copy = pltpu.make_async_copy(w_hbm.at[:, columns], w_buf.at[step], sems.at[step])
        copy.start()
        copies.append(copy)
    x_copy.wait()
    x = x_buf[...]
    pieces = []
    for step in range(steps):
        copies[step].wait()
        lanes = slice(step * width, (step + 1) * width)
        part = jnp.dot(x, w_buf[step], preferred_element_type=jnp.float32).astype(jnp.bfloat16)
        kv_ref[:, lanes] = part
        wide = part.astype(jnp.float32)
        for at in range(0, width, 128):
            tile = (step * width + at) // 128
            part_buf[tile] = wide[:, at : at + 128]
            size = rows
            while size > 8:
                size //= 2
                even = part_buf[tile, pl.ds(0, size, stride=2), :]
                odd = part_buf[tile, pl.ds(1, size, stride=2), :]
                level = ((even + odd) * 0.5).astype(jnp.bfloat16)
                if size == BLOCK:
                    near_ref[BLOCK:, tile * 128 : (tile + 1) * 128] = level
                if size == BLOCK // 2:
                    l3_ref[:, tile * 128 : (tile + 1) * 128] = level
                part_buf[tile, :size, :] = level.astype(jnp.float32)
            pieces.append(level.astype(jnp.float32))
    packed = pooled(jnp.concatenate(pieces, axis=0).astype(jnp.bfloat16))
    size = packed.shape[0]
    for copy in range(packed_ref.shape[0] // size):
        packed_ref[copy * size : (copy + 1) * size, :] = packed
    core = place[0] & 1
    last = rows - BLOCK
    low = pl.multiple_of(core * last, BLOCK)
    high = pl.multiple_of((1 - core) * last, BLOCK)
    near_ref[:BLOCK, :] = kv_ref[pl.ds(high, BLOCK), :]
    other_ref[...] = kv_ref[pl.ds(low, BLOCK), :]


def unpack_kernel(place, in_ref, out_ref, wide):
    members, rows, _ = in_ref.shape
    wide[...] = in_ref[...].reshape(members * rows, 128).astype(jnp.float32)
    y = (place[0] >> 4) & 3

    def mean(one, two):
        return ((one + two) * 0.5).astype(jnp.bfloat16).astype(jnp.float32)

    for tile in range(rows // 4):
        lanes = slice(tile * 128, (tile + 1) * 128)

        def level_6(start, count):
            return [
                wide[pl.ds(start * rows + tile * 4 + row, count, stride=rows), :]
                for row in range(4)
            ]

        def level_7(start, count):
            r = level_6(start, count)
            return [mean(r[0], r[1]), mean(r[2], r[3])]

        parts = (
            level_6((y ^ 1) * 8, 8)
            + level_7(((y >> 1) ^ 1) * 16, 16)
            + [mean(*level_7(0, members))]
        )
        out_ref[:, lanes] = jnp.concatenate(parts, axis=0).astype(jnp.bfloat16)


def own_8_kernel(mine_ref, sib_ref, out_ref):
    half = BLOCK // 2
    out_ref[:half, :] = mine_ref[BLOCK:, :]
    out_ref[half:, :] = sib_ref[BLOCK:, :]


def pool_near_kernel(mine_ref, sib_ref, out_ref):
    out_ref[: BLOCK // 2, :] = mine_ref[...]
    out_ref[BLOCK // 2 :, :] = pooled(sib_ref[BLOCK:, :])


def pool_halves_kernel(own_ref, sib_ref, out_ref):
    half = BLOCK // 2
    for num, ref in enumerate((own_ref, sib_ref)):
        block = ref[...].astype(jnp.float32)
        out_ref[num * half : (num + 1) * half, :] = (
            (block[:half] + block[half:]) * 0.5
        ).astype(jnp.bfloat16)


def pool_kernel(*refs):
    ins, out_ref = refs[:-1], refs[-1]
    half = BLOCK // len(ins)
    for num, ref in enumerate(ins):
        out_ref[num * half : (num + 1) * half, :] = pooled(ref[...])


def attend_pair(q, keys, values, ones):
    rows = q.shape[0]
    lane = lax.broadcasted_iota(jnp.int32, q.shape, 1)
    first = lane < 64
    zero = jnp.zeros_like(q)
    both = jnp.concatenate([jnp.where(first, q, zero), jnp.where(first, zero, q)], axis=0)
    scores = lax.dot_general(
        both, keys, (((1,), (1,)), ((), ())), preferred_element_type=jnp.float32
    )
    weights = jnp.exp(scores).astype(jnp.bfloat16)
    sums = jnp.dot(
        weights, jnp.concatenate([values, ones], axis=1), preferred_element_type=jnp.float32
    )
    num = jnp.where(first, sums[:rows, :128], sums[rows:, :128])
    tot = jnp.where(first, sums[:rows, 128:], sums[rows:, 128:])
    return num, tot


def local_kernel(
    count, place, x_ref, w_hbm, kv_ref, near_ref, other_ref, both_3_ref, sib_4_ref,
    mine_ref, theirs_ref, sib_8_ref, q_ref, num_ref, tot_ref, pad, l1, w_ref, sem
):
    rows, model = x_ref.shape
    blocks = rows // BLOCK
    copy = pltpu.make_async_copy(w_hbm.at[:, pl.ds(0, model)], w_ref, sem)
    copy.start()
    core = place[0] & 1
    sib_halo = near_ref[:BLOCK, :]
    other = other_ref[...]
    is_first = core == 0
    pad[:BLOCK, :] = jnp.where(is_first, other, sib_halo)
    pad[BLOCK : BLOCK + rows, :] = kv_ref[...]
    pad[BLOCK + rows :, :] = jnp.where(is_first, sib_halo, other)
    l1[...] = pooled(kv_ref[...])
    copy.wait()
    q_ref[...] = (
        jnp.dot(x_ref[...], w_ref[...], preferred_element_type=jnp.float32)
        .astype(jnp.bfloat16) * jnp.bfloat16(0.125)
    )
    key_row = lax.broadcasted_iota(jnp.int32, (4 * BLOCK, 128), 0)
    for i in range(blocks):
        ones = jnp.ones((4 * BLOCK, 128), jnp.float32)
        if i == 0:
            ones = jnp.where((key_row < BLOCK) & (place[0] == 0), 0.0, ones)
        if i == blocks - 1:
            ones = jnp.where((key_row >= 2 * BLOCK) & (key_row < 3 * BLOCK) & (place[0] == count - 1), 0.0, ones)
        ones = ones.astype(jnp.bfloat16)
        sib = (i >> 1) ^ 1
        here = slice(i * BLOCK, (i + 1) * BLOCK)
        for lanes in range(0, model, 128):
            kl = slice(lanes, lanes + 128)
            vl = slice(model + lanes, model + lanes + 128)
            keys = jnp.concatenate(
                [pad[i * BLOCK : (i + 3) * BLOCK, kl], l1[sib * BLOCK : (sib + 1) * BLOCK, kl]], axis=0
            )
            values = jnp.concatenate(
                [pad[i * BLOCK : (i + 3) * BLOCK, vl], l1[sib * BLOCK : (sib + 1) * BLOCK, vl]], axis=0
            )
            num, tot = attend_pair(q_ref[here, kl], keys, values, ones)
            num_ref[here, kl] = num
            tot_ref[here, kl] = tot
    start = pl.multiple_of((1 - ((place[0] >> 1) & 1)) * BLOCK, BLOCK)
    sib_3 = both_3_ref[pl.ds(start, BLOCK), :]
    far = far_blocks((near_ref, sib_3, sib_4_ref, mine_ref, theirs_ref, sib_8_ref))
    for lanes in range(0, model, 128):
        kl = slice(lanes, lanes + 128)
        num, tot = far_sums(far, q_ref[:, kl], lanes, model)
        num_ref[:, kl] += num
        tot_ref[:, kl] += tot


def far_blocks(refs):
    blocks = []
    for ref in refs:
        if ref.shape[0] == 2 * BLOCK:
            blocks.append(ref[BLOCK:, :])
        else:
            blocks.append(ref[:BLOCK, :])
    return jnp.concatenate(blocks, axis=0)


def far_sums(far, q, lanes, model):
    keys = far[:, lanes : lanes + 128]
    values = far[:, model + lanes : model + lanes + 128]
    return attend_pair(q, keys, values, jnp.ones(values.shape, jnp.bfloat16))


def final_kernel(
    q_ref, num_in, tot_in, sib_5_ref, sib_9_ref, sib_10_ref, w_hbm, out_ref, att, w_ref, sem
):
    copy = pltpu.make_async_copy(w_hbm, w_ref, sem)
    copy.start()
    model = q_ref.shape[1]
    far = far_blocks((sib_5_ref, sib_9_ref, sib_10_ref))
    for lanes in range(0, model, 128):
        at = slice(lanes, lanes + 128)
        num, tot = far_sums(far, q_ref[:, at], lanes, model)
        att[:, at] = ((num_in[:, at] + num) / (tot_in[:, at] + tot)).astype(jnp.bfloat16)
    copy.wait()
    out_ref[...] = jnp.dot(att[...], w_ref[...], preferred_element_type=jnp.float32).astype(
        jnp.bfloat16
    )


def per_device(tokens, w_qkv, w_out):
    rows, model = tokens.shape
    index = lax.axis_index(AXES)
    count = lax.axis_size(AXES)
    place = index.astype(jnp.int32).reshape(1)
    bf16 = lambda *shape: jax.ShapeDtypeStruct(shape, jnp.bfloat16)
    f32 = lambda *shape: jax.ShapeDtypeStruct(shape, jnp.float32)
    in_hbm = pl.BlockSpec(memory_space=pl.ANY)
    stay = lambda array: pltpu.with_memory_space_constraint(array, pltpu.HBM)
    steps = 2
    width = 2 * model // steps
    members = 32
    packed = 4 * 2 * model // 128
    block = bf16(BLOCK, 2 * model)
    kv, near, other, level_3, level_6 = call(
        project_kernel,
        (
            bf16(rows, 2 * model), bf16(2 * BLOCK, 2 * model), block,
            bf16(BLOCK // 2, 2 * model), bf16(members * packed, 128),
        ),
        [SMEM, in_hbm, in_hbm],
        place, stay(tokens), stay(w_qkv),
        flops=4 * rows * model * model,
        scratch=(
            pltpu.VMEM((rows, model), jnp.bfloat16),
            pltpu.VMEM((steps, model, width), jnp.bfloat16),
            pltpu.VMEM((2 * model // 128, rows, 128), jnp.float32),
            pltpu.SemaphoreType.DMA((steps + 1,)),
        ),
    )
    swap = [(i, i + 1) for i in range(1, count - 1, 2)]
    swap += [(j, i) for i, j in swap]
    def exchange(own, bit):
        return lax.ppermute(own, AXES, list(enumerate(partners(bit, count))))

    def pool(own, got, *after):
        return call(pool_kernel, block, vmem(2), own, got, after=after)

    teams = [
        [i for i in range(count) if i >> 6 == part and i & 1 == core]
        for part in range(count >> 6)
        for core in range(2)
    ]
    spread = lax.all_to_all(level_6, AXES, 0, 0, axis_index_groups=teams, tiled=True)
    near_sib = exchange(near, 0)
    own_3 = call(pool_near_kernel, block, vmem(2), level_3, near_sib)
    z_pairs = [[i, i ^ 2] for i in range(count) if not i & 2]
    both_3 = lax.all_gather(own_3, AXES, axis_index_groups=z_pairs, tiled=True)
    mine = call(
        unpack_kernel, bf16(3 * BLOCK // 2, 2 * model), [SMEM, *vmem(1)],
        place, spread.reshape(members, packed, 128),
        scratch=(pltpu.VMEM((members * packed, 128), jnp.float32),),
        after=(both_3,),
    )
    theirs = exchange(mine, 0)
    own_4 = call(pool_kernel, block, vmem(1), both_3, after=(mine,))
    sib_4 = exchange(own_4, 2)
    own_8 = call(own_8_kernel, block, vmem(2), mine, theirs)
    sib_8 = exchange(own_8, 6)
    own_5 = pool(own_4, sib_4, own_8)
    other, _ = lax.optimization_barrier((other, own_5))
    other_halo = lax.ppermute(other, AXES, swap)
    sib_5 = exchange(own_5, 3)
    own_9 = call(pool_halves_kernel, block, vmem(2), own_8, sib_8, after=(own_5,))
    sib_9 = exchange(own_9, 7)
    own_10 = pool(own_9, sib_9, other_halo)
    sib_10 = exchange(own_10, 8)
    q, num, tot = call(
        functools.partial(local_kernel, count),
        (bf16(rows, model), f32(rows, model), f32(rows, model)),
        [SMEM, *vmem(1), in_hbm, *vmem(8)],
        place, tokens, stay(w_qkv), kv, near_sib, other_halo, both_3, sib_4, mine, theirs, sib_8,
        flops=10**9,
        scratch=(
            pltpu.VMEM((rows + 2 * BLOCK, 2 * model), jnp.bfloat16),
            pltpu.VMEM((rows // 2, 2 * model), jnp.bfloat16),
            pltpu.VMEM((model, model), jnp.bfloat16),
            pltpu.SemaphoreType.DMA(()),
        ),
        after=(own_10,),
    )
    return call(
        final_kernel,
        bf16(rows, model),
        [*vmem(6), in_hbm],
        q, num, tot, sib_5, sib_9, sib_10, stay(w_out),
        flops=10**9,
        scratch=(
            pltpu.VMEM((rows, model), jnp.bfloat16),
            pltpu.VMEM((model, model), jnp.bfloat16),
            pltpu.SemaphoreType.DMA(()),
        ),
    )


def solution(mesh):
    return jax.shard_map(
        per_device,
        mesh=mesh,
        in_specs=(P(AXES, None), P(), P()),
        out_specs=P(AXES, None),
        check_vma=False,
    )
```

```python
import functools

import jax
import jax.numpy as jnp
import numpy as np
from jax import lax
from jax.experimental import pallas as pl
from jax.experimental.pallas import tpu as pltpu
from jax.sharding import PartitionSpec as P

HEADS = 8
BLOCK = 64
AXES = ("gx", "gy")
FAR8 = (6, 7, 4, 5, 2, 3, 0, 1)
FAR4 = (3, 2, 1, 0)


def partners(bit, count):
    route = []
    for index in range(count):
        if bit == 3:
            route.append(index & ~14 | FAR8[index >> 1 & 7] << 1)
        elif bit == 6:
            route.append(index & ~112 | FAR8[index >> 4 & 7] << 4)
        elif bit == 8:
            route.append(index & ~384 | FAR4[index >> 7 & 3] << 7)
        else:
            route.append(index ^ 1 << bit)
    return route


def vmem(count):
    return [pl.BlockSpec(memory_space=pltpu.VMEM)] * count


SMEM = pl.BlockSpec(memory_space=pltpu.SMEM)


def call(kernel, outs, in_specs, *args, flops=0, scratch=(), limit=10, after=()):
    count = len(args)

    def body(*refs):
        kernel(*refs[:count], *refs[count + len(after) :])

    return pl.pallas_call(
        body,
        out_shape=outs,
        in_specs=list(in_specs) + [pl.BlockSpec(memory_space=pl.ANY)] * len(after),
        out_specs=jax.tree.map(lambda _: pl.BlockSpec(memory_space=pltpu.VMEM), outs),
        scratch_shapes=list(scratch),
        compiler_params=pltpu.CompilerParams(vmem_limit_bytes=limit * 2**20),
        cost_estimate=pl.CostEstimate(flops=flops, bytes_accessed=2**20, transcendentals=0),
    )(*args, *after)


def pool_matrix(rows):
    r = lax.broadcasted_iota(jnp.int32, (rows, 2 * rows), 0)
    c = lax.broadcasted_iota(jnp.int32, (rows, 2 * rows), 1)
    return jnp.where(c >> 1 == r, 0.5, 0.0).astype(jnp.bfloat16)


def pooled(block):
    return jnp.dot(
        pool_matrix(block.shape[0] // 2), block, preferred_element_type=jnp.float32
    ).astype(jnp.bfloat16)


def project_kernel(
    place, x_hbm, w_hbm, kv_ref, near_ref, other_ref, l3_ref, packed_ref, x_buf, w_buf, part_buf, sems
):
    rows, model = x_buf.shape
    width = w_buf.shape[2]
    steps = w_buf.shape[0]
    x_copy = pltpu.make_async_copy(x_hbm, x_buf, sems.at[steps])
    x_copy.start()
    copies = []
    for step in range(steps):
        columns = pl.ds(model + step * width, width)
        copy = pltpu.make_async_copy(w_hbm.at[:, columns], w_buf.at[step], sems.at[step])
        copy.start()
        copies.append(copy)
    x_copy.wait()
    x = x_buf[...]
    pieces = []
    for step in range(steps):
        copies[step].wait()
        lanes = slice(step * width, (step + 1) * width)
        part = jnp.dot(x, w_buf[step], preferred_element_type=jnp.float32).astype(jnp.bfloat16)
        kv_ref[:, lanes] = part
        wide = part.astype(jnp.float32)
        for at in range(0, width, 128):
            tile = (step * width + at) // 128
            part_buf[tile] = wide[:, at : at + 128]
            size = rows
            while size > 8:
                size //= 2
                even = part_buf[tile, pl.ds(0, size, stride=2), :]
                odd = part_buf[tile, pl.ds(1, size, stride=2), :]
                level = ((even + odd) * 0.5).astype(jnp.bfloat16)
                if size == BLOCK:
                    near_ref[BLOCK:, tile * 128 : (tile + 1) * 128] = level
                if size == BLOCK // 2:
                    l3_ref[:, tile * 128 : (tile + 1) * 128] = level
                part_buf[tile, :size, :] = level.astype(jnp.float32)
            pieces.append(level.astype(jnp.float32))
    packed = pooled(jnp.concatenate(pieces, axis=0).astype(jnp.bfloat16))
    size = packed.shape[0]
    for copy in range(packed_ref.shape[0] // size):
        packed_ref[copy * size : (copy + 1) * size, :] = packed
    core = place[0] & 1
    last = rows - BLOCK
    low = pl.multiple_of(core * last, BLOCK)
    high = pl.multiple_of((1 - core) * last, BLOCK)
    near_ref[:BLOCK, :] = kv_ref[pl.ds(high, BLOCK), :]
    other_ref[...] = kv_ref[pl.ds(low, BLOCK), :]


def unpack_kernel(place, in_ref, out_ref, wide):
    members, rows, _ = in_ref.shape
    wide[...] = in_ref[...].reshape(members * rows, 128).astype(jnp.float32)
    y = (place[0] >> 4) & 3

    def mean(one, two):
        return ((one + two) * 0.5).astype(jnp.bfloat16).astype(jnp.float32)

    for tile in range(rows // 4):
        lanes = slice(tile * 128, (tile + 1) * 128)

        def level_6(start, count):
            return [
                wide[pl.ds(start * rows + tile * 4 + row, count, stride=rows), :]
                for row in range(4)
            ]

        def level_7(start, count):
            r = level_6(start, count)
            return [mean(r[0], r[1]), mean(r[2], r[3])]

        parts = (
            level_6((y ^ 1) * 8, 8)
            + level_7(((y >> 1) ^ 1) * 16, 16)
            + [mean(*level_7(0, members))]
        )
        out_ref[:, lanes] = jnp.concatenate(parts, axis=0).astype(jnp.bfloat16)


def own_8_kernel(mine_ref, sib_ref, out_ref):
    half = BLOCK // 2
    out_ref[:half, :] = mine_ref[BLOCK:, :]
    out_ref[half:, :] = sib_ref[BLOCK:, :]


def pool_near_kernel(mine_ref, sib_ref, out_ref):
    out_ref[: BLOCK // 2, :] = mine_ref[...]
    out_ref[BLOCK // 2 :, :] = pooled(sib_ref[BLOCK:, :])


def pool_halves_kernel(own_ref, sib_ref, out_ref):
    half = BLOCK // 2
    for num, ref in enumerate((own_ref, sib_ref)):
        block = ref[...].astype(jnp.float32)
        out_ref[num * half : (num + 1) * half, :] = (
            (block[:half] + block[half:]) * 0.5
        ).astype(jnp.bfloat16)


def pool_kernel(*refs):
    ins, out_ref = refs[:-1], refs[-1]
    half = BLOCK // len(ins)
    for num, ref in enumerate(ins):
        out_ref[num * half : (num + 1) * half, :] = pooled(ref[...])


def attend_pair(q, keys, values, ones):
    rows = q.shape[0]
    lane = lax.broadcasted_iota(jnp.int32, q.shape, 1)
    first = lane < 64
    zero = jnp.zeros_like(q)
    both = jnp.concatenate([jnp.where(first, q, zero), jnp.where(first, zero, q)], axis=0)
    scores = lax.dot_general(
        both, keys, (((1,), (1,)), ((), ())), preferred_element_type=jnp.float32
    )
    weights = jnp.exp(scores).astype(jnp.bfloat16)
    sums = jnp.dot(
        weights, jnp.concatenate([values, ones], axis=1), preferred_element_type=jnp.float32
    )
    num = jnp.where(first, sums[:rows, :128], sums[rows:, :128])
    tot = jnp.where(first, sums[:rows, 128:], sums[rows:, 128:])
    return num, tot


def local_kernel(
    count, place, x_ref, w_hbm, kv_ref, near_ref, other_ref, both_3_ref, sib_4_ref,
    mine_ref, theirs_ref, sib_8_ref, q_ref, num_ref, tot_ref, pad, l1, w_ref, sem
):
    rows, model = x_ref.shape
    blocks = rows // BLOCK
    copy = pltpu.make_async_copy(w_hbm.at[:, pl.ds(0, model)], w_ref, sem)
    copy.start()
    core = place[0] & 1
    sib_halo = near_ref[:BLOCK, :]
    other = other_ref[...]
    is_first = core == 0
    pad[:BLOCK, :] = jnp.where(is_first, other, sib_halo)
    pad[BLOCK : BLOCK + rows, :] = kv_ref[...]
    pad[BLOCK + rows :, :] = jnp.where(is_first, sib_halo, other)
    l1[...] = pooled(kv_ref[...])
    copy.wait()
    q_ref[...] = (
        jnp.dot(x_ref[...], w_ref[...], preferred_element_type=jnp.float32)
        .astype(jnp.bfloat16) * jnp.bfloat16(0.125)
    )
    key_row = lax.broadcasted_iota(jnp.int32, (4 * BLOCK, 128), 0)
    for i in range(blocks):
        ones = jnp.ones((4 * BLOCK, 128), jnp.float32)
        if i == 0:
            ones = jnp.where((key_row < BLOCK) & (place[0] == 0), 0.0, ones)
        if i == blocks - 1:
            ones = jnp.where((key_row >= 2 * BLOCK) & (key_row < 3 * BLOCK) & (place[0] == count - 1), 0.0, ones)
        ones = ones.astype(jnp.bfloat16)
        sib = (i >> 1) ^ 1
        here = slice(i * BLOCK, (i + 1) * BLOCK)
        for lanes in range(0, model, 128):
            kl = slice(lanes, lanes + 128)
            vl = slice(model + lanes, model + lanes + 128)
            keys = jnp.concatenate(
                [pad[i * BLOCK : (i + 3) * BLOCK, kl], l1[sib * BLOCK : (sib + 1) * BLOCK, kl]], axis=0
            )
            values = jnp.concatenate(
                [pad[i * BLOCK : (i + 3) * BLOCK, vl], l1[sib * BLOCK : (sib + 1) * BLOCK, vl]], axis=0
            )
            num, tot = attend_pair(q_ref[here, kl], keys, values, ones)
            num_ref[here, kl] = num
            tot_ref[here, kl] = tot
    start = pl.multiple_of((1 - ((place[0] >> 1) & 1)) * BLOCK, BLOCK)
    sib_3 = both_3_ref[pl.ds(start, BLOCK), :]
    far = far_blocks((near_ref, sib_3, sib_4_ref, mine_ref, theirs_ref, sib_8_ref))
    for lanes in range(0, model, 128):
        kl = slice(lanes, lanes + 128)
        num, tot = far_sums(far, q_ref[:, kl], lanes, model)
        num_ref[:, kl] += num
        tot_ref[:, kl] += tot


def far_blocks(refs):
    blocks = []
    for ref in refs:
        if ref.shape[0] == 2 * BLOCK:
            blocks.append(ref[BLOCK:, :])
        else:
            blocks.append(ref[:BLOCK, :])
    return jnp.concatenate(blocks, axis=0)


def far_sums(far, q, lanes, model):
    keys = far[:, lanes : lanes + 128]
    values = far[:, model + lanes : model + lanes + 128]
    return attend_pair(q, keys, values, jnp.ones(values.shape, jnp.bfloat16))


def final_kernel(
    q_ref, num_in, tot_in, sib_5_ref, sib_9_ref, sib_10_ref, w_hbm, out_ref, att, w_ref, sem
):
    copy = pltpu.make_async_copy(w_hbm, w_ref, sem)
    copy.start()
    model = q_ref.shape[1]
    far = far_blocks((sib_5_ref, sib_9_ref, sib_10_ref))
    for lanes in range(0, model, 128):
        at = slice(lanes, lanes + 128)
        num, tot = far_sums(far, q_ref[:, at], lanes, model)
        att[:, at] = ((num_in[:, at] + num) / (tot_in[:, at] + tot)).astype(jnp.bfloat16)
    copy.wait()
    out_ref[...] = jnp.dot(att[...], w_ref[...], preferred_element_type=jnp.float32).astype(
        jnp.bfloat16
    )


def per_device(tokens, w_qkv, w_out):
    rows, model = tokens.shape
    index = lax.axis_index(AXES)
    count = lax.axis_size(AXES)
    place = index.astype(jnp.int32).reshape(1)
    bf16 = lambda *shape: jax.ShapeDtypeStruct(shape, jnp.bfloat16)
    f32 = lambda *shape: jax.ShapeDtypeStruct(shape, jnp.float32)
    in_hbm = pl.BlockSpec(memory_space=pl.ANY)
    stay = lambda array: pltpu.with_memory_space_constraint(array, pltpu.HBM)
    steps = 2
    width = 2 * model // steps
    members = 32
    packed = 4 * 2 * model // 128
    block = bf16(BLOCK, 2 * model)
    kv, near, other, level_3, level_6 = call(
        project_kernel,
        (
            bf16(rows, 2 * model), bf16(2 * BLOCK, 2 * model), block,
            bf16(BLOCK // 2, 2 * model), bf16(members * packed, 128),
        ),
        [SMEM, in_hbm, in_hbm],
        place, stay(tokens), stay(w_qkv),
        flops=4 * rows * model * model,
        scratch=(
            pltpu.VMEM((rows, model), jnp.bfloat16),
            pltpu.VMEM((steps, model, width), jnp.bfloat16),
            pltpu.VMEM((2 * model // 128, rows, 128), jnp.float32),
            pltpu.SemaphoreType.DMA((steps + 1,)),
        ),
    )
    swap = [(i, i + 1) for i in range(1, count - 1, 2)]
    swap += [(j, i) for i, j in swap]
    def exchange(own, bit):
        return lax.ppermute(own, AXES, list(enumerate(partners(bit, count))))

    def pool(own, got, *after):
        return call(pool_kernel, block, vmem(2), own, got, after=after)

    teams = [
        [i for i in range(count) if i >> 6 == part and i & 1 == core]
        for part in range(count >> 6)
        for core in range(2)
    ]
    spread = lax.all_to_all(level_6, AXES, 0, 0, axis_index_groups=teams, tiled=True)
    near_sib = exchange(near, 0)
    own_3 = call(pool_near_kernel, block, vmem(2), level_3, near_sib)
    z_pairs = [[i, i ^ 2] for i in range(count) if not i & 2]
    both_3 = lax.all_gather(own_3, AXES, axis_index_groups=z_pairs, tiled=True)
    other_halo = lax.ppermute(other, AXES, swap)
    mine = call(
        unpack_kernel, bf16(3 * BLOCK // 2, 2 * model), [SMEM, *vmem(1)],
        place, spread.reshape(members, packed, 128),
        scratch=(pltpu.VMEM((members * packed, 128), jnp.float32),),
        after=(both_3, other_halo),
    )
    theirs = exchange(mine, 0)
    own_4 = call(pool_kernel, block, vmem(1), both_3, after=(mine,))
    sib_4 = exchange(own_4, 2)
    own_8 = call(own_8_kernel, block, vmem(2), mine, theirs)
    sib_8 = exchange(own_8, 6)
    own_5 = pool(own_4, sib_4, own_8)
    sib_5 = exchange(own_5, 3)
    own_9 = call(pool_halves_kernel, block, vmem(2), own_8, sib_8, after=(own_5,))
    sib_9 = exchange(own_9, 7)
    own_10 = pool(own_9, sib_9)
    sib_10 = exchange(own_10, 8)
    q, num, tot = call(
        functools.partial(local_kernel, count),
        (bf16(rows, model), f32(rows, model), f32(rows, model)),
        [SMEM, *vmem(1), in_hbm, *vmem(8)],
        place, tokens, stay(w_qkv), kv, near_sib, other_halo, both_3, sib_4, mine, theirs, sib_8,
        flops=10**9,
        scratch=(
            pltpu.VMEM((rows + 2 * BLOCK, 2 * model), jnp.bfloat16),
            pltpu.VMEM((rows // 2, 2 * model), jnp.bfloat16),
            pltpu.VMEM((model, model), jnp.bfloat16),
            pltpu.SemaphoreType.DMA(()),
        ),
        after=(own_10,),
    )
    return call(
        final_kernel,
        bf16(rows, model),
        [*vmem(6), in_hbm],
        q, num, tot, sib_5, sib_9, sib_10, stay(w_out),
        flops=10**9,
        scratch=(
            pltpu.VMEM((rows, model), jnp.bfloat16),
            pltpu.VMEM((model, model), jnp.bfloat16),
            pltpu.SemaphoreType.DMA(()),
        ),
    )


def solution(mesh):
    return jax.shard_map(
        per_device,
        mesh=mesh,
        in_specs=(P(AXES, None), P(), P()),
        out_specs=P(AXES, None),
        check_vma=False,
    )
```

```python
import functools

import jax
import jax.numpy as jnp
import numpy as np
from jax import lax
from jax.experimental import pallas as pl
from jax.experimental.pallas import tpu as pltpu
from jax.sharding import PartitionSpec as P

HEADS = 8
BLOCK = 64
AXES = ("gx", "gy")
FAR8 = (6, 7, 4, 5, 2, 3, 0, 1)
FAR4 = (3, 2, 1, 0)


def partners(bit, count):
    route = []
    for index in range(count):
        if bit == 3:
            route.append(index & ~14 | FAR8[index >> 1 & 7] << 1)
        elif bit == 6:
            route.append(index & ~112 | FAR8[index >> 4 & 7] << 4)
        elif bit == 8:
            route.append(index & ~384 | FAR4[index >> 7 & 3] << 7)
        else:
            route.append(index ^ 1 << bit)
    return route


def vmem(count):
    return [pl.BlockSpec(memory_space=pltpu.VMEM)] * count


SMEM = pl.BlockSpec(memory_space=pltpu.SMEM)


def call(kernel, outs, in_specs, *args, flops=0, scratch=(), limit=10, after=()):
    count = len(args)

    def body(*refs):
        kernel(*refs[:count], *refs[count + len(after) :])

    return pl.pallas_call(
        body,
        out_shape=outs,
        in_specs=list(in_specs) + [pl.BlockSpec(memory_space=pl.ANY)] * len(after),
        out_specs=jax.tree.map(lambda _: pl.BlockSpec(memory_space=pltpu.VMEM), outs),
        scratch_shapes=list(scratch),
        compiler_params=pltpu.CompilerParams(vmem_limit_bytes=limit * 2**20),
        cost_estimate=pl.CostEstimate(flops=flops, bytes_accessed=2**20, transcendentals=0),
    )(*args, *after)


def pool_matrix(rows):
    r = lax.broadcasted_iota(jnp.int32, (rows, 2 * rows), 0)
    c = lax.broadcasted_iota(jnp.int32, (rows, 2 * rows), 1)
    return jnp.where(c >> 1 == r, 0.5, 0.0).astype(jnp.bfloat16)


def pooled(block):
    return jnp.dot(
        pool_matrix(block.shape[0] // 2), block, preferred_element_type=jnp.float32
    ).astype(jnp.bfloat16)


def project_kernel(
    place, x_hbm, w_hbm, kv_ref, near_ref, other_ref, l3_ref, packed_ref, x_buf, w_buf, part_buf, sems
):
    rows, model = x_buf.shape
    width = w_buf.shape[2]
    steps = w_buf.shape[0]
    x_copy = pltpu.make_async_copy(x_hbm, x_buf, sems.at[steps])
    x_copy.start()
    copies = []
    for step in range(steps):
        columns = pl.ds(model + step * width, width)
        copy = pltpu.make_async_copy(w_hbm.at[:, columns], w_buf.at[step], sems.at[step])
        copy.start()
        copies.append(copy)
    x_copy.wait()
    x = x_buf[...]
    pieces = []
    for step in range(steps):
        copies[step].wait()
        lanes = slice(step * width, (step + 1) * width)
        part = jnp.dot(x, w_buf[step], preferred_element_type=jnp.float32).astype(jnp.bfloat16)
        kv_ref[:, lanes] = part
        wide = part.astype(jnp.float32)
        for at in range(0, width, 128):
            tile = (step * width + at) // 128
            part_buf[tile] = wide[:, at : at + 128]
            size = rows
            while size > 8:
                size //= 2
                even = part_buf[tile, pl.ds(0, size, stride=2), :]
                odd = part_buf[tile, pl.ds(1, size, stride=2), :]
                level = ((even + odd) * 0.5).astype(jnp.bfloat16)
                if size == BLOCK:
                    near_ref[BLOCK:, tile * 128 : (tile + 1) * 128] = level
                if size == BLOCK // 2:
                    l3_ref[:, tile * 128 : (tile + 1) * 128] = level
                part_buf[tile, :size, :] = level.astype(jnp.float32)
            pieces.append(level.astype(jnp.float32))
    packed = pooled(jnp.concatenate(pieces, axis=0).astype(jnp.bfloat16))
    size = packed.shape[0]
    for copy in range(packed_ref.shape[0] // size):
        packed_ref[copy * size : (copy + 1) * size, :] = packed
    core = place[0] & 1
    last = rows - BLOCK
    low = pl.multiple_of(core * last, BLOCK)
    high = pl.multiple_of((1 - core) * last, BLOCK)
    near_ref[:BLOCK, :] = kv_ref[pl.ds(high, BLOCK), :]
    other_ref[...] = kv_ref[pl.ds(low, BLOCK), :]


def unpack_kernel(place, in_ref, out_ref, wide):
    members, rows, _ = in_ref.shape
    wide[...] = in_ref[...].reshape(members * rows, 128).astype(jnp.float32)
    y = (place[0] >> 4) & 3

    def mean(one, two):
        return ((one + two) * 0.5).astype(jnp.bfloat16).astype(jnp.float32)

    for tile in range(rows // 4):
        lanes = slice(tile * 128, (tile + 1) * 128)

        def level_6(start, count):
            return [
                wide[pl.ds(start * rows + tile * 4 + row, count, stride=rows), :]
                for row in range(4)
            ]

        def level_7(start, count):
            r = level_6(start, count)
            return [mean(r[0], r[1]), mean(r[2], r[3])]

        parts = (
            level_6((y ^ 1) * 8, 8)
            + level_7(((y >> 1) ^ 1) * 16, 16)
            + [mean(*level_7(0, members))]
        )
        out_ref[:, lanes] = jnp.concatenate(parts, axis=0).astype(jnp.bfloat16)


def own_8_kernel(mine_ref, sib_ref, out_ref):
    half = BLOCK // 2
    out_ref[:half, :] = mine_ref[BLOCK:, :]
    out_ref[half:, :] = sib_ref[BLOCK:, :]


def pool_near_kernel(mine_ref, sib_ref, out_ref):
    out_ref[: BLOCK // 2, :] = mine_ref[...]
    out_ref[BLOCK // 2 :, :] = pooled(sib_ref[BLOCK:, :])


def pool_halves_kernel(own_ref, sib_ref, out_ref):
    half = BLOCK // 2
    for num, ref in enumerate((own_ref, sib_ref)):
        block = ref[...].astype(jnp.float32)
        out_ref[num * half : (num + 1) * half, :] = (
            (block[:half] + block[half:]) * 0.5
        ).astype(jnp.bfloat16)


def pool_kernel(*refs):
    ins, out_ref = refs[:-1], refs[-1]
    half = BLOCK // len(ins)
    for num, ref in enumerate(ins):
        out_ref[num * half : (num + 1) * half, :] = pooled(ref[...])


def attend_pair(q, keys, values, ones):
    rows = q.shape[0]
    lane = lax.broadcasted_iota(jnp.int32, q.shape, 1)
    first = lane < 64
    zero = jnp.zeros_like(q)
    both = jnp.concatenate([jnp.where(first, q, zero), jnp.where(first, zero, q)], axis=0)
    scores = lax.dot_general(
        both, keys, (((1,), (1,)), ((), ())), preferred_element_type=jnp.float32
    )
    weights = jnp.exp(scores).astype(jnp.bfloat16)
    sums = jnp.dot(
        weights, jnp.concatenate([values, ones], axis=1), preferred_element_type=jnp.float32
    )
    num = jnp.where(first, sums[:rows, :128], sums[rows:, :128])
    tot = jnp.where(first, sums[:rows, 128:], sums[rows:, 128:])
    return num, tot


def local_kernel(
    count, place, x_ref, w_hbm, kv_ref, near_ref, other_ref, both_3_ref,
    mine_ref, theirs_ref, q_ref, num_ref, tot_ref, pad, l1, w_ref, sem
):
    rows, model = x_ref.shape
    blocks = rows // BLOCK
    copy = pltpu.make_async_copy(w_hbm.at[:, pl.ds(0, model)], w_ref, sem)
    copy.start()
    core = place[0] & 1
    sib_halo = near_ref[:BLOCK, :]
    other = other_ref[...]
    is_first = core == 0
    pad[:BLOCK, :] = jnp.where(is_first, other, sib_halo)
    pad[BLOCK : BLOCK + rows, :] = kv_ref[...]
    pad[BLOCK + rows :, :] = jnp.where(is_first, sib_halo, other)
    l1[...] = pooled(kv_ref[...])
    copy.wait()
    q_ref[...] = (
        jnp.dot(x_ref[...], w_ref[...], preferred_element_type=jnp.float32)
        .astype(jnp.bfloat16) * jnp.bfloat16(0.125)
    )
    key_row = lax.broadcasted_iota(jnp.int32, (4 * BLOCK, 128), 0)
    for i in range(blocks):
        ones = jnp.ones((4 * BLOCK, 128), jnp.float32)
        if i == 0:
            ones = jnp.where((key_row < BLOCK) & (place[0] == 0), 0.0, ones)
        if i == blocks - 1:
            ones = jnp.where((key_row >= 2 * BLOCK) & (key_row < 3 * BLOCK) & (place[0] == count - 1), 0.0, ones)
        ones = ones.astype(jnp.bfloat16)
        sib = (i >> 1) ^ 1
        here = slice(i * BLOCK, (i + 1) * BLOCK)
        for lanes in range(0, model, 128):
            kl = slice(lanes, lanes + 128)
            vl = slice(model + lanes, model + lanes + 128)
            keys = jnp.concatenate(
                [pad[i * BLOCK : (i + 3) * BLOCK, kl], l1[sib * BLOCK : (sib + 1) * BLOCK, kl]], axis=0
            )
            values = jnp.concatenate(
                [pad[i * BLOCK : (i + 3) * BLOCK, vl], l1[sib * BLOCK : (sib + 1) * BLOCK, vl]], axis=0
            )
            num, tot = attend_pair(q_ref[here, kl], keys, values, ones)
            num_ref[here, kl] = num
            tot_ref[here, kl] = tot
    start = pl.multiple_of((1 - ((place[0] >> 1) & 1)) * BLOCK, BLOCK)
    sib_3 = both_3_ref[pl.ds(start, BLOCK), :]
    far = far_blocks((near_ref, sib_3, mine_ref, theirs_ref))
    for lanes in range(0, model, 128):
        kl = slice(lanes, lanes + 128)
        num, tot = far_sums(far, q_ref[:, kl], lanes, model)
        num_ref[:, kl] += num
        tot_ref[:, kl] += tot


def far_blocks(refs):
    blocks = []
    for ref in refs:
        if ref.shape[0] == 2 * BLOCK:
            blocks.append(ref[BLOCK:, :])
        else:
            blocks.append(ref[:BLOCK, :])
    return jnp.concatenate(blocks, axis=0)


def far_sums(far, q, lanes, model):
    keys = far[:, lanes : lanes + 128]
    values = far[:, model + lanes : model + lanes + 128]
    return attend_pair(q, keys, values, jnp.ones(values.shape, jnp.bfloat16))


def far_kernel(q_ref, num_in, tot_in, *refs):
    num_ref, tot_ref = refs[-2:]
    model = q_ref.shape[1]
    far = far_blocks(refs[:-2])
    for lanes in range(0, model, 128):
        at = slice(lanes, lanes + 128)
        num, tot = far_sums(far, q_ref[:, at], lanes, model)
        num_ref[:, at] = num_in[:, at] + num
        tot_ref[:, at] = tot_in[:, at] + tot


def final_kernel(
    q_ref, num_in, tot_in, sib_5_ref, sib_10_ref, w_hbm, out_ref, att, w_ref, sem
):
    copy = pltpu.make_async_copy(w_hbm, w_ref, sem)
    copy.start()
    model = q_ref.shape[1]
    far = far_blocks((sib_5_ref, sib_10_ref))
    for lanes in range(0, model, 128):
        at = slice(lanes, lanes + 128)
        num, tot = far_sums(far, q_ref[:, at], lanes, model)
        att[:, at] = ((num_in[:, at] + num) / (tot_in[:, at] + tot)).astype(jnp.bfloat16)
    copy.wait()
    out_ref[...] = jnp.dot(att[...], w_ref[...], preferred_element_type=jnp.float32).astype(
        jnp.bfloat16
    )


def per_device(tokens, w_qkv, w_out):
    rows, model = tokens.shape
    index = lax.axis_index(AXES)
    count = lax.axis_size(AXES)
    place = index.astype(jnp.int32).reshape(1)
    bf16 = lambda *shape: jax.ShapeDtypeStruct(shape, jnp.bfloat16)
    f32 = lambda *shape: jax.ShapeDtypeStruct(shape, jnp.float32)
    in_hbm = pl.BlockSpec(memory_space=pl.ANY)
    stay = lambda array: pltpu.with_memory_space_constraint(array, pltpu.HBM)
    steps = 2
    width = 2 * model // steps
    members = 32
    packed = 4 * 2 * model // 128
    block = bf16(BLOCK, 2 * model)
    kv, near, other, level_3, level_6 = call(
        project_kernel,
        (
            bf16(rows, 2 * model), bf16(2 * BLOCK, 2 * model), block,
            bf16(BLOCK // 2, 2 * model), bf16(members * packed, 128),
        ),
        [SMEM, in_hbm, in_hbm],
        place, stay(tokens), stay(w_qkv),
        flops=4 * rows * model * model,
        scratch=(
            pltpu.VMEM((rows, model), jnp.bfloat16),
            pltpu.VMEM((steps, model, width), jnp.bfloat16),
            pltpu.VMEM((2 * model // 128, rows, 128), jnp.float32),
            pltpu.SemaphoreType.DMA((steps + 1,)),
        ),
    )
    swap = [(i, i + 1) for i in range(1, count - 1, 2)]
    swap += [(j, i) for i, j in swap]
    def exchange(own, bit):
        return lax.ppermute(own, AXES, list(enumerate(partners(bit, count))))

    def pool(own, got, *after):
        return call(pool_kernel, block, vmem(2), own, got, after=after)

    teams = [
        [i for i in range(count) if i >> 6 == part and i & 1 == core]
        for part in range(count >> 6)
        for core in range(2)
    ]
    spread = lax.all_to_all(level_6, AXES, 0, 0, axis_index_groups=teams, tiled=True)
    near_sib = exchange(near, 0)
    own_3 = call(pool_near_kernel, block, vmem(2), level_3, near_sib)
    z_pairs = [[i, i ^ 2] for i in range(count) if not i & 2]
    both_3 = lax.all_gather(own_3, AXES, axis_index_groups=z_pairs, tiled=True)
    other_halo = lax.ppermute(other, AXES, swap)
    mine = call(
        unpack_kernel, bf16(3 * BLOCK // 2, 2 * model), [SMEM, *vmem(1)],
        place, spread.reshape(members, packed, 128),
        scratch=(pltpu.VMEM((members * packed, 128), jnp.float32),),
        after=(both_3, other_halo),
    )
    theirs = exchange(mine, 0)
    own_8 = call(own_8_kernel, block, vmem(2), mine, theirs)
    sib_8 = exchange(own_8, 6)
    own_4 = call(pool_kernel, block, vmem(1), both_3, after=(own_8,))
    sib_4 = exchange(own_4, 2)
    q, num, tot = call(
        functools.partial(local_kernel, count),
        (bf16(rows, model), f32(rows, model), f32(rows, model)),
        [SMEM, *vmem(1), in_hbm, *vmem(6)],
        place, tokens, stay(w_qkv), kv, near_sib, other_halo, both_3, mine, theirs,
        flops=10**9,
        scratch=(
            pltpu.VMEM((rows + 2 * BLOCK, 2 * model), jnp.bfloat16),
            pltpu.VMEM((rows // 2, 2 * model), jnp.bfloat16),
            pltpu.VMEM((model, model), jnp.bfloat16),
            pltpu.SemaphoreType.DMA(()),
        ),
        after=(own_4,),
    )
    own_9 = call(pool_halves_kernel, block, vmem(2), own_8, sib_8, after=(q,))
    sib_9 = exchange(own_9, 7)
    own_5 = pool(own_4, sib_4, own_9)
    sib_5 = exchange(own_5, 3)
    own_10 = pool(own_9, sib_9, own_5)
    sib_10 = exchange(own_10, 8)
    num, tot = call(
        far_kernel,
        (f32(rows, model), f32(rows, model)),
        vmem(6),
        q, num, tot, sib_4, sib_8, sib_9,
        flops=10**9,
        after=(own_10,),
    )
    return call(
        final_kernel,
        bf16(rows, model),
        [*vmem(5), in_hbm],
        q, num, tot, sib_5, sib_10, stay(w_out),
        flops=10**9,
        scratch=(
            pltpu.VMEM((rows, model), jnp.bfloat16),
            pltpu.VMEM((model, model), jnp.bfloat16),
            pltpu.SemaphoreType.DMA(()),
        ),
    )


def solution(mesh):
    return jax.shard_map(
        per_device,
        mesh=mesh,
        in_specs=(P(AXES, None), P(), P()),
        out_specs=P(AXES, None),
        check_vma=False,
    )
```

```python
import functools

import jax
import jax.numpy as jnp
import numpy as np
from jax import lax
from jax.experimental import pallas as pl
from jax.experimental.pallas import tpu as pltpu
from jax.sharding import PartitionSpec as P

HEADS = 8
BLOCK = 64
AXES = ("gx", "gy")
FAR8 = (6, 7, 4, 5, 2, 3, 0, 1)
FAR4 = (3, 2, 1, 0)


def partners(bit, count):
    route = []
    for index in range(count):
        if bit == 3:
            route.append(index & ~14 | FAR8[index >> 1 & 7] << 1)
        elif bit == 6:
            route.append(index & ~112 | FAR8[index >> 4 & 7] << 4)
        elif bit == 8:
            route.append(index & ~384 | FAR4[index >> 7 & 3] << 7)
        else:
            route.append(index ^ 1 << bit)
    return route


def vmem(count):
    return [pl.BlockSpec(memory_space=pltpu.VMEM)] * count


SMEM = pl.BlockSpec(memory_space=pltpu.SMEM)


def call(kernel, outs, in_specs, *args, flops=0, scratch=(), limit=10, after=()):
    count = len(args)

    def body(*refs):
        kernel(*refs[:count], *refs[count + len(after) :])

    return pl.pallas_call(
        body,
        out_shape=outs,
        in_specs=list(in_specs) + [pl.BlockSpec(memory_space=pl.ANY)] * len(after),
        out_specs=jax.tree.map(lambda _: pl.BlockSpec(memory_space=pltpu.VMEM), outs),
        scratch_shapes=list(scratch),
        compiler_params=pltpu.CompilerParams(vmem_limit_bytes=limit * 2**20),
        cost_estimate=pl.CostEstimate(flops=flops, bytes_accessed=2**20, transcendentals=0),
    )(*args, *after)


def pool_matrix(rows):
    r = lax.broadcasted_iota(jnp.int32, (rows, 2 * rows), 0)
    c = lax.broadcasted_iota(jnp.int32, (rows, 2 * rows), 1)
    return jnp.where(c >> 1 == r, 0.5, 0.0).astype(jnp.bfloat16)


def pooled(block):
    return jnp.dot(
        pool_matrix(block.shape[0] // 2), block, preferred_element_type=jnp.float32
    ).astype(jnp.bfloat16)


def project_kernel(
    place, x_hbm, w_hbm, kv_ref, near_ref, other_ref, l3_ref, packed_ref, x_buf, w_buf, part_buf, sems
):
    rows, model = x_buf.shape
    width = w_buf.shape[2]
    steps = w_buf.shape[0]
    x_copy = pltpu.make_async_copy(x_hbm, x_buf, sems.at[steps])
    x_copy.start()
    copies = []
    for step in range(steps):
        columns = pl.ds(model + step * width, width)
        copy = pltpu.make_async_copy(w_hbm.at[:, columns], w_buf.at[step], sems.at[step])
        copy.start()
        copies.append(copy)
    x_copy.wait()
    x = x_buf[...]
    pieces = []
    for step in range(steps):
        copies[step].wait()
        lanes = slice(step * width, (step + 1) * width)
        part = jnp.dot(x, w_buf[step], preferred_element_type=jnp.float32).astype(jnp.bfloat16)
        kv_ref[:, lanes] = part
        wide = part.astype(jnp.float32)
        for at in range(0, width, 128):
            tile = (step * width + at) // 128
            part_buf[tile] = wide[:, at : at + 128]
            size = rows
            while size > 8:
                size //= 2
                even = part_buf[tile, pl.ds(0, size, stride=2), :]
                odd = part_buf[tile, pl.ds(1, size, stride=2), :]
                level = ((even + odd) * 0.5).astype(jnp.bfloat16)
                if size == BLOCK:
                    near_ref[BLOCK:, tile * 128 : (tile + 1) * 128] = level
                if size == BLOCK // 2:
                    l3_ref[:, tile * 128 : (tile + 1) * 128] = level
                part_buf[tile, :size, :] = level.astype(jnp.float32)
            pieces.append(level.astype(jnp.float32))
    packed = pooled(jnp.concatenate(pieces, axis=0).astype(jnp.bfloat16))
    size = packed.shape[0]
    for copy in range(packed_ref.shape[0] // size):
        packed_ref[copy * size : (copy + 1) * size, :] = packed
    core = place[0] & 1
    last = rows - BLOCK
    low = pl.multiple_of(core * last, BLOCK)
    high = pl.multiple_of((1 - core) * last, BLOCK)
    near_ref[:BLOCK, :] = kv_ref[pl.ds(high, BLOCK), :]
    other_ref[...] = kv_ref[pl.ds(low, BLOCK), :]


def unpack_kernel(place, in_ref, out_ref, wide):
    members, rows, _ = in_ref.shape
    wide[...] = in_ref[...].reshape(members * rows, 128).astype(jnp.float32)
    y = (place[0] >> 4) & 3

    def mean(one, two):
        return ((one + two) * 0.5).astype(jnp.bfloat16).astype(jnp.float32)

    for tile in range(rows // 4):
        lanes = slice(tile * 128, (tile + 1) * 128)

        def level_6(start, count):
            return [
                wide[pl.ds(start * rows + tile * 4 + row, count, stride=rows), :]
                for row in range(4)
            ]

        def level_7(start, count):
            r = level_6(start, count)
            return [mean(r[0], r[1]), mean(r[2], r[3])]

        parts = (
            level_6((y ^ 1) * 8, 8)
            + level_7(((y >> 1) ^ 1) * 16, 16)
            + [mean(*level_7(0, members))]
        )
        out_ref[:, lanes] = jnp.concatenate(parts, axis=0).astype(jnp.bfloat16)


def own_8_kernel(mine_ref, sib_ref, out_ref):
    half = BLOCK // 2
    out_ref[:half, :] = mine_ref[BLOCK:, :]
    out_ref[half:, :] = sib_ref[BLOCK:, :]


def pool_near_kernel(mine_ref, sib_ref, out_ref):
    out_ref[: BLOCK // 2, :] = mine_ref[...]
    out_ref[BLOCK // 2 :, :] = pooled(sib_ref[BLOCK:, :])


def pool_halves_kernel(own_ref, sib_ref, out_ref):
    half = BLOCK // 2
    for num, ref in enumerate((own_ref, sib_ref)):
        block = ref[...].astype(jnp.float32)
        out_ref[num * half : (num + 1) * half, :] = (
            (block[:half] + block[half:]) * 0.5
        ).astype(jnp.bfloat16)


def pool_kernel(*refs):
    ins, out_ref = refs[:-1], refs[-1]
    half = BLOCK // len(ins)
    for num, ref in enumerate(ins):
        out_ref[num * half : (num + 1) * half, :] = pooled(ref[...])


def attend_pair(q, keys, values, ones):
    rows = q.shape[0]
    lane = lax.broadcasted_iota(jnp.int32, q.shape, 1)
    first = lane < 64
    zero = jnp.zeros_like(q)
    both = jnp.concatenate([jnp.where(first, q, zero), jnp.where(first, zero, q)], axis=0)
    scores = lax.dot_general(
        both, keys, (((1,), (1,)), ((), ())), preferred_element_type=jnp.float32
    )
    weights = jnp.exp(scores).astype(jnp.bfloat16)
    sums = jnp.dot(
        weights, jnp.concatenate([values, ones], axis=1), preferred_element_type=jnp.float32
    )
    num = jnp.where(first, sums[:rows, :128], sums[rows:, :128])
    tot = jnp.where(first, sums[:rows, 128:], sums[rows:, 128:])
    return num, tot


def local_kernel(
    count, place, x_ref, w_hbm, kv_ref, near_ref, other_ref, both_3_ref, sib_4_ref,
    mine_ref, theirs_ref, sib_8_ref, q_ref, num_ref, tot_ref, pad, l1, w_ref, sem
):
    rows, model = x_ref.shape
    blocks = rows // BLOCK
    copy = pltpu.make_async_copy(w_hbm.at[:, pl.ds(0, model)], w_ref, sem)
    copy.start()
    core = place[0] & 1
    sib_halo = near_ref[:BLOCK, :]
    other = other_ref[...]
    is_first = core == 0
    pad[:BLOCK, :] = jnp.where(is_first, other, sib_halo)
    pad[BLOCK : BLOCK + rows, :] = kv_ref[...]
    pad[BLOCK + rows :, :] = jnp.where(is_first, sib_halo, other)
    l1[...] = pooled(kv_ref[...])
    copy.wait()
    q_ref[...] = (
        jnp.dot(x_ref[...], w_ref[...], preferred_element_type=jnp.float32)
        .astype(jnp.bfloat16) * jnp.bfloat16(0.125)
    )
    key_row = lax.broadcasted_iota(jnp.int32, (4 * BLOCK, 128), 0)
    for i in range(blocks):
        ones = jnp.ones((4 * BLOCK, 128), jnp.float32)
        if i == 0:
            ones = jnp.where((key_row < BLOCK) & (place[0] == 0), 0.0, ones)
        if i == blocks - 1:
            ones = jnp.where((key_row >= 2 * BLOCK) & (key_row < 3 * BLOCK) & (place[0] == count - 1), 0.0, ones)
        ones = ones.astype(jnp.bfloat16)
        sib = (i >> 1) ^ 1
        here = slice(i * BLOCK, (i + 1) * BLOCK)
        for lanes in range(0, model, 128):
            kl = slice(lanes, lanes + 128)
            vl = slice(model + lanes, model + lanes + 128)
            keys = jnp.concatenate(
                [pad[i * BLOCK : (i + 3) * BLOCK, kl], l1[sib * BLOCK : (sib + 1) * BLOCK, kl]], axis=0
            )
            values = jnp.concatenate(
                [pad[i * BLOCK : (i + 3) * BLOCK, vl], l1[sib * BLOCK : (sib + 1) * BLOCK, vl]], axis=0
            )
            num, tot = attend_pair(q_ref[here, kl], keys, values, ones)
            num_ref[here, kl] = num
            tot_ref[here, kl] = tot
    start = pl.multiple_of((1 - ((place[0] >> 1) & 1)) * BLOCK, BLOCK)
    sib_3 = both_3_ref[pl.ds(start, BLOCK), :]
    far = far_blocks((near_ref, sib_3, sib_4_ref, mine_ref, theirs_ref, sib_8_ref))
    for lanes in range(0, model, 128):
        kl = slice(lanes, lanes + 128)
        num, tot = far_sums(far, q_ref[:, kl], lanes, model)
        num_ref[:, kl] += num
        tot_ref[:, kl] += tot


def far_blocks(refs):
    blocks = []
    for ref in refs:
        if ref.shape[0] == 2 * BLOCK:
            blocks.append(ref[BLOCK:, :])
        else:
            blocks.append(ref[:BLOCK, :])
    return jnp.concatenate(blocks, axis=0)


def far_sums(far, q, lanes, model):
    keys = far[:, lanes : lanes + 128]
    values = far[:, model + lanes : model + lanes + 128]
    return attend_pair(q, keys, values, jnp.ones(values.shape, jnp.bfloat16))


def final_kernel(
    q_ref, num_in, tot_in, sib_5_ref, sib_9_ref, sib_10_ref, w_hbm, out_ref, att, w_ref, sem
):
    copy = pltpu.make_async_copy(w_hbm, w_ref, sem)
    copy.start()
    model = q_ref.shape[1]
    far = far_blocks((sib_5_ref, sib_9_ref, sib_10_ref))
    for lanes in range(0, model, 128):
        at = slice(lanes, lanes + 128)
        num, tot = far_sums(far, q_ref[:, at], lanes, model)
        att[:, at] = ((num_in[:, at] + num) / (tot_in[:, at] + tot)).astype(jnp.bfloat16)
    copy.wait()
    out_ref[...] = jnp.dot(att[...], w_ref[...], preferred_element_type=jnp.float32).astype(
        jnp.bfloat16
    )


def per_device(tokens, w_qkv, w_out):
    rows, model = tokens.shape
    index = lax.axis_index(AXES)
    count = lax.axis_size(AXES)
    place = index.astype(jnp.int32).reshape(1)
    bf16 = lambda *shape: jax.ShapeDtypeStruct(shape, jnp.bfloat16)
    f32 = lambda *shape: jax.ShapeDtypeStruct(shape, jnp.float32)
    in_hbm = pl.BlockSpec(memory_space=pl.ANY)
    stay = lambda array: pltpu.with_memory_space_constraint(array, pltpu.HBM)
    steps = 2
    width = 2 * model // steps
    members = 32
    packed = 4 * 2 * model // 128
    block = bf16(BLOCK, 2 * model)
    kv, near, other, level_3, level_6 = call(
        project_kernel,
        (
            bf16(rows, 2 * model), bf16(2 * BLOCK, 2 * model), block,
            bf16(BLOCK // 2, 2 * model), bf16(members * packed, 128),
        ),
        [SMEM, in_hbm, in_hbm],
        place, stay(tokens), stay(w_qkv),
        flops=4 * rows * model * model,
        scratch=(
            pltpu.VMEM((rows, model), jnp.bfloat16),
            pltpu.VMEM((steps, model, width), jnp.bfloat16),
            pltpu.VMEM((2 * model // 128, rows, 128), jnp.float32),
            pltpu.SemaphoreType.DMA((steps + 1,)),
        ),
    )
    swap = [(i, i + 1) for i in range(1, count - 1, 2)]
    swap += [(j, i) for i, j in swap]
    def exchange(own, bit):
        return lax.ppermute(own, AXES, list(enumerate(partners(bit, count))))

    def pool(own, got, *after):
        return call(pool_kernel, block, vmem(2), own, got, after=after)

    teams = [
        [i for i in range(count) if i >> 6 == part and i & 1 == core]
        for part in range(count >> 6)
        for core in range(2)
    ]
    spread = lax.all_to_all(level_6, AXES, 0, 0, axis_index_groups=teams, tiled=True)
    near_sib = exchange(near, 0)
    own_3 = call(pool_near_kernel, block, vmem(2), level_3, near_sib)
    z_pairs = [[i, i ^ 2] for i in range(count) if not i & 2]
    both_3 = lax.all_gather(own_3, AXES, axis_index_groups=z_pairs, tiled=True)
    other_halo = lax.ppermute(other, AXES, swap)
    mine = call(
        unpack_kernel, bf16(3 * BLOCK // 2, 2 * model), [SMEM, *vmem(1)],
        place, spread.reshape(members, packed, 128),
        scratch=(pltpu.VMEM((members * packed, 128), jnp.float32),),
        after=(both_3, other_halo),
    )
    theirs = exchange(mine, 0)
    own_8 = call(own_8_kernel, block, vmem(2), mine, theirs)
    sib_8 = exchange(own_8, 6)
    own_4 = call(pool_kernel, block, vmem(1), both_3, after=(own_8,))
    sib_4 = exchange(own_4, 2)
    own_9 = call(pool_halves_kernel, block, vmem(2), own_8, sib_8, after=(own_4,))
    sib_9 = exchange(own_9, 7)
    own_5 = pool(own_4, sib_4, own_9)
    sib_5 = exchange(own_5, 3)
    own_10 = pool(own_9, sib_9, own_5)
    sib_10 = exchange(own_10, 8)
    q, num, tot = call(
        functools.partial(local_kernel, count),
        (bf16(rows, model), f32(rows, model), f32(rows, model)),
        [SMEM, *vmem(1), in_hbm, *vmem(8)],
        place, tokens, stay(w_qkv), kv, near_sib, other_halo, both_3, sib_4, mine, theirs, sib_8,
        flops=10**9,
        scratch=(
            pltpu.VMEM((rows + 2 * BLOCK, 2 * model), jnp.bfloat16),
            pltpu.VMEM((rows // 2, 2 * model), jnp.bfloat16),
            pltpu.VMEM((model, model), jnp.bfloat16),
            pltpu.SemaphoreType.DMA(()),
        ),
        after=(own_10,),
    )
    return call(
        final_kernel,
        bf16(rows, model),
        [*vmem(6), in_hbm],
        q, num, tot, sib_5, sib_9, sib_10, stay(w_out),
        flops=10**9,
        scratch=(
            pltpu.VMEM((rows, model), jnp.bfloat16),
            pltpu.VMEM((model, model), jnp.bfloat16),
            pltpu.SemaphoreType.DMA(()),
        ),
    )


def solution(mesh):
    return jax.shard_map(
        per_device,
        mesh=mesh,
        in_specs=(P(AXES, None), P(), P()),
        out_specs=P(AXES, None),
        check_vma=False,
    )
```

```python
import functools

import jax
import jax.numpy as jnp
import numpy as np
from jax import lax
from jax.experimental import pallas as pl
from jax.experimental.pallas import tpu as pltpu
from jax.sharding import PartitionSpec as P

HEADS = 8
BLOCK = 64
AXES = ("gx", "gy")
FAR8 = (6, 7, 4, 5, 2, 3, 0, 1)
FAR4 = (3, 2, 1, 0)


def partners(bit, count):
    route = []
    for index in range(count):
        if bit == 3:
            route.append(index & ~14 | FAR8[index >> 1 & 7] << 1)
        elif bit == 8:
            route.append(index & ~384 | FAR4[index >> 7 & 3] << 7)
        else:
            route.append(index ^ 1 << bit)
    return route


def vmem(count):
    return [pl.BlockSpec(memory_space=pltpu.VMEM)] * count


SMEM = pl.BlockSpec(memory_space=pltpu.SMEM)


def call(kernel, outs, in_specs, *args, flops=0, scratch=(), limit=10, after=()):
    count = len(args)

    def body(*refs):
        kernel(*refs[:count], *refs[count + len(after) :])

    return pl.pallas_call(
        body,
        out_shape=outs,
        in_specs=list(in_specs) + [pl.BlockSpec(memory_space=pl.ANY)] * len(after),
        out_specs=jax.tree.map(lambda _: pl.BlockSpec(memory_space=pltpu.VMEM), outs),
        scratch_shapes=list(scratch),
        compiler_params=pltpu.CompilerParams(vmem_limit_bytes=limit * 2**20),
        cost_estimate=pl.CostEstimate(flops=flops, bytes_accessed=2**20, transcendentals=0),
    )(*args, *after)


def pool_matrix(rows):
    r = lax.broadcasted_iota(jnp.int32, (rows, 2 * rows), 0)
    c = lax.broadcasted_iota(jnp.int32, (rows, 2 * rows), 1)
    return jnp.where(c >> 1 == r, 0.5, 0.0).astype(jnp.bfloat16)


def pooled(block):
    return jnp.dot(
        pool_matrix(block.shape[0] // 2), block, preferred_element_type=jnp.float32
    ).astype(jnp.bfloat16)


def project_kernel(
    place, x_hbm, w_hbm, kv_ref, near_ref, other_ref, l3_ref, packed_ref, x_buf, w_buf, part_buf, sems
):
    rows, model = x_buf.shape
    width = w_buf.shape[2]
    steps = w_buf.shape[0]
    x_copy = pltpu.make_async_copy(x_hbm, x_buf, sems.at[steps])
    x_copy.start()
    copies = []
    for step in range(steps):
        columns = pl.ds(model + step * width, width)
        copy = pltpu.make_async_copy(w_hbm.at[:, columns], w_buf.at[step], sems.at[step])
        copy.start()
        copies.append(copy)
    x_copy.wait()
    x = x_buf[...]
    pieces = []
    for step in range(steps):
        copies[step].wait()
        lanes = slice(step * width, (step + 1) * width)
        part = jnp.dot(x, w_buf[step], preferred_element_type=jnp.float32).astype(jnp.bfloat16)
        kv_ref[:, lanes] = part
        wide = part.astype(jnp.float32)
        for at in range(0, width, 128):
            tile = (step * width + at) // 128
            part_buf[tile] = wide[:, at : at + 128]
            size = rows
            while size > 8:
                size //= 2
                even = part_buf[tile, pl.ds(0, size, stride=2), :]
                odd = part_buf[tile, pl.ds(1, size, stride=2), :]
                level = ((even + odd) * 0.5).astype(jnp.bfloat16)
                if size == BLOCK:
                    near_ref[BLOCK:, tile * 128 : (tile + 1) * 128] = level
                if size == BLOCK // 2:
                    l3_ref[:, tile * 128 : (tile + 1) * 128] = level
                part_buf[tile, :size, :] = level.astype(jnp.float32)
            pieces.append(level.astype(jnp.float32))
    packed = pooled(jnp.concatenate(pieces, axis=0).astype(jnp.bfloat16))
    size = packed.shape[0]
    for copy in range(packed_ref.shape[0] // size):
        packed_ref[copy * size : (copy + 1) * size, :] = packed
    core = place[0] & 1
    last = rows - BLOCK
    low = pl.multiple_of(core * last, BLOCK)
    high = pl.multiple_of((1 - core) * last, BLOCK)
    near_ref[:BLOCK, :] = kv_ref[pl.ds(high, BLOCK), :]
    other_ref[...] = kv_ref[pl.ds(low, BLOCK), :]


def unpack_kernel(place, in_ref, out_ref, wide):
    members, rows, _ = in_ref.shape
    wide[...] = in_ref[...].reshape(members * rows, 128).astype(jnp.float32)
    y = (place[0] >> 4) & 7

    def mean(one, two):
        return ((one + two) * 0.5).astype(jnp.bfloat16).astype(jnp.float32)

    for tile in range(rows // 4):
        lanes = slice(tile * 128, (tile + 1) * 128)

        def level_6(start, count):
            return [
                wide[pl.ds(start * rows + tile * 4 + row, count, stride=rows), :]
                for row in range(4)
            ]

        def level_7(start, count):
            r = level_6(start, count)
            return [mean(r[0], r[1]), mean(r[2], r[3])]

        parts = (
            level_6((y ^ 1) * 8, 8)
            + level_7(((y >> 1) ^ 1) * 16, 16)
            + [mean(*level_7(((y >> 2) ^ 1) * 32, 32))]
            + [mean(*level_7(0, members))]
        )
        out_ref[:, lanes] = jnp.concatenate(parts, axis=0).astype(jnp.bfloat16)


def own_9_kernel(mine_ref, sib_ref, out_ref):
    at = 3 * BLOCK // 2
    both = mine_ref[at:, :].astype(jnp.float32) + sib_ref[at:, :].astype(jnp.float32)
    out_ref[...] = (both * 0.5).astype(jnp.bfloat16)


def pool_near_kernel(mine_ref, sib_ref, out_ref):
    out_ref[: BLOCK // 2, :] = mine_ref[...]
    out_ref[BLOCK // 2 :, :] = pooled(sib_ref[BLOCK:, :])


def pool_kernel(*refs):
    ins, out_ref = refs[:-1], refs[-1]
    half = BLOCK // len(ins)
    for num, ref in enumerate(ins):
        out_ref[num * half : (num + 1) * half, :] = pooled(ref[...])


def attend_pair(q, keys, values, ones):
    rows = q.shape[0]
    lane = lax.broadcasted_iota(jnp.int32, q.shape, 1)
    first = lane < 64
    zero = jnp.zeros_like(q)
    both = jnp.concatenate([jnp.where(first, q, zero), jnp.where(first, zero, q)], axis=0)
    scores = lax.dot_general(
        both, keys, (((1,), (1,)), ((), ())), preferred_element_type=jnp.float32
    )
    weights = jnp.exp(scores).astype(jnp.bfloat16)
    sums = jnp.dot(
        weights, jnp.concatenate([values, ones], axis=1), preferred_element_type=jnp.float32
    )
    num = jnp.where(first, sums[:rows, :128], sums[rows:, :128])
    tot = jnp.where(first, sums[:rows, 128:], sums[rows:, 128:])
    return num, tot


def local_kernel(
    count, place, x_ref, w_hbm, kv_ref, near_ref, other_ref, mine_ref, theirs_ref, both_3_ref,
    both_4_ref, q_ref, num_ref, tot_ref, pad, l1, w_ref, sem
):
    rows, model = x_ref.shape
    blocks = rows // BLOCK
    copy = pltpu.make_async_copy(w_hbm.at[:, pl.ds(0, model)], w_ref, sem)
    copy.start()
    core = place[0] & 1
    sib_halo = near_ref[:BLOCK, :]
    other = other_ref[...]
    is_first = core == 0
    pad[:BLOCK, :] = jnp.where(is_first, other, sib_halo)
    pad[BLOCK : BLOCK + rows, :] = kv_ref[...]
    pad[BLOCK + rows :, :] = jnp.where(is_first, sib_halo, other)
    l1[...] = pooled(kv_ref[...])
    copy.wait()
    q_ref[...] = (
        jnp.dot(x_ref[...], w_ref[...], preferred_element_type=jnp.float32)
        .astype(jnp.bfloat16) * jnp.bfloat16(0.125)
    )
    key_row = lax.broadcasted_iota(jnp.int32, (4 * BLOCK, 128), 0)
    for i in range(blocks):
        ones = jnp.ones((4 * BLOCK, 128), jnp.float32)
        if i == 0:
            ones = jnp.where((key_row < BLOCK) & (place[0] == 0), 0.0, ones)
        if i == blocks - 1:
            ones = jnp.where((key_row >= 2 * BLOCK) & (key_row < 3 * BLOCK) & (place[0] == count - 1), 0.0, ones)
        ones = ones.astype(jnp.bfloat16)
        sib = (i >> 1) ^ 1
        here = slice(i * BLOCK, (i + 1) * BLOCK)
        for lanes in range(0, model, 128):
            kl = slice(lanes, lanes + 128)
            vl = slice(model + lanes, model + lanes + 128)
            keys = jnp.concatenate(
                [pad[i * BLOCK : (i + 3) * BLOCK, kl], l1[sib * BLOCK : (sib + 1) * BLOCK, kl]], axis=0
            )
            values = jnp.concatenate(
                [pad[i * BLOCK : (i + 3) * BLOCK, vl], l1[sib * BLOCK : (sib + 1) * BLOCK, vl]], axis=0
            )
            num, tot = attend_pair(q_ref[here, kl], keys, values, ones)
            num_ref[here, kl] = num
            tot_ref[here, kl] = tot
    picked = []
    for bit, ref in ((1, both_3_ref), (2, both_4_ref)):
        start = pl.multiple_of((1 - ((place[0] >> bit) & 1)) * BLOCK, BLOCK)
        picked.append(ref[pl.ds(start, BLOCK), :])
    for refs in ((mine_ref, theirs_ref), (near_ref, *picked)):
        far = far_blocks(refs)
        for lanes in range(0, model, 128):
            kl = slice(lanes, lanes + 128)
            num, tot = far_sums(far, q_ref[:, kl], lanes, model)
            num_ref[:, kl] += num
            tot_ref[:, kl] += tot


def far_blocks(refs):
    blocks = []
    for ref in refs:
        if ref.shape[0] == 2 * BLOCK:
            blocks.append(ref[BLOCK:, :])
        elif ref.shape[0] > 2 * BLOCK:
            blocks.append(ref[: 3 * BLOCK // 2, :])
        else:
            blocks.append(ref[...])
    return jnp.concatenate(blocks, axis=0)


def far_sums(far, q, lanes, model):
    keys = far[:, lanes : lanes + 128]
    values = far[:, model + lanes : model + lanes + 128]
    return attend_pair(q, keys, values, jnp.ones(values.shape, jnp.bfloat16))


def final_kernel(
    q_ref, num_in, tot_in, sib_5_ref, sib_9_ref, sib_10_ref, w_hbm, out_ref, att, w_ref, sem
):
    copy = pltpu.make_async_copy(w_hbm, w_ref, sem)
    copy.start()
    model = q_ref.shape[1]
    far = far_blocks((sib_5_ref, sib_9_ref, sib_10_ref))
    for lanes in range(0, model, 128):
        at = slice(lanes, lanes + 128)
        num, tot = far_sums(far, q_ref[:, at], lanes, model)
        att[:, at] = ((num_in[:, at] + num) / (tot_in[:, at] + tot)).astype(jnp.bfloat16)
    copy.wait()
    out_ref[...] = jnp.dot(att[...], w_ref[...], preferred_element_type=jnp.float32).astype(
        jnp.bfloat16
    )


def per_device(tokens, w_qkv, w_out):
    rows, model = tokens.shape
    index = lax.axis_index(AXES)
    count = lax.axis_size(AXES)
    place = index.astype(jnp.int32).reshape(1)
    bf16 = lambda *shape: jax.ShapeDtypeStruct(shape, jnp.bfloat16)
    f32 = lambda *shape: jax.ShapeDtypeStruct(shape, jnp.float32)
    in_hbm = pl.BlockSpec(memory_space=pl.ANY)
    stay = lambda array: pltpu.with_memory_space_constraint(array, pltpu.HBM)
    steps = 2
    width = 2 * model // steps
    members = 64
    packed = 4 * 2 * model // 128
    block = bf16(BLOCK, 2 * model)
    kv, near, other, level_3, level_6 = call(
        project_kernel,
        (
            bf16(rows, 2 * model), bf16(2 * BLOCK, 2 * model), block,
            bf16(BLOCK // 2, 2 * model), bf16(members * packed, 128),
        ),
        [SMEM, in_hbm, in_hbm],
        place, stay(tokens), stay(w_qkv),
        flops=4 * rows * model * model,
        scratch=(
            pltpu.VMEM((rows, model), jnp.bfloat16),
            pltpu.VMEM((steps, model, width), jnp.bfloat16),
            pltpu.VMEM((2 * model // 128, rows, 128), jnp.float32),
            pltpu.SemaphoreType.DMA((steps + 1,)),
        ),
    )
    swap = [(i, i + 1) for i in range(1, count - 1, 2)]
    swap += [(j, i) for i, j in swap]
    def exchange(own, bit):
        return lax.ppermute(own, AXES, list(enumerate(partners(bit, count))))

    def pool(own, got, *after):
        return call(pool_kernel, block, vmem(2), own, got, after=after)

    teams = [
        [i for i in range(count) if i >> 7 == x and i & 1 == core]
        for x in range(count >> 7)
        for core in range(2)
    ]
    spread = lax.all_to_all(level_6, AXES, 0, 0, axis_index_groups=teams, tiled=True)
    near_sib = exchange(near, 0)
    own_3 = call(pool_near_kernel, block, vmem(2), level_3, near_sib)
    other_halo = lax.ppermute(other, AXES, swap)

    def pair_gather(own, bit):
        pairs = [[i, i ^ 1 << bit] for i in range(count) if not i >> bit & 1]
        return lax.all_gather(own, AXES, axis_index_groups=pairs, tiled=True)

    both_3 = pair_gather(own_3, 1)
    own_4 = call(pool_kernel, block, vmem(1), both_3)
    both_4 = pair_gather(own_4, 2)
    mine = call(
        unpack_kernel, bf16(5 * BLOCK // 2, 2 * model), [SMEM, *vmem(1)],
        place, spread.reshape(members, packed, 128),
        scratch=(pltpu.VMEM((members * packed, 128), jnp.float32),),
        after=(both_4, other_halo),
    )
    theirs = exchange(mine, 0)
    own_9 = call(own_9_kernel, block, vmem(2), mine, theirs)
    sib_9 = exchange(own_9, 7)
    own_5 = call(pool_kernel, block, vmem(1), both_4, after=(own_9,))
    sib_5 = exchange(own_5, 3)
    own_10 = pool(own_9, sib_9, own_5)
    sib_10 = exchange(own_10, 8)
    q, num, tot = call(
        functools.partial(local_kernel, count),
        (bf16(rows, model), f32(rows, model), f32(rows, model)),
        [SMEM, *vmem(1), in_hbm, *vmem(7)],
        place, tokens, stay(w_qkv), kv, near_sib, other_halo, mine, theirs, both_3, both_4,
        flops=10**9,
        scratch=(
            pltpu.VMEM((rows + 2 * BLOCK, 2 * model), jnp.bfloat16),
            pltpu.VMEM((rows // 2, 2 * model), jnp.bfloat16),
            pltpu.VMEM((model, model), jnp.bfloat16),
            pltpu.SemaphoreType.DMA(()),
        ),
        after=(own_10,),
    )
    return call(
        final_kernel,
        bf16(rows, model),
        [*vmem(6), in_hbm],
        q, num, tot, sib_5, sib_9, sib_10, stay(w_out),
        flops=10**9,
        scratch=(
            pltpu.VMEM((rows, model), jnp.bfloat16),
            pltpu.VMEM((model, model), jnp.bfloat16),
            pltpu.SemaphoreType.DMA(()),
        ),
    )


def solution(mesh):
    return jax.shard_map(
        per_device,
        mesh=mesh,
        in_specs=(P(AXES, None), P(), P()),
        out_specs=P(AXES, None),
        check_vma=False,
    )
```

```python
import functools

import jax
import jax.numpy as jnp
import numpy as np
from jax import lax
from jax.experimental import pallas as pl
from jax.experimental.pallas import tpu as pltpu
from jax.sharding import PartitionSpec as P

HEADS = 8
BLOCK = 64
AXES = ("gx", "gy")
FAR8 = (6, 7, 4, 5, 2, 3, 0, 1)
FAR4 = (3, 2, 1, 0)


def partners(bit, count):
    route = []
    for index in range(count):
        if bit == 3:
            route.append(index & ~14 | FAR8[index >> 1 & 7] << 1)
        elif bit == 6:
            route.append(index & ~112 | FAR8[index >> 4 & 7] << 4)
        elif bit == 8:
            route.append(index & ~384 | FAR4[index >> 7 & 3] << 7)
        else:
            route.append(index ^ 1 << bit)
    return route


def vmem(count):
    return [pl.BlockSpec(memory_space=pltpu.VMEM)] * count


SMEM = pl.BlockSpec(memory_space=pltpu.SMEM)


def call(kernel, outs, in_specs, *args, flops=0, scratch=(), limit=10, after=()):
    count = len(args)

    def body(*refs):
        kernel(*refs[:count], *refs[count + len(after) :])

    return pl.pallas_call(
        body,
        out_shape=outs,
        in_specs=list(in_specs) + [pl.BlockSpec(memory_space=pl.ANY)] * len(after),
        out_specs=jax.tree.map(lambda _: pl.BlockSpec(memory_space=pltpu.VMEM), outs),
        scratch_shapes=list(scratch),
        compiler_params=pltpu.CompilerParams(vmem_limit_bytes=limit * 2**20),
        cost_estimate=pl.CostEstimate(flops=flops, bytes_accessed=2**20, transcendentals=0),
    )(*args, *after)


def pool_matrix(rows):
    r = lax.broadcasted_iota(jnp.int32, (rows, 2 * rows), 0)
    c = lax.broadcasted_iota(jnp.int32, (rows, 2 * rows), 1)
    return jnp.where(c >> 1 == r, 0.5, 0.0).astype(jnp.bfloat16)


def pooled(block):
    return jnp.dot(
        pool_matrix(block.shape[0] // 2), block, preferred_element_type=jnp.float32
    ).astype(jnp.bfloat16)


def project_kernel(
    place, x_hbm, w_hbm, kv_ref, near_ref, other_ref, l3_ref, packed_ref, x_buf, w_buf, part_buf, sems
):
    rows, model = x_buf.shape
    width = w_buf.shape[2]
    steps = w_buf.shape[0]
    x_copy = pltpu.make_async_copy(x_hbm, x_buf, sems.at[steps])
    x_copy.start()
    copies = []
    for step in range(steps):
        columns = pl.ds(model + step * width, width)
        copy = pltpu.make_async_copy(w_hbm.at[:, columns], w_buf.at[step], sems.at[step])
        copy.start()
        copies.append(copy)
    x_copy.wait()
    x = x_buf[...]
    pieces = []
    for step in range(steps):
        copies[step].wait()
        lanes = slice(step * width, (step + 1) * width)
        part = jnp.dot(x, w_buf[step], preferred_element_type=jnp.float32).astype(jnp.bfloat16)
        kv_ref[:, lanes] = part
        wide = part.astype(jnp.float32)
        for at in range(0, width, 128):
            tile = (step * width + at) // 128
            part_buf[tile] = wide[:, at : at + 128]
            size = rows
            while size > 8:
                size //= 2
                even = part_buf[tile, pl.ds(0, size, stride=2), :]
                odd = part_buf[tile, pl.ds(1, size, stride=2), :]
                level = ((even + odd) * 0.5).astype(jnp.bfloat16)
                if size == BLOCK:
                    near_ref[BLOCK:, tile * 128 : (tile + 1) * 128] = level
                if size == BLOCK // 2:
                    l3_ref[:, tile * 128 : (tile + 1) * 128] = level
                part_buf[tile, :size, :] = level.astype(jnp.float32)
            pieces.append(level.astype(jnp.float32))
    packed = pooled(jnp.concatenate(pieces, axis=0).astype(jnp.bfloat16))
    size = packed.shape[0]
    for copy in range(packed_ref.shape[0] // size):
        packed_ref[copy * size : (copy + 1) * size, :] = packed
    core = place[0] & 1
    last = rows - BLOCK
    low = pl.multiple_of(core * last, BLOCK)
    high = pl.multiple_of((1 - core) * last, BLOCK)
    near_ref[:BLOCK, :] = kv_ref[pl.ds(high, BLOCK), :]
    other_ref[...] = kv_ref[pl.ds(low, BLOCK), :]


def unpack_kernel(place, in_ref, out_ref, wide):
    members, rows, _ = in_ref.shape
    wide[...] = in_ref[...].reshape(members * rows, 128).astype(jnp.float32)
    y = (place[0] >> 4) & 3

    def mean(one, two):
        return ((one + two) * 0.5).astype(jnp.bfloat16).astype(jnp.float32)

    for tile in range(rows // 4):
        lanes = slice(tile * 128, (tile + 1) * 128)

        def level_6(start, count):
            return [
                wide[pl.ds(start * rows + tile * 4 + row, count, stride=rows), :]
                for row in range(4)
            ]

        def level_7(start, count):
            r = level_6(start, count)
            return [mean(r[0], r[1]), mean(r[2], r[3])]

        parts = (
            level_6((y ^ 1) * 8, 8)
            + level_7(((y >> 1) ^ 1) * 16, 16)
            + [mean(*level_7(0, members))]
        )
        out_ref[:, lanes] = jnp.concatenate(parts, axis=0).astype(jnp.bfloat16)


def own_8_kernel(both_ref, out_ref):
    half = BLOCK // 2
    out_ref[:half, :] = both_ref[BLOCK : BLOCK + half, :]
    out_ref[half:, :] = both_ref[2 * BLOCK + half :, :]


def pool_near_kernel(mine_ref, sib_ref, out_ref):
    out_ref[: BLOCK // 2, :] = mine_ref[...]
    out_ref[BLOCK // 2 :, :] = pooled(sib_ref[BLOCK:, :])


def pool_halves_kernel(own_ref, sib_ref, out_ref):
    half = BLOCK // 2
    for num, ref in enumerate((own_ref, sib_ref)):
        block = ref[...].astype(jnp.float32)
        out_ref[num * half : (num + 1) * half, :] = (
            (block[:half] + block[half:]) * 0.5
        ).astype(jnp.bfloat16)


def pool_kernel(*refs):
    ins, out_ref = refs[:-1], refs[-1]
    half = BLOCK // len(ins)
    for num, ref in enumerate(ins):
        out_ref[num * half : (num + 1) * half, :] = pooled(ref[...])


def attend_pair(q, keys, values, ones):
    rows = q.shape[0]
    lane = lax.broadcasted_iota(jnp.int32, q.shape, 1)
    first = lane < 64
    zero = jnp.zeros_like(q)
    both = jnp.concatenate([jnp.where(first, q, zero), jnp.where(first, zero, q)], axis=0)
    scores = lax.dot_general(
        both, keys, (((1,), (1,)), ((), ())), preferred_element_type=jnp.float32
    )
    weights = jnp.exp(scores).astype(jnp.bfloat16)
    sums = jnp.dot(
        weights, jnp.concatenate([values, ones], axis=1), preferred_element_type=jnp.float32
    )
    num = jnp.where(first, sums[:rows, :128], sums[rows:, :128])
    tot = jnp.where(first, sums[:rows, 128:], sums[rows:, 128:])
    return num, tot


def local_kernel(
    count, place, x_ref, w_hbm, kv_ref, near_ref, other_ref, both_3_ref, both_ref,
    q_ref, num_ref, tot_ref, pad, l1, w_ref, sem
):
    rows, model = x_ref.shape
    blocks = rows // BLOCK
    copy = pltpu.make_async_copy(w_hbm.at[:, pl.ds(0, model)], w_ref, sem)
    copy.start()
    core = place[0] & 1
    sib_halo = near_ref[:BLOCK, :]
    other = other_ref[...]
    is_first = core == 0
    pad[:BLOCK, :] = jnp.where(is_first, other, sib_halo)
    pad[BLOCK : BLOCK + rows, :] = kv_ref[...]
    pad[BLOCK + rows :, :] = jnp.where(is_first, sib_halo, other)
    l1[...] = pooled(kv_ref[...])
    copy.wait()
    q_ref[...] = (
        jnp.dot(x_ref[...], w_ref[...], preferred_element_type=jnp.float32)
        .astype(jnp.bfloat16) * jnp.bfloat16(0.125)
    )
    key_row = lax.broadcasted_iota(jnp.int32, (4 * BLOCK, 128), 0)
    for i in range(blocks):
        ones = jnp.ones((4 * BLOCK, 128), jnp.float32)
        if i == 0:
            ones = jnp.where((key_row < BLOCK) & (place[0] == 0), 0.0, ones)
        if i == blocks - 1:
            ones = jnp.where((key_row >= 2 * BLOCK) & (key_row < 3 * BLOCK) & (place[0] == count - 1), 0.0, ones)
        ones = ones.astype(jnp.bfloat16)
        sib = (i >> 1) ^ 1
        here = slice(i * BLOCK, (i + 1) * BLOCK)
        for lanes in range(0, model, 128):
            kl = slice(lanes, lanes + 128)
            vl = slice(model + lanes, model + lanes + 128)
            keys = jnp.concatenate(
                [pad[i * BLOCK : (i + 3) * BLOCK, kl], l1[sib * BLOCK : (sib + 1) * BLOCK, kl]], axis=0
            )
            values = jnp.concatenate(
                [pad[i * BLOCK : (i + 3) * BLOCK, vl], l1[sib * BLOCK : (sib + 1) * BLOCK, vl]], axis=0
            )
            num, tot = attend_pair(q_ref[here, kl], keys, values, ones)
            num_ref[here, kl] = num
            tot_ref[here, kl] = tot
    start = pl.multiple_of((1 - ((place[0] >> 1) & 1)) * BLOCK, BLOCK)
    sib_3 = both_3_ref[pl.ds(start, BLOCK), :]
    far = far_blocks((near_ref, sib_3, both_ref[:BLOCK, :], both_ref[3 * BLOCK // 2 : 5 * BLOCK // 2, :]))
    for lanes in range(0, model, 128):
        kl = slice(lanes, lanes + 128)
        num, tot = far_sums(far, q_ref[:, kl], lanes, model)
        num_ref[:, kl] += num
        tot_ref[:, kl] += tot


def far_blocks(refs):
    blocks = []
    for ref in refs:
        if ref.shape[0] == 2 * BLOCK:
            blocks.append(ref[BLOCK:, :])
        else:
            blocks.append(ref[:BLOCK, :])
    return jnp.concatenate(blocks, axis=0)


def far_sums(far, q, lanes, model):
    keys = far[:, lanes : lanes + 128]
    values = far[:, model + lanes : model + lanes + 128]
    return attend_pair(q, keys, values, jnp.ones(values.shape, jnp.bfloat16))


def final_kernel(
    place, q_ref, num_in, tot_in, sib_4_ref, sib_5_ref, sib_8_ref, sib_9_ref, pair_ref, w_hbm,
    out_ref, att, w_ref, sem
):
    copy = pltpu.make_async_copy(w_hbm, w_ref, sem)
    copy.start()
    model = q_ref.shape[1]
    start = pl.multiple_of((1 - ((place[0] >> 8) & 1)) * BLOCK, BLOCK)
    sib_10 = pair_ref[pl.ds(start, BLOCK), :]
    far = far_blocks((sib_4_ref, sib_5_ref, sib_8_ref, sib_9_ref, sib_10))
    for lanes in range(0, model, 128):
        at = slice(lanes, lanes + 128)
        num, tot = far_sums(far, q_ref[:, at], lanes, model)
        att[:, at] = ((num_in[:, at] + num) / (tot_in[:, at] + tot)).astype(jnp.bfloat16)
    copy.wait()
    out_ref[...] = jnp.dot(att[...], w_ref[...], preferred_element_type=jnp.float32).astype(
        jnp.bfloat16
    )


def per_device(tokens, w_qkv, w_out):
    rows, model = tokens.shape
    index = lax.axis_index(AXES)
    count = lax.axis_size(AXES)
    place = index.astype(jnp.int32).reshape(1)
    bf16 = lambda *shape: jax.ShapeDtypeStruct(shape, jnp.bfloat16)
    f32 = lambda *shape: jax.ShapeDtypeStruct(shape, jnp.float32)
    in_hbm = pl.BlockSpec(memory_space=pl.ANY)
    stay = lambda array: pltpu.with_memory_space_constraint(array, pltpu.HBM)
    steps = 2
    width = 2 * model // steps
    members = 32
    packed = 4 * 2 * model // 128
    block = bf16(BLOCK, 2 * model)
    kv, near, other, level_3, level_6 = call(
        project_kernel,
        (
            bf16(rows, 2 * model), bf16(2 * BLOCK, 2 * model), block,
            bf16(BLOCK // 2, 2 * model), bf16(members * packed, 128),
        ),
        [SMEM, in_hbm, in_hbm],
        place, stay(tokens), stay(w_qkv),
        flops=4 * rows * model * model,
        scratch=(
            pltpu.VMEM((rows, model), jnp.bfloat16),
            pltpu.VMEM((steps, model, width), jnp.bfloat16),
            pltpu.VMEM((2 * model // 128, rows, 128), jnp.float32),
            pltpu.SemaphoreType.DMA((steps + 1,)),
        ),
    )
    swap = [(i, i + 1) for i in range(1, count - 1, 2)]
    swap += [(j, i) for i, j in swap]
    def exchange(own, bit):
        return lax.ppermute(own, AXES, list(enumerate(partners(bit, count))))

    def pool(own, got, *after):
        return call(pool_kernel, block, vmem(2), own, got, after=after)

    teams = [
        [i for i in range(count) if i >> 6 == part and i & 1 == core]
        for part in range(count >> 6)
        for core in range(2)
    ]
    spread = lax.all_to_all(level_6, AXES, 0, 0, axis_index_groups=teams, tiled=True)
    near_sib = exchange(near, 0)
    own_3 = call(pool_near_kernel, block, vmem(2), level_3, near_sib)
    z_pairs = [[i, i ^ 2] for i in range(count) if not i & 2]
    both_3 = lax.all_gather(own_3, AXES, axis_index_groups=z_pairs, tiled=True)
    other_halo = lax.ppermute(other, AXES, swap)
    mine = call(
        unpack_kernel, bf16(3 * BLOCK // 2, 2 * model), [SMEM, *vmem(1)],
        place, spread.reshape(members, packed, 128),
        scratch=(pltpu.VMEM((members * packed, 128), jnp.float32),),
        after=(both_3, other_halo),
    )

    def pair_gather(own, bit):
        to = partners(bit, count)
        pairs = [[i, to[i]] for i in range(count) if not i >> bit & 1]
        return lax.all_gather(own, AXES, axis_index_groups=pairs, tiled=True)

    both = pair_gather(mine, 0)
    own_8 = call(own_8_kernel, block, vmem(1), both)
    sib_8 = exchange(own_8, 6)
    own_4 = call(pool_kernel, block, vmem(1), both_3, after=(own_8,))
    sib_4 = exchange(own_4, 2)
    q, num, tot = call(
        functools.partial(local_kernel, count),
        (bf16(rows, model), f32(rows, model), f32(rows, model)),
        [SMEM, *vmem(1), in_hbm, *vmem(5)],
        place, tokens, stay(w_qkv), kv, near_sib, other_halo, both_3, both,
        flops=10**9,
        scratch=(
            pltpu.VMEM((rows + 2 * BLOCK, 2 * model), jnp.bfloat16),
            pltpu.VMEM((rows // 2, 2 * model), jnp.bfloat16),
            pltpu.VMEM((model, model), jnp.bfloat16),
            pltpu.SemaphoreType.DMA(()),
        ),
        after=(own_4,),
    )
    own_9 = call(pool_halves_kernel, block, vmem(2), own_8, sib_8, after=(q,))
    sib_9 = exchange(own_9, 7)
    own_5 = pool(own_4, sib_4, own_9)
    sib_5 = exchange(own_5, 3)
    own_10 = pool(own_9, sib_9, own_5)
    pair = pair_gather(own_10, 8)
    return call(
        final_kernel,
        bf16(rows, model),
        [SMEM, *vmem(8), in_hbm],
        place, q, num, tot, sib_4, sib_5, sib_8, sib_9, pair, stay(w_out),
        flops=10**9,
        scratch=(
            pltpu.VMEM((rows, model), jnp.bfloat16),
            pltpu.VMEM((model, model), jnp.bfloat16),
            pltpu.SemaphoreType.DMA(()),
        ),
    )


def solution(mesh):
    return jax.shard_map(
        per_device,
        mesh=mesh,
        in_specs=(P(AXES, None), P(), P()),
        out_specs=P(AXES, None),
        check_vma=False,
    )
```

```python
import functools

import jax
import jax.numpy as jnp
import numpy as np
from jax import lax
from jax.experimental import pallas as pl
from jax.experimental.pallas import tpu as pltpu
from jax.sharding import PartitionSpec as P

HEADS = 8
BLOCK = 64
AXES = ("gx", "gy")
FAR8 = (6, 7, 4, 5, 2, 3, 0, 1)
FAR4 = (3, 2, 1, 0)


def partners(bit, count):
    route = []
    for index in range(count):
        if bit == 3:
            route.append(index & ~14 | FAR8[index >> 1 & 7] << 1)
        elif bit == 6:
            route.append(index & ~112 | FAR8[index >> 4 & 7] << 4)
        elif bit == 8:
            route.append(index & ~384 | FAR4[index >> 7 & 3] << 7)
        else:
            route.append(index ^ 1 << bit)
    return route


def vmem(count):
    return [pl.BlockSpec(memory_space=pltpu.VMEM)] * count


SMEM = pl.BlockSpec(memory_space=pltpu.SMEM)


def call(kernel, outs, in_specs, *args, flops=0, scratch=(), limit=10, after=()):
    count = len(args)

    def body(*refs):
        kernel(*refs[:count], *refs[count + len(after) :])

    return pl.pallas_call(
        body,
        out_shape=outs,
        in_specs=list(in_specs) + [pl.BlockSpec(memory_space=pl.ANY)] * len(after),
        out_specs=jax.tree.map(lambda _: pl.BlockSpec(memory_space=pltpu.VMEM), outs),
        scratch_shapes=list(scratch),
        compiler_params=pltpu.CompilerParams(vmem_limit_bytes=limit * 2**20),
        cost_estimate=pl.CostEstimate(flops=flops, bytes_accessed=2**20, transcendentals=0),
    )(*args, *after)


def pool_matrix(rows):
    r = lax.broadcasted_iota(jnp.int32, (rows, 2 * rows), 0)
    c = lax.broadcasted_iota(jnp.int32, (rows, 2 * rows), 1)
    return jnp.where(c >> 1 == r, 0.5, 0.0).astype(jnp.bfloat16)


def pooled(block):
    return jnp.dot(
        pool_matrix(block.shape[0] // 2), block, preferred_element_type=jnp.float32
    ).astype(jnp.bfloat16)


def project_kernel(
    place, x_hbm, w_hbm, kv_ref, near_ref, other_ref, l3_ref, packed_ref, x_buf, w_buf, part_buf, sems
):
    rows, model = x_buf.shape
    width = w_buf.shape[2]
    steps = w_buf.shape[0]
    x_copy = pltpu.make_async_copy(x_hbm, x_buf, sems.at[steps])
    x_copy.start()
    copies = []
    for step in range(steps):
        columns = pl.ds(model + step * width, width)
        copy = pltpu.make_async_copy(w_hbm.at[:, columns], w_buf.at[step], sems.at[step])
        copy.start()
        copies.append(copy)
    x_copy.wait()
    x = x_buf[...]
    pieces = []
    for step in range(steps):
        copies[step].wait()
        lanes = slice(step * width, (step + 1) * width)
        part = jnp.dot(x, w_buf[step], preferred_element_type=jnp.float32).astype(jnp.bfloat16)
        kv_ref[:, lanes] = part
        wide = part.astype(jnp.float32)
        for at in range(0, width, 128):
            tile = (step * width + at) // 128
            part_buf[tile] = wide[:, at : at + 128]
            size = rows
            while size > 8:
                size //= 2
                even = part_buf[tile, pl.ds(0, size, stride=2), :]
                odd = part_buf[tile, pl.ds(1, size, stride=2), :]
                level = ((even + odd) * 0.5).astype(jnp.bfloat16)
                if size == BLOCK:
                    near_ref[BLOCK:, tile * 128 : (tile + 1) * 128] = level
                if size == BLOCK // 2:
                    l3_ref[:, tile * 128 : (tile + 1) * 128] = level
                part_buf[tile, :size, :] = level.astype(jnp.float32)
            pieces.append(level.astype(jnp.float32))
    packed = pooled(jnp.concatenate(pieces, axis=0).astype(jnp.bfloat16))
    size = packed.shape[0]
    for copy in range(packed_ref.shape[0] // size):
        packed_ref[copy * size : (copy + 1) * size, :] = packed
    core = place[0] & 1
    last = rows - BLOCK
    low = pl.multiple_of(core * last, BLOCK)
    high = pl.multiple_of((1 - core) * last, BLOCK)
    near_ref[:BLOCK, :] = kv_ref[pl.ds(high, BLOCK), :]
    other_ref[...] = kv_ref[pl.ds(low, BLOCK), :]


def unpack_kernel(place, in_ref, out_ref, l8_ref, wide):
    members, rows, _ = in_ref.shape
    wide[...] = in_ref[...].reshape(members * rows, 128).astype(jnp.float32)
    y = (place[0] >> 4) & 3

    def mean(one, two):
        return ((one + two) * 0.5).astype(jnp.bfloat16).astype(jnp.float32)

    for tile in range(rows // 4):
        lanes = slice(tile * 128, (tile + 1) * 128)

        def level_6(start, count):
            return [
                wide[pl.ds(start * rows + tile * 4 + row, count, stride=rows), :]
                for row in range(4)
            ]

        def level_7(start, count):
            r = level_6(start, count)
            return [mean(r[0], r[1]), mean(r[2], r[3])]

        parts = (
            level_6((y ^ 1) * 8, 8)
            + level_7(((y >> 1) ^ 1) * 16, 16)
        )
        l8_ref[:, lanes] = mean(*level_7(0, members)).astype(jnp.bfloat16)
        out_ref[:, lanes] = jnp.concatenate(parts, axis=0).astype(jnp.bfloat16)


def stack_kernel(mine_ref, l8_ref, got_ref, out_ref):
    half = BLOCK // 2
    out_ref[:BLOCK, :] = mine_ref[...]
    out_ref[BLOCK : BLOCK + half, :] = l8_ref[...]
    out_ref[BLOCK + half :, :] = got_ref[...]


def own_9_kernel(both_ref, out_ref):
    one = both_ref[BLOCK : 2 * BLOCK, :].astype(jnp.float32)
    two = both_ref[3 * BLOCK :, :].astype(jnp.float32)
    out_ref[...] = ((one + two) * 0.5).astype(jnp.bfloat16)


def pool_near_kernel(mine_ref, sib_ref, out_ref):
    out_ref[: BLOCK // 2, :] = mine_ref[...]
    out_ref[BLOCK // 2 :, :] = pooled(sib_ref[BLOCK:, :])


def pool_kernel(*refs):
    ins, out_ref = refs[:-1], refs[-1]
    half = BLOCK // len(ins)
    for num, ref in enumerate(ins):
        out_ref[num * half : (num + 1) * half, :] = pooled(ref[...])


def attend_pair(q, keys, values, ones):
    rows = q.shape[0]
    lane = lax.broadcasted_iota(jnp.int32, q.shape, 1)
    first = lane < 64
    zero = jnp.zeros_like(q)
    both = jnp.concatenate([jnp.where(first, q, zero), jnp.where(first, zero, q)], axis=0)
    scores = lax.dot_general(
        both, keys, (((1,), (1,)), ((), ())), preferred_element_type=jnp.float32
    )
    weights = jnp.exp(scores).astype(jnp.bfloat16)
    sums = jnp.dot(
        weights, jnp.concatenate([values, ones], axis=1), preferred_element_type=jnp.float32
    )
    num = jnp.where(first, sums[:rows, :128], sums[rows:, :128])
    tot = jnp.where(first, sums[:rows, 128:], sums[rows:, 128:])
    return num, tot


def local_kernel(
    count, place, x_ref, w_hbm, kv_ref, near_ref, other_ref, both_3_ref, sib_4_ref, both_ref,
    q_ref, num_ref, tot_ref, pad, l1, w_ref, sem
):
    rows, model = x_ref.shape
    blocks = rows // BLOCK
    copy = pltpu.make_async_copy(w_hbm.at[:, pl.ds(0, model)], w_ref, sem)
    copy.start()
    core = place[0] & 1
    sib_halo = near_ref[:BLOCK, :]
    other = other_ref[...]
    is_first = core == 0
    pad[:BLOCK, :] = jnp.where(is_first, other, sib_halo)
    pad[BLOCK : BLOCK + rows, :] = kv_ref[...]
    pad[BLOCK + rows :, :] = jnp.where(is_first, sib_halo, other)
    l1[...] = pooled(kv_ref[...])
    copy.wait()
    q_ref[...] = (
        jnp.dot(x_ref[...], w_ref[...], preferred_element_type=jnp.float32)
        .astype(jnp.bfloat16) * jnp.bfloat16(0.125)
    )
    key_row = lax.broadcasted_iota(jnp.int32, (4 * BLOCK, 128), 0)
    for i in range(blocks):
        ones = jnp.ones((4 * BLOCK, 128), jnp.float32)
        if i == 0:
            ones = jnp.where((key_row < BLOCK) & (place[0] == 0), 0.0, ones)
        if i == blocks - 1:
            ones = jnp.where((key_row >= 2 * BLOCK) & (key_row < 3 * BLOCK) & (place[0] == count - 1), 0.0, ones)
        ones = ones.astype(jnp.bfloat16)
        sib = (i >> 1) ^ 1
        here = slice(i * BLOCK, (i + 1) * BLOCK)
        for lanes in range(0, model, 128):
            kl = slice(lanes, lanes + 128)
            vl = slice(model + lanes, model + lanes + 128)
            keys = jnp.concatenate(
                [pad[i * BLOCK : (i + 3) * BLOCK, kl], l1[sib * BLOCK : (sib + 1) * BLOCK, kl]], axis=0
            )
            values = jnp.concatenate(
                [pad[i * BLOCK : (i + 3) * BLOCK, vl], l1[sib * BLOCK : (sib + 1) * BLOCK, vl]], axis=0
            )
            num, tot = attend_pair(q_ref[here, kl], keys, values, ones)
            num_ref[here, kl] = num
            tot_ref[here, kl] = tot
    start = pl.multiple_of((1 - ((place[0] >> 1) & 1)) * BLOCK, BLOCK)
    sib_3 = both_3_ref[pl.ds(start, BLOCK), :]
    half = BLOCK // 2
    far = jnp.concatenate(
        [near_ref[BLOCK:, :], sib_3, sib_4_ref[...], both_ref[:BLOCK, :]]
        + [both_ref[BLOCK + half : 3 * BLOCK, :], both_ref[3 * BLOCK + half :, :]],
        axis=0,
    )
    for lanes in range(0, model, 128):
        kl = slice(lanes, lanes + 128)
        num, tot = far_sums(far, q_ref[:, kl], lanes, model)
        num_ref[:, kl] += num
        tot_ref[:, kl] += tot


def far_blocks(refs):
    blocks = []
    for ref in refs:
        if ref.shape[0] == 2 * BLOCK:
            blocks.append(ref[BLOCK:, :])
        else:
            blocks.append(ref[:BLOCK, :])
    return jnp.concatenate(blocks, axis=0)


def far_sums(far, q, lanes, model):
    keys = far[:, lanes : lanes + 128]
    values = far[:, model + lanes : model + lanes + 128]
    return attend_pair(q, keys, values, jnp.ones(values.shape, jnp.bfloat16))


def final_kernel(
    q_ref, num_in, tot_in, sib_5_ref, sib_9_ref, sib_10_ref, w_hbm, out_ref, att, w_ref, sem
):
    copy = pltpu.make_async_copy(w_hbm, w_ref, sem)
    copy.start()
    model = q_ref.shape[1]
    far = far_blocks((sib_5_ref, sib_9_ref, sib_10_ref))
    for lanes in range(0, model, 128):
        at = slice(lanes, lanes + 128)
        num, tot = far_sums(far, q_ref[:, at], lanes, model)
        att[:, at] = ((num_in[:, at] + num) / (tot_in[:, at] + tot)).astype(jnp.bfloat16)
    copy.wait()
    out_ref[...] = jnp.dot(att[...], w_ref[...], preferred_element_type=jnp.float32).astype(
        jnp.bfloat16
    )


def per_device(tokens, w_qkv, w_out):
    rows, model = tokens.shape
    index = lax.axis_index(AXES)
    count = lax.axis_size(AXES)
    place = index.astype(jnp.int32).reshape(1)
    bf16 = lambda *shape: jax.ShapeDtypeStruct(shape, jnp.bfloat16)
    f32 = lambda *shape: jax.ShapeDtypeStruct(shape, jnp.float32)
    in_hbm = pl.BlockSpec(memory_space=pl.ANY)
    stay = lambda array: pltpu.with_memory_space_constraint(array, pltpu.HBM)
    steps = 2
    width = 2 * model // steps
    members = 32
    packed = 4 * 2 * model // 128
    block = bf16(BLOCK, 2 * model)
    kv, near, other, level_3, level_6 = call(
        project_kernel,
        (
            bf16(rows, 2 * model), bf16(2 * BLOCK, 2 * model), block,
            bf16(BLOCK // 2, 2 * model), bf16(members * packed, 128),
        ),
        [SMEM, in_hbm, in_hbm],
        place, stay(tokens), stay(w_qkv),
        flops=4 * rows * model * model,
        scratch=(
            pltpu.VMEM((rows, model), jnp.bfloat16),
            pltpu.VMEM((steps, model, width), jnp.bfloat16),
            pltpu.VMEM((2 * model // 128, rows, 128), jnp.float32),
            pltpu.SemaphoreType.DMA((steps + 1,)),
        ),
    )
    swap = [(i, i + 1) for i in range(1, count - 1, 2)]
    swap += [(j, i) for i, j in swap]
    def exchange(own, bit):
        return lax.ppermute(own, AXES, list(enumerate(partners(bit, count))))

    def pool(own, got, *after):
        return call(pool_kernel, block, vmem(2), own, got, after=after)

    teams = [
        [i for i in range(count) if i >> 6 == part and i & 1 == core]
        for part in range(count >> 6)
        for core in range(2)
    ]
    spread = lax.all_to_all(level_6, AXES, 0, 0, axis_index_groups=teams, tiled=True)
    near_sib = exchange(near, 0)
    own_3 = call(pool_near_kernel, block, vmem(2), level_3, near_sib)
    z_pairs = [[i, i ^ 2] for i in range(count) if not i & 2]
    both_3 = lax.all_gather(own_3, AXES, axis_index_groups=z_pairs, tiled=True)
    other_halo = lax.ppermute(other, AXES, swap)
    def pair_gather(own, bit):
        to = partners(bit, count)
        pairs = [[i, to[i]] for i in range(count) if not i >> bit & 1]
        return lax.all_gather(own, AXES, axis_index_groups=pairs, tiled=True)

    mine, l8 = call(
        unpack_kernel, (block, bf16(BLOCK // 2, 2 * model)), [SMEM, *vmem(1)],
        place, spread.reshape(members, packed, 128),
        scratch=(pltpu.VMEM((members * packed, 128), jnp.float32),),
        after=(both_3, other_halo),
    )
    got_8 = exchange(l8, 6)
    own_4 = call(pool_kernel, block, vmem(1), both_3, after=(mine,))
    sib_4 = exchange(own_4, 2)
    stack = call(
        stack_kernel, bf16(2 * BLOCK, 2 * model), vmem(3), mine, l8, got_8, after=(own_4,)
    )
    both = pair_gather(stack, 0)
    own_9 = call(own_9_kernel, block, vmem(1), both)
    sib_9 = exchange(own_9, 7)
    own_5 = pool(own_4, sib_4, own_9)
    sib_5 = exchange(own_5, 3)
    own_10 = pool(own_9, sib_9, own_5)
    sib_10 = exchange(own_10, 8)
    q, num, tot = call(
        functools.partial(local_kernel, count),
        (bf16(rows, model), f32(rows, model), f32(rows, model)),
        [SMEM, *vmem(1), in_hbm, *vmem(6)],
        place, tokens, stay(w_qkv), kv, near_sib, other_halo, both_3, sib_4, both,
        flops=10**9,
        scratch=(
            pltpu.VMEM((rows + 2 * BLOCK, 2 * model), jnp.bfloat16),
            pltpu.VMEM((rows // 2, 2 * model), jnp.bfloat16),
            pltpu.VMEM((model, model), jnp.bfloat16),
            pltpu.SemaphoreType.DMA(()),
        ),
        after=(own_10,),
    )
    return call(
        final_kernel,
        bf16(rows, model),
        [*vmem(6), in_hbm],
        q, num, tot, sib_5, sib_9, sib_10, stay(w_out),
        flops=10**9,
        scratch=(
            pltpu.VMEM((rows, model), jnp.bfloat16),
            pltpu.VMEM((model, model), jnp.bfloat16),
            pltpu.SemaphoreType.DMA(()),
        ),
    )


def solution(mesh):
    return jax.shard_map(
        per_device,
        mesh=mesh,
        in_specs=(P(AXES, None), P(), P()),
        out_specs=P(AXES, None),
        check_vma=False,
    )
```

```python
import functools

import jax
import jax.numpy as jnp
import numpy as np
from jax import lax
from jax.experimental import pallas as pl
from jax.experimental.pallas import tpu as pltpu
from jax.sharding import PartitionSpec as P

HEADS = 8
BLOCK = 64
AXES = ("gx", "gy")
FAR8 = (6, 7, 4, 5, 2, 3, 0, 1)
FAR4 = (3, 2, 1, 0)


def partners(bit, count):
    route = []
    for index in range(count):
        if bit == 3:
            route.append(index & ~14 | FAR8[index >> 1 & 7] << 1)
        elif bit == 6:
            route.append(index & ~112 | FAR8[index >> 4 & 7] << 4)
        elif bit == 8:
            route.append(index & ~384 | FAR4[index >> 7 & 3] << 7)
        else:
            route.append(index ^ 1 << bit)
    return route


def vmem(count):
    return [pl.BlockSpec(memory_space=pltpu.VMEM)] * count


SMEM = pl.BlockSpec(memory_space=pltpu.SMEM)


def call(kernel, outs, in_specs, *args, flops=0, scratch=(), limit=10, after=()):
    count = len(args)

    def body(*refs):
        kernel(*refs[:count], *refs[count + len(after) :])

    return pl.pallas_call(
        body,
        out_shape=outs,
        in_specs=list(in_specs) + [pl.BlockSpec(memory_space=pl.ANY)] * len(after),
        out_specs=jax.tree.map(lambda _: pl.BlockSpec(memory_space=pltpu.VMEM), outs),
        scratch_shapes=list(scratch),
        compiler_params=pltpu.CompilerParams(vmem_limit_bytes=limit * 2**20),
        cost_estimate=pl.CostEstimate(flops=flops, bytes_accessed=2**20, transcendentals=0),
    )(*args, *after)


def pool_matrix(rows):
    r = lax.broadcasted_iota(jnp.int32, (rows, 2 * rows), 0)
    c = lax.broadcasted_iota(jnp.int32, (rows, 2 * rows), 1)
    return jnp.where(c >> 1 == r, 0.5, 0.0).astype(jnp.bfloat16)


def pooled(block):
    return jnp.dot(
        pool_matrix(block.shape[0] // 2), block, preferred_element_type=jnp.float32
    ).astype(jnp.bfloat16)


def project_kernel(
    place, x_hbm, w_hbm, kv_ref, near_ref, other_ref, l3_ref, packed_ref, x_buf, w_buf, part_buf, sems
):
    rows, model = x_buf.shape
    width = w_buf.shape[2]
    steps = w_buf.shape[0]
    x_copy = pltpu.make_async_copy(x_hbm, x_buf, sems.at[steps])
    x_copy.start()
    copies = []
    for step in range(steps):
        columns = pl.ds(model + step * width, width)
        copy = pltpu.make_async_copy(w_hbm.at[:, columns], w_buf.at[step], sems.at[step])
        copy.start()
        copies.append(copy)
    x_copy.wait()
    x = x_buf[...]
    pieces = []
    for step in range(steps):
        copies[step].wait()
        lanes = slice(step * width, (step + 1) * width)
        part = jnp.dot(x, w_buf[step], preferred_element_type=jnp.float32).astype(jnp.bfloat16)
        kv_ref[:, lanes] = part
        wide = part.astype(jnp.float32)
        for at in range(0, width, 128):
            tile = (step * width + at) // 128
            part_buf[tile] = wide[:, at : at + 128]
            size = rows
            while size > 8:
                size //= 2
                even = part_buf[tile, pl.ds(0, size, stride=2), :]
                odd = part_buf[tile, pl.ds(1, size, stride=2), :]
                level = ((even + odd) * 0.5).astype(jnp.bfloat16)
                if size == BLOCK:
                    near_ref[BLOCK:, tile * 128 : (tile + 1) * 128] = level
                if size == BLOCK // 2:
                    l3_ref[:, tile * 128 : (tile + 1) * 128] = level
                part_buf[tile, :size, :] = level.astype(jnp.float32)
            pieces.append(level.astype(jnp.float32))
    packed = pooled(jnp.concatenate(pieces, axis=0).astype(jnp.bfloat16))
    size = packed.shape[0]
    for copy in range(packed_ref.shape[0] // size):
        packed_ref[copy * size : (copy + 1) * size, :] = packed
    core = place[0] & 1
    last = rows - BLOCK
    low = pl.multiple_of(core * last, BLOCK)
    high = pl.multiple_of((1 - core) * last, BLOCK)
    near_ref[:BLOCK, :] = kv_ref[pl.ds(high, BLOCK), :]
    other_ref[...] = kv_ref[pl.ds(low, BLOCK), :]


def unpack_kernel(place, in_ref, out_ref, l8_ref, wide):
    members, rows, _ = in_ref.shape
    wide[...] = in_ref[...].reshape(members * rows, 128).astype(jnp.float32)
    y = (place[0] >> 4) & 3

    def mean(one, two):
        return ((one + two) * 0.5).astype(jnp.bfloat16).astype(jnp.float32)

    for tile in range(rows // 4):
        lanes = slice(tile * 128, (tile + 1) * 128)

        def level_6(start, count):
            return [
                wide[pl.ds(start * rows + tile * 4 + row, count, stride=rows), :]
                for row in range(4)
            ]

        def level_7(start, count):
            r = level_6(start, count)
            return [mean(r[0], r[1]), mean(r[2], r[3])]

        parts = (
            level_6((y ^ 1) * 8, 8)
            + level_7(((y >> 1) ^ 1) * 16, 16)
        )
        l8_ref[:, lanes] = mean(*level_7(0, members)).astype(jnp.bfloat16)
        out_ref[:, lanes] = jnp.concatenate(parts, axis=0).astype(jnp.bfloat16)


def stack_kernel(mine_ref, l8_ref, got_ref, out_ref):
    half = BLOCK // 2
    out_ref[:BLOCK, :] = mine_ref[...]
    out_ref[BLOCK : BLOCK + half, :] = l8_ref[...]
    out_ref[BLOCK + half :, :] = got_ref[...]


def own_9_kernel(both_ref, out_ref):
    one = both_ref[BLOCK : 2 * BLOCK, :].astype(jnp.float32)
    two = both_ref[3 * BLOCK :, :].astype(jnp.float32)
    out_ref[...] = ((one + two) * 0.5).astype(jnp.bfloat16)


def pool_near_kernel(mine_ref, sib_ref, out_ref):
    out_ref[: BLOCK // 2, :] = mine_ref[...]
    out_ref[BLOCK // 2 :, :] = pooled(sib_ref[BLOCK:, :])


def pool_kernel(*refs):
    ins, out_ref = refs[:-1], refs[-1]
    half = BLOCK // len(ins)
    for num, ref in enumerate(ins):
        out_ref[num * half : (num + 1) * half, :] = pooled(ref[...])


def attend_pair(q, keys, values, ones):
    rows = q.shape[0]
    lane = lax.broadcasted_iota(jnp.int32, q.shape, 1)
    first = lane < 64
    zero = jnp.zeros_like(q)
    both = jnp.concatenate([jnp.where(first, q, zero), jnp.where(first, zero, q)], axis=0)
    scores = lax.dot_general(
        both, keys, (((1,), (1,)), ((), ())), preferred_element_type=jnp.float32
    )
    weights = jnp.exp(scores).astype(jnp.bfloat16)
    sums = jnp.dot(
        weights, jnp.concatenate([values, ones], axis=1), preferred_element_type=jnp.float32
    )
    num = jnp.where(first, sums[:rows, :128], sums[rows:, :128])
    tot = jnp.where(first, sums[:rows, 128:], sums[rows:, 128:])
    return num, tot


def local_kernel(
    count, place, x_ref, w_hbm, kv_ref, near_ref, other_ref, both_3_ref, sib_4_ref, both_ref,
    q_ref, num_ref, tot_ref, pad, l1, w_ref, sem
):
    rows, model = x_ref.shape
    blocks = rows // BLOCK
    copy = pltpu.make_async_copy(w_hbm.at[:, pl.ds(0, model)], w_ref, sem)
    copy.start()
    core = place[0] & 1
    sib_halo = near_ref[:BLOCK, :]
    other = other_ref[...]
    is_first = core == 0
    pad[:BLOCK, :] = jnp.where(is_first, other, sib_halo)
    pad[BLOCK : BLOCK + rows, :] = kv_ref[...]
    pad[BLOCK + rows :, :] = jnp.where(is_first, sib_halo, other)
    l1[...] = pooled(kv_ref[...])
    copy.wait()
    q_ref[...] = (
        jnp.dot(x_ref[...], w_ref[...], preferred_element_type=jnp.float32)
        .astype(jnp.bfloat16) * jnp.bfloat16(0.125)
    )
    key_row = lax.broadcasted_iota(jnp.int32, (4 * BLOCK, 128), 0)
    for i in range(blocks):
        ones = jnp.ones((4 * BLOCK, 128), jnp.float32)
        if i == 0:
            ones = jnp.where((key_row < BLOCK) & (place[0] == 0), 0.0, ones)
        if i == blocks - 1:
            ones = jnp.where((key_row >= 2 * BLOCK) & (key_row < 3 * BLOCK) & (place[0] == count - 1), 0.0, ones)
        ones = ones.astype(jnp.bfloat16)
        sib = (i >> 1) ^ 1
        here = slice(i * BLOCK, (i + 1) * BLOCK)
        for lanes in range(0, model, 128):
            kl = slice(lanes, lanes + 128)
            vl = slice(model + lanes, model + lanes + 128)
            keys = jnp.concatenate(
                [pad[i * BLOCK : (i + 3) * BLOCK, kl], l1[sib * BLOCK : (sib + 1) * BLOCK, kl]], axis=0
            )
            values = jnp.concatenate(
                [pad[i * BLOCK : (i + 3) * BLOCK, vl], l1[sib * BLOCK : (sib + 1) * BLOCK, vl]], axis=0
            )
            num, tot = attend_pair(q_ref[here, kl], keys, values, ones)
            num_ref[here, kl] = num
            tot_ref[here, kl] = tot
    start = pl.multiple_of((1 - ((place[0] >> 1) & 1)) * BLOCK, BLOCK)
    sib_3 = both_3_ref[pl.ds(start, BLOCK), :]
    half = BLOCK // 2
    far = jnp.concatenate(
        [near_ref[BLOCK:, :], sib_3, sib_4_ref[...], both_ref[:BLOCK, :]]
        + [both_ref[BLOCK + half : 3 * BLOCK, :], both_ref[3 * BLOCK + half :, :]],
        axis=0,
    )
    for lanes in range(0, model, 128):
        kl = slice(lanes, lanes + 128)
        num, tot = far_sums(far, q_ref[:, kl], lanes, model)
        num_ref[:, kl] += num
        tot_ref[:, kl] += tot


def far_blocks(refs):
    blocks = []
    for ref in refs:
        if ref.shape[0] == 2 * BLOCK:
            blocks.append(ref[BLOCK:, :])
        else:
            blocks.append(ref[:BLOCK, :])
    return jnp.concatenate(blocks, axis=0)


def far_sums(far, q, lanes, model):
    keys = far[:, lanes : lanes + 128]
    values = far[:, model + lanes : model + lanes + 128]
    return attend_pair(q, keys, values, jnp.ones(values.shape, jnp.bfloat16))


def final_kernel(
    q_ref, num_in, tot_in, sib_5_ref, sib_9_ref, sib_10_ref, w_hbm, out_ref, att, w_ref, sem
):
    copy = pltpu.make_async_copy(w_hbm, w_ref, sem)
    copy.start()
    model = q_ref.shape[1]
    far = far_blocks((sib_5_ref, sib_9_ref, sib_10_ref))
    for lanes in range(0, model, 128):
        at = slice(lanes, lanes + 128)
        num, tot = far_sums(far, q_ref[:, at], lanes, model)
        att[:, at] = ((num_in[:, at] + num) / (tot_in[:, at] + tot)).astype(jnp.bfloat16)
    copy.wait()
    out_ref[...] = jnp.dot(att[...], w_ref[...], preferred_element_type=jnp.float32).astype(
        jnp.bfloat16
    )


def per_device(tokens, w_qkv, w_out):
    rows, model = tokens.shape
    index = lax.axis_index(AXES)
    count = lax.axis_size(AXES)
    place = index.astype(jnp.int32).reshape(1)
    bf16 = lambda *shape: jax.ShapeDtypeStruct(shape, jnp.bfloat16)
    f32 = lambda *shape: jax.ShapeDtypeStruct(shape, jnp.float32)
    in_hbm = pl.BlockSpec(memory_space=pl.ANY)
    stay = lambda array: pltpu.with_memory_space_constraint(array, pltpu.HBM)
    steps = 2
    width = 2 * model // steps
    members = 32
    packed = 4 * 2 * model // 128
    block = bf16(BLOCK, 2 * model)
    kv, near, other, level_3, level_6 = call(
        project_kernel,
        (
            bf16(rows, 2 * model), bf16(2 * BLOCK, 2 * model), block,
            bf16(BLOCK // 2, 2 * model), bf16(members * packed, 128),
        ),
        [SMEM, in_hbm, in_hbm],
        place, stay(tokens), stay(w_qkv),
        flops=4 * rows * model * model,
        scratch=(
            pltpu.VMEM((rows, model), jnp.bfloat16),
            pltpu.VMEM((steps, model, width), jnp.bfloat16),
            pltpu.VMEM((2 * model // 128, rows, 128), jnp.float32),
            pltpu.SemaphoreType.DMA((steps + 1,)),
        ),
    )
    swap = [(i, i + 1) for i in range(1, count - 1, 2)]
    swap += [(j, i) for i, j in swap]
    def exchange(own, bit):
        return lax.ppermute(own, AXES, list(enumerate(partners(bit, count))))

    def pool(own, got, *after):
        return call(pool_kernel, block, vmem(2), own, got, after=after)

    teams = [
        [i for i in range(count) if i >> 6 == part and i & 1 == core]
        for part in range(count >> 6)
        for core in range(2)
    ]
    spread = lax.all_to_all(level_6, AXES, 0, 0, axis_index_groups=teams, tiled=True)
    near_sib = exchange(near, 0)
    own_3 = call(pool_near_kernel, block, vmem(2), level_3, near_sib)
    z_pairs = [[i, i ^ 2] for i in range(count) if not i & 2]
    both_3 = lax.all_gather(own_3, AXES, axis_index_groups=z_pairs, tiled=True)
    def pair_gather(own, bit):
        to = partners(bit, count)
        pairs = [[i, to[i]] for i in range(count) if not i >> bit & 1]
        return lax.all_gather(own, AXES, axis_index_groups=pairs, tiled=True)

    mine, l8 = call(
        unpack_kernel, (block, bf16(BLOCK // 2, 2 * model)), [SMEM, *vmem(1)],
        place, spread.reshape(members, packed, 128),
        scratch=(pltpu.VMEM((members * packed, 128), jnp.float32),),
        after=(both_3,),
    )
    got_8 = exchange(l8, 6)
    own_4 = call(pool_kernel, block, vmem(1), both_3, after=(mine,))
    sib_4 = exchange(own_4, 2)
    other, _ = lax.optimization_barrier((other, own_4))
    other_halo = lax.ppermute(other, AXES, swap)
    stack = call(
        stack_kernel, bf16(2 * BLOCK, 2 * model), vmem(3), mine, l8, got_8, after=(own_4,)
    )
    both = pair_gather(stack, 0)
    own_9 = call(own_9_kernel, block, vmem(1), both)
    sib_9 = exchange(own_9, 7)
    own_5 = pool(own_4, sib_4, own_9)
    sib_5 = exchange(own_5, 3)
    own_10 = pool(own_9, sib_9, own_5, other_halo)
    sib_10 = exchange(own_10, 8)
    q, num, tot = call(
        functools.partial(local_kernel, count),
        (bf16(rows, model), f32(rows, model), f32(rows, model)),
        [SMEM, *vmem(1), in_hbm, *vmem(6)],
        place, tokens, stay(w_qkv), kv, near_sib, other_halo, both_3, sib_4, both,
        flops=10**9,
        scratch=(
            pltpu.VMEM((rows + 2 * BLOCK, 2 * model), jnp.bfloat16),
            pltpu.VMEM((rows // 2, 2 * model), jnp.bfloat16),
            pltpu.VMEM((model, model), jnp.bfloat16),
            pltpu.SemaphoreType.DMA(()),
        ),
        after=(own_10,),
    )
    return call(
        final_kernel,
        bf16(rows, model),
        [*vmem(6), in_hbm],
        q, num, tot, sib_5, sib_9, sib_10, stay(w_out),
        flops=10**9,
        scratch=(
            pltpu.VMEM((rows, model), jnp.bfloat16),
            pltpu.VMEM((model, model), jnp.bfloat16),
            pltpu.SemaphoreType.DMA(()),
        ),
    )


def solution(mesh):
    return jax.shard_map(
        per_device,
        mesh=mesh,
        in_specs=(P(AXES, None), P(), P()),
        out_specs=P(AXES, None),
        check_vma=False,
    )
```

```python
import functools

import jax
import jax.numpy as jnp
import numpy as np
from jax import lax
from jax.experimental import pallas as pl
from jax.experimental.pallas import tpu as pltpu
from jax.sharding import PartitionSpec as P

HEADS = 8
BLOCK = 64
AXES = ("gx", "gy")
FAR8 = (6, 7, 4, 5, 2, 3, 0, 1)
FAR4 = (3, 2, 1, 0)


def partners(bit, count):
    route = []
    for index in range(count):
        if bit == 3:
            route.append(index & ~14 | FAR8[index >> 1 & 7] << 1)
        elif bit == 6:
            route.append(index & ~112 | FAR8[index >> 4 & 7] << 4)
        elif bit == 8:
            route.append(index & ~384 | FAR4[index >> 7 & 3] << 7)
        else:
            route.append(index ^ 1 << bit)
    return route


def vmem(count):
    return [pl.BlockSpec(memory_space=pltpu.VMEM)] * count


SMEM = pl.BlockSpec(memory_space=pltpu.SMEM)


def call(kernel, outs, in_specs, *args, flops=0, scratch=(), limit=10, after=()):
    count = len(args)

    def body(*refs):
        kernel(*refs[:count], *refs[count + len(after) :])

    return pl.pallas_call(
        body,
        out_shape=outs,
        in_specs=list(in_specs) + [pl.BlockSpec(memory_space=pl.ANY)] * len(after),
        out_specs=jax.tree.map(lambda _: pl.BlockSpec(memory_space=pltpu.VMEM), outs),
        scratch_shapes=list(scratch),
        compiler_params=pltpu.CompilerParams(vmem_limit_bytes=limit * 2**20),
        cost_estimate=pl.CostEstimate(flops=flops, bytes_accessed=2**20, transcendentals=0),
    )(*args, *after)


def pool_matrix(rows):
    r = lax.broadcasted_iota(jnp.int32, (rows, 2 * rows), 0)
    c = lax.broadcasted_iota(jnp.int32, (rows, 2 * rows), 1)
    return jnp.where(c >> 1 == r, 0.5, 0.0).astype(jnp.bfloat16)


def pooled(block):
    return jnp.dot(
        pool_matrix(block.shape[0] // 2), block, preferred_element_type=jnp.float32
    ).astype(jnp.bfloat16)


def project_kernel(
    place, x_hbm, w_hbm, kv_ref, near_ref, other_ref, l3_ref, packed_ref, x_buf, w_buf, part_buf, sems
):
    rows, model = x_buf.shape
    width = w_buf.shape[2]
    steps = w_buf.shape[0]
    x_copy = pltpu.make_async_copy(x_hbm, x_buf, sems.at[steps])
    x_copy.start()
    copies = []
    for step in range(steps):
        columns = pl.ds(model + step * width, width)
        copy = pltpu.make_async_copy(w_hbm.at[:, columns], w_buf.at[step], sems.at[step])
        copy.start()
        copies.append(copy)
    x_copy.wait()
    x = x_buf[...]
    pieces = []
    for step in range(steps):
        copies[step].wait()
        lanes = slice(step * width, (step + 1) * width)
        part = jnp.dot(x, w_buf[step], preferred_element_type=jnp.float32).astype(jnp.bfloat16)
        kv_ref[:, lanes] = part
        wide = part.astype(jnp.float32)
        for at in range(0, width, 128):
            tile = (step * width + at) // 128
            part_buf[tile] = wide[:, at : at + 128]
            size = rows
            while size > 8:
                size //= 2
                even = part_buf[tile, pl.ds(0, size, stride=2), :]
                odd = part_buf[tile, pl.ds(1, size, stride=2), :]
                level = ((even + odd) * 0.5).astype(jnp.bfloat16)
                if size == BLOCK:
                    near_ref[BLOCK:, tile * 128 : (tile + 1) * 128] = level
                if size == BLOCK // 2:
                    l3_ref[:, tile * 128 : (tile + 1) * 128] = level
                part_buf[tile, :size, :] = level.astype(jnp.float32)
            pieces.append(level.astype(jnp.float32))
    packed = pooled(jnp.concatenate(pieces, axis=0).astype(jnp.bfloat16))
    size = packed.shape[0]
    for copy in range(packed_ref.shape[0] // size):
        packed_ref[copy * size : (copy + 1) * size, :] = packed
    core = place[0] & 1
    last = rows - BLOCK
    low = pl.multiple_of(core * last, BLOCK)
    high = pl.multiple_of((1 - core) * last, BLOCK)
    near_ref[:BLOCK, :] = kv_ref[pl.ds(high, BLOCK), :]
    other_ref[...] = kv_ref[pl.ds(low, BLOCK), :]


def unpack_kernel(place, in_ref, out_ref, l8_ref, wide):
    members, rows, _ = in_ref.shape
    wide[...] = in_ref[...].reshape(members * rows, 128).astype(jnp.float32)
    y = (place[0] >> 4) & 3

    def mean(one, two):
        return ((one + two) * 0.5).astype(jnp.bfloat16).astype(jnp.float32)

    for tile in range(rows // 4):
        lanes = slice(tile * 128, (tile + 1) * 128)

        def level_6(start, count):
            return [
                wide[pl.ds(start * rows + tile * 4 + row, count, stride=rows), :]
                for row in range(4)
            ]

        def level_7(start, count):
            r = level_6(start, count)
            return [mean(r[0], r[1]), mean(r[2], r[3])]

        parts = (
            level_6((y ^ 1) * 8, 8)
            + level_7(((y >> 1) ^ 1) * 16, 16)
        )
        l8_ref[:, lanes] = mean(*level_7(0, members)).astype(jnp.bfloat16)
        out_ref[:, lanes] = jnp.concatenate(parts, axis=0).astype(jnp.bfloat16)


def stack_kernel(mine_ref, l8_ref, got_ref, out_ref):
    half = BLOCK // 2
    out_ref[:BLOCK, :] = mine_ref[...]
    out_ref[BLOCK : BLOCK + half, :] = l8_ref[...]
    out_ref[BLOCK + half :, :] = got_ref[...]


def own_9_kernel(both_ref, out_ref):
    one = both_ref[BLOCK : 2 * BLOCK, :].astype(jnp.float32)
    two = both_ref[3 * BLOCK :, :].astype(jnp.float32)
    out_ref[...] = ((one + two) * 0.5).astype(jnp.bfloat16)


def pool_near_kernel(mine_ref, sib_ref, out_ref):
    out_ref[: BLOCK // 2, :] = mine_ref[...]
    out_ref[BLOCK // 2 :, :] = pooled(sib_ref[BLOCK:, :])


def pool_kernel(*refs):
    ins, out_ref = refs[:-1], refs[-1]
    half = BLOCK // len(ins)
    for num, ref in enumerate(ins):
        out_ref[num * half : (num + 1) * half, :] = pooled(ref[...])


def attend_pair(q, keys, values, ones):
    rows = q.shape[0]
    lane = lax.broadcasted_iota(jnp.int32, q.shape, 1)
    first = lane < 64
    zero = jnp.zeros_like(q)
    both = jnp.concatenate([jnp.where(first, q, zero), jnp.where(first, zero, q)], axis=0)
    scores = lax.dot_general(
        both, keys, (((1,), (1,)), ((), ())), preferred_element_type=jnp.float32
    )
    weights = jnp.exp(scores).astype(jnp.bfloat16)
    sums = jnp.dot(
        weights, jnp.concatenate([values, ones], axis=1), preferred_element_type=jnp.float32
    )
    num = jnp.where(first, sums[:rows, :128], sums[rows:, :128])
    tot = jnp.where(first, sums[:rows, 128:], sums[rows:, 128:])
    return num, tot


def local_kernel(
    count, place, x_ref, w_hbm, kv_ref, near_ref, other_ref, both_3_ref, sib_4_ref, both_ref,
    sib_9_ref, q_ref, num_ref, tot_ref, pad, l1, w_ref, sem
):
    rows, model = x_ref.shape
    blocks = rows // BLOCK
    copy = pltpu.make_async_copy(w_hbm.at[:, pl.ds(0, model)], w_ref, sem)
    copy.start()
    core = place[0] & 1
    sib_halo = near_ref[:BLOCK, :]
    other = other_ref[...]
    is_first = core == 0
    pad[:BLOCK, :] = jnp.where(is_first, other, sib_halo)
    pad[BLOCK : BLOCK + rows, :] = kv_ref[...]
    pad[BLOCK + rows :, :] = jnp.where(is_first, sib_halo, other)
    l1[...] = pooled(kv_ref[...])
    copy.wait()
    q_ref[...] = (
        jnp.dot(x_ref[...], w_ref[...], preferred_element_type=jnp.float32)
        .astype(jnp.bfloat16) * jnp.bfloat16(0.125)
    )
    key_row = lax.broadcasted_iota(jnp.int32, (4 * BLOCK, 128), 0)
    for i in range(blocks):
        ones = jnp.ones((4 * BLOCK, 128), jnp.float32)
        if i == 0:
            ones = jnp.where((key_row < BLOCK) & (place[0] == 0), 0.0, ones)
        if i == blocks - 1:
            ones = jnp.where((key_row >= 2 * BLOCK) & (key_row < 3 * BLOCK) & (place[0] == count - 1), 0.0, ones)
        ones = ones.astype(jnp.bfloat16)
        sib = (i >> 1) ^ 1
        here = slice(i * BLOCK, (i + 1) * BLOCK)
        for lanes in range(0, model, 128):
            kl = slice(lanes, lanes + 128)
            vl = slice(model + lanes, model + lanes + 128)
            keys = jnp.concatenate(
                [pad[i * BLOCK : (i + 3) * BLOCK, kl], l1[sib * BLOCK : (sib + 1) * BLOCK, kl]], axis=0
            )
            values = jnp.concatenate(
                [pad[i * BLOCK : (i + 3) * BLOCK, vl], l1[sib * BLOCK : (sib + 1) * BLOCK, vl]], axis=0
            )
            num, tot = attend_pair(q_ref[here, kl], keys, values, ones)
            num_ref[here, kl] = num
            tot_ref[here, kl] = tot
    start = pl.multiple_of((1 - ((place[0] >> 1) & 1)) * BLOCK, BLOCK)
    sib_3 = both_3_ref[pl.ds(start, BLOCK), :]
    half = BLOCK // 2
    far = jnp.concatenate(
        [near_ref[BLOCK:, :], sib_3, sib_4_ref[...], both_ref[:BLOCK, :]]
        + [both_ref[BLOCK + half : 3 * BLOCK, :], both_ref[3 * BLOCK + half :, :], sib_9_ref[...]],
        axis=0,
    )
    for lanes in range(0, model, 128):
        kl = slice(lanes, lanes + 128)
        num, tot = far_sums(far, q_ref[:, kl], lanes, model)
        num_ref[:, kl] += num
        tot_ref[:, kl] += tot


def far_blocks(refs):
    blocks = []
    for ref in refs:
        if ref.shape[0] == 2 * BLOCK:
            blocks.append(ref[BLOCK:, :])
        else:
            blocks.append(ref[:BLOCK, :])
    return jnp.concatenate(blocks, axis=0)


def far_sums(far, q, lanes, model):
    keys = far[:, lanes : lanes + 128]
    values = far[:, model + lanes : model + lanes + 128]
    return attend_pair(q, keys, values, jnp.ones(values.shape, jnp.bfloat16))


def final_kernel(
    q_ref, num_in, tot_in, sib_5_ref, sib_10_ref, w_hbm, out_ref, att, w_ref, sem
):
    copy = pltpu.make_async_copy(w_hbm, w_ref, sem)
    copy.start()
    model = q_ref.shape[1]
    far = far_blocks((sib_5_ref, sib_10_ref))
    for lanes in range(0, model, 128):
        at = slice(lanes, lanes + 128)
        num, tot = far_sums(far, q_ref[:, at], lanes, model)
        att[:, at] = ((num_in[:, at] + num) / (tot_in[:, at] + tot)).astype(jnp.bfloat16)
    copy.wait()
    out_ref[...] = jnp.dot(att[...], w_ref[...], preferred_element_type=jnp.float32).astype(
        jnp.bfloat16
    )


def per_device(tokens, w_qkv, w_out):
    rows, model = tokens.shape
    index = lax.axis_index(AXES)
    count = lax.axis_size(AXES)
    place = index.astype(jnp.int32).reshape(1)
    bf16 = lambda *shape: jax.ShapeDtypeStruct(shape, jnp.bfloat16)
    f32 = lambda *shape: jax.ShapeDtypeStruct(shape, jnp.float32)
    in_hbm = pl.BlockSpec(memory_space=pl.ANY)
    stay = lambda array: pltpu.with_memory_space_constraint(array, pltpu.HBM)
    steps = 2
    width = 2 * model // steps
    members = 32
    packed = 4 * 2 * model // 128
    block = bf16(BLOCK, 2 * model)
    kv, near, other, level_3, level_6 = call(
        project_kernel,
        (
            bf16(rows, 2 * model), bf16(2 * BLOCK, 2 * model), block,
            bf16(BLOCK // 2, 2 * model), bf16(members * packed, 128),
        ),
        [SMEM, in_hbm, in_hbm],
        place, stay(tokens), stay(w_qkv),
        flops=4 * rows * model * model,
        scratch=(
            pltpu.VMEM((rows, model), jnp.bfloat16),
            pltpu.VMEM((steps, model, width), jnp.bfloat16),
            pltpu.VMEM((2 * model // 128, rows, 128), jnp.float32),
            pltpu.SemaphoreType.DMA((steps + 1,)),
        ),
    )
    swap = [(i, i + 1) for i in range(1, count - 1, 2)]
    swap += [(j, i) for i, j in swap]
    def exchange(own, bit):
        return lax.ppermute(own, AXES, list(enumerate(partners(bit, count))))

    def pool(own, got, *after):
        return call(pool_kernel, block, vmem(2), own, got, after=after)

    teams = [
        [i for i in range(count) if i >> 6 == part and i & 1 == core]
        for part in range(count >> 6)
        for core in range(2)
    ]
    spread = lax.all_to_all(level_6, AXES, 0, 0, axis_index_groups=teams, tiled=True)
    near_sib = exchange(near, 0)
    own_3 = call(pool_near_kernel, block, vmem(2), level_3, near_sib)
    z_pairs = [[i, i ^ 2] for i in range(count) if not i & 2]
    both_3 = lax.all_gather(own_3, AXES, axis_index_groups=z_pairs, tiled=True)
    other_halo = lax.ppermute(other, AXES, swap)
    def pair_gather(own, bit):
        to = partners(bit, count)
        pairs = [[i, to[i]] for i in range(count) if not i >> bit & 1]
        return lax.all_gather(own, AXES, axis_index_groups=pairs, tiled=True)

    mine, l8 = call(
        unpack_kernel, (block, bf16(BLOCK // 2, 2 * model)), [SMEM, *vmem(1)],
        place, spread.reshape(members, packed, 128),
        scratch=(pltpu.VMEM((members * packed, 128), jnp.float32),),
        after=(both_3, other_halo),
    )
    got_8 = exchange(l8, 6)
    own_4 = call(pool_kernel, block, vmem(1), both_3, after=(mine,))
    sib_4 = exchange(own_4, 2)
    stack = call(
        stack_kernel, bf16(2 * BLOCK, 2 * model), vmem(3), mine, l8, got_8, after=(own_4,)
    )
    both = pair_gather(stack, 0)
    own_9 = call(own_9_kernel, block, vmem(1), both)
    sib_9 = exchange(own_9, 7)
    own_5 = pool(own_4, sib_4, own_9)
    sib_5 = exchange(own_5, 3)
    own_10 = pool(own_9, sib_9, own_5)
    sib_10 = exchange(own_10, 8)
    q, num, tot = call(
        functools.partial(local_kernel, count),
        (bf16(rows, model), f32(rows, model), f32(rows, model)),
        [SMEM, *vmem(1), in_hbm, *vmem(7)],
        place, tokens, stay(w_qkv), kv, near_sib, other_halo, both_3, sib_4, both, sib_9,
        flops=10**9,
        scratch=(
            pltpu.VMEM((rows + 2 * BLOCK, 2 * model), jnp.bfloat16),
            pltpu.VMEM((rows // 2, 2 * model), jnp.bfloat16),
            pltpu.VMEM((model, model), jnp.bfloat16),
            pltpu.SemaphoreType.DMA(()),
        ),
        after=(own_10,),
    )
    return call(
        final_kernel,
        bf16(rows, model),
        [*vmem(5), in_hbm],
        q, num, tot, sib_5, sib_10, stay(w_out),
        flops=10**9,
        scratch=(
            pltpu.VMEM((rows, model), jnp.bfloat16),
            pltpu.VMEM((model, model), jnp.bfloat16),
            pltpu.SemaphoreType.DMA(()),
        ),
    )


def solution(mesh):
    return jax.shard_map(
        per_device,
        mesh=mesh,
        in_specs=(P(AXES, None), P(), P()),
        out_specs=P(AXES, None),
        check_vma=False,
    )
```
